32 devices in a mesh: group: 1, expert: 8 (over z, y), tensor: 2 (over x), dp: 2 (over core).
Axes of the slice: x: 2, y: 2, z: 4, core: 2. Of those that a mesh axis runs over, the one named last changes fastest.
Arguments:
- tokens: bfloat16 [1536, 4096], P(('group', 'expert', 'dp'), 'tensor'), may hold values from -6 to 6
- expert_ids: int32 [1536, 8], P(('group', 'expert', 'dp')), may hold values from 0 to 15, all different within a row; in each aligned block of 96 rows (0 to 95, 96 to 191, ...) at most 72 rows name the same one
- route_weights: float32 [1536, 8], P(('group', 'expert', 'dp')), may hold values from 0.05 to 0.3
- w_gate: bfloat16 [16, 4096, 768], P(('expert', 'dp'), 'tensor'), may hold values from -0.09375 to 0.09375
- w_up: bfloat16 [16, 4096, 768], P(('expert', 'dp'), 'tensor'), may hold values from -0.09375 to 0.09375
- w_down: bfloat16 [16, 768, 4096], P(('expert', 'dp'), None, 'tensor'), may hold values from -0.21875 to 0.21875
Outputs:
- moe_output: bfloat16 [1536, 4096], P(('group', 'expert', 'dp'), 'tensor')
The draws below stay inside these ranges and needn't reach their ends.
Inputs may be any that keep to these rules, and one draw needn't show every extreme that they name: `expert_ids`: each row names 8 different experts; in each aligned block of 96 rows (the rows of one index pair of expert and dp) no expert is named by more than 72 rows.
All inputs are finite; a program needn't handle non-finite values.
Results may differ from the reference program's by a relative error of at most 0.017.
Values may be sent and summed in bfloat16 or wider, within the bound.
No kernel may reach another device: no remote copies, remote signals or barrier semaphores. Data moves between devices by JAX's collectives and lax.ppermute only.
A program may use at most 64 MiB of HBM per device.

```python
import math
import jax
import jax.numpy as jnp
import numpy as np
from jax import lax

D = 4096
FF = 768
TOP = 8
EXPERTS = 16
TOK_DEV = 96
CAP = 72
TOKENS = 1536
N_TENSOR = 2


def block_scale(stream_key, extent, pieces, low, top_value):
    gain = 1.0
    for dim, shards_of in pieces:
        draws = jax.random.uniform(jax.random.fold_in(jax.random.fold_in(stream_key, 6), dim), (shards_of,), jnp.float32, low / len(pieces), top_value / len(pieces))
        gain = gain * jnp.repeat(jnp.exp(draws), extent[dim] // shards_of).reshape((-1,) + (1,) * (len(extent) - 1 - dim))
    return gain


def assign_block(rng, own, number, rows, amount, top, reach, slope):
    ranking = jax.random.permutation(rng, amount)
    packed, usual = shares(amount, rows * top, reach, slope, True), shares(amount, rows * top, reach, slope, False)
    places = jnp.arange(amount)

    def named(lengths, offset_by):
        used = int((lengths > 0).sum())
        fixed = max(1, used // 4)
        shifted = fixed + (places - fixed + offset_by * (used - fixed)) % max(1, amount - fixed)
        return jnp.zeros((amount,), jnp.int32).at[ranking[jnp.where(places < fixed, places, shifted)]].set(jnp.asarray(lengths, jnp.int32))

    lengths = jnp.where(number % 4 == 0, named(packed, number // 4), named(usual, number - number // 4 - 1))
    mixed = jax.random.permutation(jax.random.fold_in(own, 3), amount)
    donor, receiver = mixed[0:amount // 2 * 2:2], mixed[1:amount // 2 * 2:2]
    slack = jnp.minimum(lengths[donor] - 1, reach - lengths[receiver]) // 2
    slack = jnp.where((donor == ranking[0]) | (receiver == ranking[0]) | (lengths[receiver] == 0), 0, jnp.maximum(slack, 0))
    shifted = jax.random.randint(jax.random.fold_in(own, 4), (amount // 2,), 0, 1 << 20) % (slack + 1)
    lengths = lengths.at[donor].add(-shifted).at[receiver].add(shifted)
    labels = jnp.searchsorted(jnp.cumsum(lengths), jnp.arange(rows * top), side="right").astype(jnp.int32)
    listing = labels.reshape(top, rows).T
    listing = listing[jax.random.permutation(jax.random.fold_in(own, 1), rows)]
    offset_by = jax.random.randint(jax.random.fold_in(own, 2), (rows, 1), 0, top)
    return jnp.take_along_axis(listing, (jnp.arange(top)[None, :] + offset_by) % top, axis=1)


def shares(count, total, reach, slope, full):
    portions = [(1 << 20) // math.isqrt(grade ** slope) + 1 for grade in range(1, count + 1)]
    largest = reach if full else min(reach, max(-(-total // count), total * portions[0] // sum(portions)))
    least = 1 if total - largest >= count - 1 else 0
    given, surplus = [largest] + [least] * (count - 1), total - largest - least * (count - 1)
    while surplus > 0:
        free = [i for i in range(1, count) if given[i] < largest] or [i for i in range(1, count) if given[i] < reach]
        whole, remaining = sum([portions[i] for i in free]), surplus
        for i in free:
            addition = min(reach - given[i], max(1, remaining * portions[i] // whole), surplus)
            given[i] = given[i] + addition
            surplus = surplus - addition
    return np.array(given)


def gaussian(own_key, shape, deviation, reach, cuts=(), kind=jnp.bfloat16):
    values = jax.random.normal(own_key, shape, jnp.float32) * deviation
    if len(cuts) > 0:
        values = block_scale(own_key, shape, cuts, -0.22, 0.18) * values
    return jnp.clip(values, min=-reach, max=reach).astype(kind)


def setup_inputs(seed: int = 0, part: int = 0) -> dict:
    splits = jax.random.split(jax.random.key(seed), 7)
    part_splits = jax.random.split(jax.random.fold_in(splits[6], part), 7)
    tokens = gaussian(part_splits[0], (TOKENS, D), 1.0, 6.0, ((0, 16), (1, 2)))
    expert_ids_keys = jax.random.split(jax.random.fold_in(part_splits[1], 1), TOKENS // TOK_DEV)
    expert_ids_turns = jax.random.permutation(jax.random.fold_in(part_splits[1], 3), TOKENS // TOK_DEV)
    expert_ids = jax.vmap(lambda own, number: assign_block(jax.random.fold_in(part_splits[1], 2), own, number, TOK_DEV, EXPERTS, TOP, CAP, 2))(expert_ids_keys, expert_ids_turns).reshape((TOKENS, TOP))
    route_weights = jnp.clip(jnp.exp(math.log(0.3) - 1.7917595 * jax.random.uniform(part_splits[2], (TOKENS, TOP), jnp.float32) ** block_scale(part_splits[2], (TOKENS, TOP), ((0, 16),), -0.2, 0.2)), 0.05, 0.3)
    w_gate = gaussian(splits[3], (EXPERTS, D, FF), D ** -0.5, 0.09375, ((0, 16), (1, 2)))
    w_up = gaussian(splits[4], (EXPERTS, D, FF), D ** -0.5, 0.09375, ((0, 16), (1, 2)))
    w_down = gaussian(splits[5], (EXPERTS, FF, D), FF ** -0.5, 0.21875, ((0, 16), (2, 2)))
    return dict(tokens=tokens, expert_ids=expert_ids, route_weights=route_weights, w_gate=w_gate, w_up=w_up, w_down=w_down)


def rounded(value):
    return lax.optimization_barrier(value.astype(jnp.bfloat16)).astype(jnp.float32)


def blockwise(rows, weight):
    quarter = D // N_TENSOR
    total = jnp.zeros((rows.shape[0], weight.shape[1]), jnp.float32)
    for block in range(N_TENSOR):
        lower = block * quarter
        part = jnp.dot(rows[:, lower:lower + quarter], weight[lower:lower + quarter], preferred_element_type=jnp.float32)
        total = total + rounded(part)
    return total


def reference(tokens, expert_ids, route_weights, w_gate, w_up, w_down):
    total_rows = tokens.shape[0]
    most = EXPERTS * CAP

    def one_expert(acc, expert):
        hits = expert_ids == expert
        weight = jnp.sum(jnp.where(hits, route_weights, 0.0), axis=1)
        chosen = jnp.any(hits, axis=1)
        picks = jnp.nonzero(chosen, size=most, fill_value=0)[0].astype(jnp.int32)
        live = jnp.arange(most, dtype=jnp.int32) < jnp.sum(chosen.astype(jnp.int32))
        rows = tokens[picks]
        gate = blockwise(rows, w_gate[expert])
        up = blockwise(rows, w_up[expert])
        hidden = (jax.nn.silu(gate) * up).astype(jnp.bfloat16)
        result = rounded(jnp.dot(hidden, w_down[expert], preferred_element_type=jnp.float32))
        term = jnp.where(live[:, None], weight[picks][:, None] * result, 0.0)
        return acc.at[picks].add(term), None

    start = jnp.zeros((total_rows, D), jnp.float32)
    acc = lax.scan(one_expert, start, jnp.arange(EXPERTS, dtype=jnp.int32))[0]
    return acc.astype(jnp.bfloat16)
```

```python
import jax
import jax.numpy as jnp
from jax import lax
from jax.sharding import PartitionSpec as P

F32 = jnp.float32
BF16 = jnp.bfloat16


def on_device(tokens, expert_ids, route_weights, w_gate, w_up, w_down):
    rows, width = tokens.shape
    top = expert_ids.shape[1]
    experts = lax.axis_size("expert") * lax.axis_size("dp")
    capacity = min(rows, max(2, 3 * rows * top // (2 * experts)))
    parts = lax.axis_size("tensor")
    me = lax.axis_index("expert") * lax.axis_size("dp") + lax.axis_index("dp")
    rank = lax.axis_index("tensor")
    ids = jnp.arange(experts, dtype=jnp.int32)
    hit = expert_ids[:, :, None] == ids[None, None, :]
    dense = jnp.sum(jnp.where(hit, route_weights[:, :, None], 0.0), axis=1)
    weights = lax.all_to_all(dense.T, ("expert", "dp"), split_axis=0, concat_axis=0, tiled=True)
    everyone = lax.all_gather(tokens, ("expert", "dp"), axis=0, tiled=True)
    live = weights > 0.0
    slot = jnp.cumsum(live.astype(jnp.int32), axis=1) - 1
    slot = jnp.where(live, slot, -1)
    pick = (slot[:, None, :] == jnp.arange(capacity, dtype=jnp.int32)[None, :, None]).astype(BF16)
    chosen = jnp.einsum("scn,snd->scd", pick, everyone.reshape(experts, rows, width), preferred_element_type=F32)
    chosen = chosen.astype(BF16).reshape(parts, experts * capacity // parts, width)
    gate_part = jnp.dot(chosen, w_gate[0], preferred_element_type=F32).astype(BF16)
    up_part = jnp.dot(chosen, w_up[0], preferred_element_type=F32).astype(BF16)
    both = jnp.concatenate([gate_part, up_part], axis=2)
    total = lax.dynamic_index_in_dim(both, rank, 0, keepdims=False).astype(F32)
    for step in range(1, parts):
        sent = lax.dynamic_index_in_dim(both, (rank + step) % parts, 0, keepdims=False)
        got = lax.ppermute(sent, "tensor", [(i, (i + step) % parts) for i in range(parts)])
        total = total + got.astype(F32)
    units = w_gate.shape[2]
    hidden = (jax.nn.silu(total[:, :units]) * total[:, units:]).astype(BF16)
    pieces = [hidden]
    for step in range(1, parts):
        pieces.append(lax.ppermute(hidden, "tensor", [(i, (i + step) % parts) for i in range(parts)]))
    order = (rank - jnp.arange(parts)) % parts
    hidden_all = jnp.stack(pieces)[order].reshape(experts, capacity, units)
    spread = jnp.einsum("scn,scf->snf", pick, hidden_all, preferred_element_type=F32).astype(BF16)
    result = jnp.dot(spread.reshape(experts * rows, units), w_down[0], preferred_element_type=F32)
    term = (result * weights.reshape(experts * rows)[:, None]).astype(BF16)
    return lax.psum_scatter(term, ("expert", "dp"), scatter_dimension=0, tiled=True)


def solution(mesh):
    placed = (
        P(("group", "expert", "dp"), "tensor"),
        P(("group", "expert", "dp"), None),
        P(("group", "expert", "dp"), None),
        P(("expert", "dp"), "tensor", None),
        P(("expert", "dp"), "tensor", None),
        P(("expert", "dp"), None, "tensor"),
    )
    return jax.shard_map(
        on_device,
        mesh=mesh,
        in_specs=placed,
        out_specs=P(("group", "expert", "dp"), "tensor"),
        check_vma=False,
    )
```

```python
import functools

import jax
import jax.numpy as jnp
from jax import lax
from jax.experimental import pallas as pl
from jax.experimental.pallas import tpu as pltpu
from jax.sharding import PartitionSpec as P

F32 = jnp.float32
BF16 = jnp.bfloat16
LANES = 128
VMEM = 48 * 1024 * 1024


def tile(extent, choices):
    for size in choices:
        if extent % size == 0:
            return size
    return extent


def slot_row(tails, me, experts, rows, capacity):
    total = tails.shape[0]
    column = lax.broadcasted_iota(jnp.int32, (8, tails.shape[1]), 1)
    mark = jnp.where((column == me) | (column == experts + me), 1.0, 0.0).astype(BF16)
    weight = lax.dot_general(mark, tails, (((1,), (1,)), ((), ())), preferred_element_type=F32)
    live = weight > 0.0
    above = lax.broadcasted_iota(jnp.int32, (total, total), 0)
    own = lax.broadcasted_iota(jnp.int32, (total, total), 1)
    ahead = jnp.where((above < own) & (above // rows == own // rows), 1.0, 0.0).astype(BF16)
    before = jnp.dot(jnp.where(live, 1.0, 0.0).astype(BF16), ahead, preferred_element_type=F32)
    base = lax.broadcasted_iota(jnp.int32, (8, total), 1) // rows * capacity
    return jnp.where(live, before.astype(jnp.int32) + base, -1)[0:1]


def slot_column(tails, me, experts, rows, capacity):
    total = tails.shape[0]
    column = lax.broadcasted_iota(jnp.int32, tails.shape, 1)
    mine = (column == me) | (column == experts + me)
    weight = jnp.sum(jnp.where(mine, tails.astype(F32), 0.0), axis=1, keepdims=True)
    live = weight > 0.0
    own = lax.broadcasted_iota(jnp.int32, (total, total), 0)
    above = lax.broadcasted_iota(jnp.int32, (total, total), 1)
    ahead = jnp.where((above < own) & (above // rows == own // rows), 1.0, 0.0).astype(BF16)
    flags = jnp.broadcast_to(jnp.where(live, 1.0, 0.0), (total, LANES)).astype(BF16)
    before = jnp.dot(ahead, flags, preferred_element_type=F32)[:, 0:1]
    base = lax.broadcasted_iota(jnp.int32, (total, 1), 0) // rows * capacity
    return jnp.where(live, before.astype(jnp.int32) + base, -1), weight


def pick_kernel(width, experts, capacity, me_ref, a_ref, b_ref, c_ref, d_ref, w_ref, chosen_ref, part_ref):
    rows = a_ref.shape[0]
    count = 4 * capacity

    @pl.when(pl.program_id(0) == 0)
    def _():
        blocks = (a_ref, b_ref, c_ref, d_ref)
        tails = jnp.concatenate([r[:, width:] for r in blocks], axis=0)
        slot = slot_row(tails, me_ref[0], experts, rows, capacity)
        place = lax.broadcasted_iota(jnp.int32, (count, 4 * rows), 0)
        pick = jnp.where(place == slot, 1.0, 0.0).astype(BF16)
        x = jnp.concatenate([r[:, :width] for r in blocks], axis=0)
        chosen_ref[...] = jnp.dot(pick, x, preferred_element_type=F32).astype(BF16)

    part_ref[...] = jnp.dot(chosen_ref[...], w_ref[...], preferred_element_type=F32).astype(BF16)


def pick_rows(me, blocks, weights, width, experts, capacity):
    rows, padded = blocks[0].shape
    columns = weights.shape[1]
    step = tile(columns, (256, 384))
    whole = pl.BlockSpec((rows, padded), lambda i: (0, 0))
    count = 4 * capacity
    return pl.pallas_call(
        functools.partial(pick_kernel, width, experts, capacity),
        grid=(columns // step,),
        out_shape=(
            jax.ShapeDtypeStruct((count, width), BF16),
            jax.ShapeDtypeStruct((count, columns), BF16),
        ),
        in_specs=[pl.BlockSpec(memory_space=pltpu.SMEM)] + [whole] * 4 + [pl.BlockSpec((width, step), lambda i: (0, i))],
        out_specs=(
            pl.BlockSpec((count, width), lambda i: (0, 0)),
            pl.BlockSpec((count, step), lambda i: (0, i)),
        ),
        compiler_params=pltpu.CompilerParams(vmem_limit_bytes=VMEM),
        cost_estimate=pl.CostEstimate(
            flops=2 * count * width * columns + 8 * count * rows * width,
            bytes_accessed=2 * (4 * rows * padded + width * columns + count * (width + columns)),
            transcendentals=0,
        ),
    )(me, *blocks, weights)


def down_kernel(experts, capacity, rows, pieces, me_ref, *refs):
    hidden_refs = refs[:pieces]
    tail_refs = refs[pieces:pieces + 4]
    w_ref, out_ref, spread_ref, weight_ref = refs[pieces + 4:]
    total = 4 * rows

    @pl.when(pl.program_id(0) == 0)
    def _():
        tails = jnp.concatenate([r[...] for r in tail_refs], axis=0)
        slot, weight = slot_column(tails, me_ref[0], experts, rows, capacity)
        place = lax.broadcasted_iota(jnp.int32, (total, 4 * capacity), 1)
        spread = jnp.where(place == slot, 1.0, 0.0).astype(BF16)
        units = hidden_refs[0].shape[1]
        for i, ref in enumerate(hidden_refs):
            value = jnp.dot(spread, ref[...], preferred_element_type=F32)
            spread_ref[:, i * units:(i + 1) * units] = value.astype(BF16)
        weight_ref[...] = weight

    result = jnp.dot(spread_ref[...], w_ref[...], preferred_element_type=F32)
    out_ref[...] = (result * weight_ref[...]).astype(BF16)


def down_rows(me, hiddens, blocks, weights, width, experts, capacity):
    rows, padded = blocks[0].shape
    units = weights.shape[0]
    step = tile(width, (512, 256))
    tail = pl.BlockSpec((rows, padded - width), lambda i: (0, width // (padded - width)))
    pieces = len(hiddens)
    return pl.pallas_call(
        functools.partial(down_kernel, experts, capacity, rows, pieces),
        grid=(width // step,),
        out_shape=jax.ShapeDtypeStruct((4 * rows, width), BF16),
        in_specs=[pl.BlockSpec(memory_space=pltpu.SMEM)]
        + [pl.BlockSpec(hiddens[0].shape, lambda i: (0, 0))] * pieces
        + [tail] * 4
        + [pl.BlockSpec((units, step), lambda i: (0, i))],
        out_specs=pl.BlockSpec((4 * rows, step), lambda i: (0, i)),
        scratch_shapes=[pltpu.VMEM((4 * rows, units), BF16), pltpu.VMEM((4 * rows, 1), F32)],
        compiler_params=pltpu.CompilerParams(vmem_limit_bytes=VMEM),
        cost_estimate=pl.CostEstimate(
            flops=8 * rows * units * (width + 4 * capacity),
            bytes_accessed=2 * (4 * rows * width + units * width + 4 * capacity * units),
            transcendentals=0,
        ),
    )(me, *hiddens, *blocks, weights)


def on_device(tokens, expert_ids, route_weights, w_gate, w_up, w_down):
    rows, width = tokens.shape
    top = expert_ids.shape[1]
    ring = lax.axis_size("expert")
    experts = ring * lax.axis_size("dp")
    capacity = min(rows, max(2, 3 * rows * top // (2 * experts)))
    parts = lax.axis_size("tensor")
    units = w_gate.shape[2] // parts
    me = lax.axis_index("expert") * lax.axis_size("dp") + lax.axis_index("dp")
    me = me.astype(jnp.int32).reshape(1)
    rank = lax.axis_index("tensor")
    hops = ring // 2

    def over_y(x):
        return lax.ppermute(x, "expert", [(i, i ^ 1) for i in range(ring)])

    def over_z(x):
        return lax.ppermute(x, "expert", [(i, (i + 2) % ring) for i in range(ring)])

    def over_core(x):
        return lax.ppermute(x, "dp", [(0, 1), (1, 0)])

    def over_x(x, step):
        return lax.ppermute(x, "tensor", [(i, (i + step) % parts) for i in range(parts)])

    ids = jnp.arange(experts, dtype=jnp.int32)
    hit = expert_ids[:, :, None] == ids[None, None, :]
    dense = jnp.sum(jnp.where(hit, route_weights[:, :, None], 0.0), axis=1)
    high = lax.reduce_precision(dense, 8, 7)
    low = dense - high
    spare = -(2 * experts) % LANES
    block = jnp.concatenate(
        [tokens, high.astype(BF16), low.astype(BF16), jnp.zeros((rows, spare), BF16)], axis=1
    )

    def unit_slice(w, offset, axis):
        return lax.dynamic_slice_in_dim(w, (rank + offset) % parts * units, units, axis)

    away = []
    for step in range(1, parts):
        away += [unit_slice(w_gate[0], step, 1), unit_slice(w_up[0], step, 1)]
    w_away = jnp.concatenate(away, axis=1)
    w_home = jnp.concatenate([unit_slice(w_gate[0], 0, 1), unit_slice(w_up[0], 0, 1)], axis=1)
    w_out = jnp.concatenate([unit_slice(w_down[0], parts - step, 0) for step in range(parts)], axis=0)

    carried = None
    own = None
    for hop in range(hops):
        if hop > 0:
            block = over_z(block)
        beside = over_y(block)
        blocks = (block, beside, over_core(block), over_core(beside))
        chosen, away_part = pick_rows(me, blocks, w_away, width, experts, capacity)
        got = [over_x(away_part[:, 2 * units * (s - 1):2 * units * s], s) for s in range(1, parts)]
        total = jnp.dot(chosen, w_home, preferred_element_type=F32)
        for piece in got:
            total = total + piece.astype(F32)
        hidden = (jax.nn.silu(total[:, :units]) * total[:, units:]).astype(BF16)
        hiddens = [hidden] + [over_x(hidden, s) for s in range(1, parts)]
        term = down_rows(me, hiddens, blocks, w_out, width, experts, capacity)
        pair = term[:2 * rows].astype(F32) + over_core(term[2 * rows:]).astype(F32)
        here = pair[:rows] + over_y(pair[rows:].astype(BF16)).astype(F32)
        if hop == 0:
            own = here
        else:
            if carried is not None:
                here = here + carried.astype(F32)
            carried = over_z(here.astype(BF16))
    if carried is not None:
        own = own + carried.astype(F32)
    return own.astype(BF16)


def solution(mesh):
    placed = (
        P(("group", "expert", "dp"), "tensor"),
        P(("group", "expert", "dp"), None),
        P(("group", "expert", "dp"), None),
        P(("expert", "dp"), "tensor", None),
        P(("expert", "dp"), "tensor", None),
        P(("expert", "dp"), None, "tensor"),
    )
    return jax.shard_map(
        on_device,
        mesh=mesh,
        in_specs=placed,
        out_specs=P(("group", "expert", "dp"), "tensor"),
        check_vma=False,
    )
```

```python
import functools

import jax
import jax.numpy as jnp
from jax import lax
from jax.experimental import pallas as pl
from jax.experimental.pallas import tpu as pltpu
from jax.sharding import PartitionSpec as P

F32 = jnp.float32
BF16 = jnp.bfloat16
LANES = 128
VMEM = 24 * 1024 * 1024
SMEM = pl.BlockSpec(memory_space=pltpu.SMEM)
ANY = pl.BlockSpec(memory_space=pl.ANY)


def tile(extent, choices):
    for size in choices:
        if extent % size == 0:
            return size
    return extent


def whole(x):
    return pl.BlockSpec(x.shape, lambda i: (0,) * len(x.shape))


def params():
    return pltpu.CompilerParams(vmem_limit_bytes=VMEM)


def cost():
    return pl.CostEstimate(flops=1, bytes_accessed=1, transcendentals=0)


def block_kernel(experts, tokens_ref, ids_ref, route_ref, out_ref):
    rows, width = tokens_ref.shape
    out_ref[:, :width] = tokens_ref[...]
    ids = ids_ref[...].T
    route = route_ref[...].T
    column = lax.broadcasted_iota(jnp.int32, (rows, out_ref.shape[1] - width), 1)
    expert = jnp.where(column < experts, column, column - experts)
    value = jnp.zeros(column.shape, F32)
    for k in range(ids.shape[1]):
        value = value + jnp.where(expert == ids[:, k:k + 1], route[:, k:k + 1], 0.0)
    high = value.astype(BF16).astype(F32)
    out_ref[:, width:] = jnp.where(column < experts, high, value - high).astype(BF16)


def make_block(tokens, expert_ids, route_weights, experts):
    rows, width = tokens.shape
    padded = width + 2 * experts + (-(2 * experts)) % LANES
    args = (tokens, expert_ids.T, route_weights.T)
    return pl.pallas_call(
        functools.partial(block_kernel, experts),
        grid=(1,),
        out_shape=jax.ShapeDtypeStruct((rows, padded), BF16),
        in_specs=[whole(a) for a in args],
        out_specs=pl.BlockSpec((rows, padded), lambda i: (0, 0)),
        compiler_params=params(),
        cost_estimate=cost(),
    )(*args)


def slot_row(tails, me, experts, rows, capacity):
    total = tails.shape[0]
    column = lax.broadcasted_iota(jnp.int32, (8, tails.shape[1]), 1)
    mark = jnp.where((column == me) | (column == experts + me), 1.0, 0.0).astype(BF16)
    weight = lax.dot_general(mark, tails, (((1,), (1,)), ((), ())), preferred_element_type=F32)
    live = weight > 0.0
    number = lax.broadcasted_iota(jnp.int32, (8, total), 1) // rows
    above = lax.broadcasted_iota(jnp.int32, (total, total), 0)
    own = lax.broadcasted_iota(jnp.int32, (total, total), 1)
    ahead = jnp.where((above < own) & (above >= (number * rows)[0:1]), 1.0, 0.0).astype(BF16)
    before = jnp.dot(jnp.where(live, 1.0, 0.0).astype(BF16), ahead, preferred_element_type=F32)
    return jnp.where(live, before.astype(jnp.int32) + number * capacity, -1)[0:1]


def slot_column(tails, me, experts, rows, capacity):
    total = tails.shape[0]
    column = lax.broadcasted_iota(jnp.int32, tails.shape, 1)
    mine = (column == me) | (column == experts + me)
    weight = jnp.sum(jnp.where(mine, tails.astype(F32), 0.0), axis=1, keepdims=True)
    live = weight > 0.0
    number = lax.broadcasted_iota(jnp.int32, (total, 1), 0) // rows
    own = lax.broadcasted_iota(jnp.int32, (total, total), 0)
    above = lax.broadcasted_iota(jnp.int32, (total, total), 1)
    ahead = jnp.where((above < own) & (above >= number * rows), 1.0, 0.0).astype(BF16)
    flags = jnp.broadcast_to(jnp.where(live, 1.0, 0.0), (total, LANES)).astype(BF16)
    before = jnp.dot(ahead, flags, preferred_element_type=F32)[:, 0:1]
    return jnp.where(live, before.astype(jnp.int32) + number * capacity, -1), weight


def layout(groups, capacity):
    offsets, total = [], 0
    for _, members in groups:
        offsets.append(total)
        total += -(-len(members) * capacity // 16) * 16
    return offsets + [total]


def multiply(x_ref, rows, weights, start, units, out_ref):
    def store(x, w, column, count):
        out_ref[rows, column:column + count] = jnp.dot(x, w, preferred_element_type=F32).astype(out_ref.dtype)

    x = x_ref[rows, :]
    if start is None:
        w_ref = weights[0]
        step = tile(w_ref.shape[1], (256, 384))
        for column in range(0, w_ref.shape[1], step):
            store(x, w_ref[:, column:column + step], column, step)
        return
    full = units // 256 * 256
    for i, ref in enumerate(weights):
        for column in range(0, full, 256):
            store(x, ref[:, pl.ds(pl.multiple_of(start + column, LANES), 256)], i * units + column, 256)
    if full < units:
        rest = pl.ds(pl.multiple_of(start + full, LANES), units - full)
        w = jnp.concatenate([ref[:, rest] for ref in weights], axis=1)
        y = jnp.dot(x, w, preferred_element_type=F32).astype(out_ref.dtype)
        out_ref[rows, full:units] = y[:, :units - full]
        out_ref[rows, units + full:] = y[:, units - full:]


def pick_kernel(width, experts, capacity, units, groups, count, kinds, split, copied, scalars, *refs):
    blocks, weights = refs[:count], refs[count:]
    if copied:
        *_, source_ref, chosen_ref, part_ref, target_ref, sem = refs
        copy = pltpu.make_async_copy(source_ref, target_ref, sem)
        copy.start()
    else:
        chosen_ref, part_ref = refs[-2:]
    rows = blocks[0].shape[0]
    offsets = layout(groups, capacity)
    step = tile(width, (512, 256))
    for g, (expert, members) in enumerate(groups):
        tails = jnp.concatenate([blocks[m][:, width:] for m in members], axis=0)
        slot = slot_row(tails, scalars[expert], experts, rows, capacity)
        here = offsets[g + 1] - offsets[g]
        place = lax.broadcasted_iota(jnp.int32, (here, len(members) * rows), 0)
        pick = jnp.where(place == slot, 1.0, 0.0).astype(BF16)
        for column in range(0, width, step):
            x = jnp.concatenate([blocks[m][:, column:column + step] for m in members], axis=0)
            value = jnp.dot(pick, x, preferred_element_type=F32).astype(BF16)
            chosen_ref[offsets[g]:offsets[g + 1], column:column + step] = value
    for g in range(len(groups)):
        mine = weights[kinds * g:kinds * (g + 1)]
        multiply(chosen_ref, slice(offsets[g], offsets[g + 1]), mine, scalars[2] if split else None, units, part_ref)
    if copied:
        copy.wait()


def pick_rows(scalars, groups, blocks, weights, split, copying, after, width, experts, capacity, units):
    columns = 2 * units if split else weights[0][0].shape[1]
    taken = layout(groups, capacity)[-1]
    flat = [w for expert, _ in groups for w in weights[expert]]
    kinds = len(weights[0])
    copied = len(copying)
    kernel = functools.partial(pick_kernel, width, experts, capacity, units, groups, len(blocks), kinds, split, copied)
    return pl.pallas_call(
        kernel,
        grid=(1,),
        out_shape=(
            jax.ShapeDtypeStruct((taken, width), BF16),
            jax.ShapeDtypeStruct((taken, columns), BF16),
            *[jax.ShapeDtypeStruct(a.shape, a.dtype) for a in copying],
        ),
        in_specs=[SMEM] + [whole(x) for x in (*blocks, *flat)] + [ANY] * (len(after) + copied),
        out_specs=(
            pl.BlockSpec((taken, width), lambda i: (0, 0)),
            pl.BlockSpec((taken, columns), lambda i: (0, 0)),
            *[ANY] * copied,
        ),
        scratch_shapes=[pltpu.SemaphoreType.DMA] * copied,
        compiler_params=params(),
        cost_estimate=cost(),
    )(scalars, *blocks, *flat, *after, *copying)


def home_kernel(capacity, units, groups, kinds, split, passed, scalars, x_ref, *refs):
    out_ref = refs[-1 - passed]
    offsets = layout(groups, capacity)
    for g in range(len(groups)):
        mine = refs[kinds * g:kinds * (g + 1)]
        multiply(x_ref, slice(offsets[g], offsets[g + 1]), mine, scalars[3] if split else None, units, out_ref)


def home_rows(scalars, groups, chosen, weights, split, passing, after, capacity, units):
    flat = [w for expert, _ in groups for w in weights[expert]]
    out = jax.ShapeDtypeStruct((chosen.shape[0], 2 * units), F32)
    args = (scalars, chosen, *flat, *after, *passing)
    result = pl.pallas_call(
        functools.partial(home_kernel, capacity, units, groups, len(weights[0]), split, len(passing)),
        grid=(1,),
        out_shape=(out, *[jax.ShapeDtypeStruct(p.shape, p.dtype) for p in passing]),
        in_specs=[SMEM, whole(chosen)] + [whole(w) for w in flat] + [ANY] * (len(after) + len(passing)),
        out_specs=(whole(out), *[ANY] * len(passing)),
        input_output_aliases={len(args) - len(passing) + i: 1 + i for i in range(len(passing))},
        compiler_params=params(),
        cost_estimate=cost(),
    )(*args)
    return result[0], result[1:]


def down_kernel(experts, capacity, groups, count, pieces, wide, passed, scalars, *refs):
    hiddens, refs = refs[:pieces], refs[pieces:]
    tail_refs, weights = refs[:count], refs[count:]
    scratch = refs[-2 * len(groups):]
    out_ref = refs[-2 * len(groups) - 1 - passed]
    rows = tail_refs[0].shape[0]
    units = hiddens[0].shape[1]
    offsets = layout(groups, capacity)
    starts = [scalars[4 + s] for s in range(pieces)]
    for g, (expert, members) in enumerate(groups):
        spread_ref, weight_ref = scratch[2 * g:2 * g + 2]
        tails = jnp.concatenate([tail_refs[m][...] for m in members], axis=0)
        slot, weight = slot_column(tails, scalars[expert], experts, rows, capacity)
        weight_ref[...] = weight
        place = lax.broadcasted_iota(jnp.int32, (len(members) * rows, offsets[g + 1] - offsets[g]), 1)
        spread = jnp.where(place == slot, 1.0, 0.0).astype(BF16)
        for s, ref in enumerate(hiddens):
            value = jnp.dot(spread, ref[offsets[g]:offsets[g + 1], :], preferred_element_type=F32).astype(BF16)
            if wide:
                spread_ref[:, pl.ds(pl.multiple_of(starts[s], LANES), units)] = value
            else:
                spread_ref[s] = value
    width = out_ref.shape[1]
    step = tile(width, (256,))

    @pl.loop(0, width // step)
    def _(i):
        span = pl.ds(pl.multiple_of(i * step, LANES), step)
        sums = [None] * count
        for g, (expert, members) in enumerate(groups):
            spread_ref, weight_ref = scratch[2 * g:2 * g + 2]
            w_ref = weights[g]
            if wide:
                result = jnp.dot(spread_ref[...], w_ref[:, span], preferred_element_type=F32)
            else:
                result = jnp.zeros((len(members) * rows, step), F32)
                for s in range(pieces):
                    w = w_ref[pl.ds(pl.multiple_of(starts[s], 16), units), span]
                    result = result + jnp.dot(spread_ref[s], w, preferred_element_type=F32)
            result = result * weight_ref[...]
            for k, m in enumerate(members):
                part = result[k * rows:(k + 1) * rows]
                sums[m] = part if sums[m] is None else sums[m] + part
        for m, value in enumerate(sums):
            out_ref[m * rows:(m + 1) * rows, span] = value.astype(BF16)


def down_rows(scalars, groups, hiddens, blocks, weights, passing, after, width, experts, capacity):
    rows, padded = blocks[0].shape
    units = hiddens[0].shape[1]
    pieces = len(hiddens)
    wide = units % LANES == 0
    tail = pl.BlockSpec((rows, padded - width), lambda i: (0, width // (padded - width)))
    scratch = []
    for _, members in groups:
        spread = (len(members) * rows, pieces * units) if wide else (pieces, len(members) * rows, units)
        scratch += [pltpu.VMEM(spread, BF16), pltpu.VMEM((len(members) * rows, 1), F32)]
    out = jax.ShapeDtypeStruct((len(blocks) * rows, width), BF16)
    args = (scalars, *hiddens, *blocks, *[weights[e] for e, _ in groups], *after, *passing)
    result = pl.pallas_call(
        functools.partial(down_kernel, experts, capacity, groups, len(blocks), pieces, wide, len(passing)),
        grid=(1,),
        out_shape=(out, *[jax.ShapeDtypeStruct(p.shape, p.dtype) for p in passing]),
        in_specs=[SMEM] + [whole(h) for h in hiddens] + [tail] * len(blocks)
        + [whole(weights[0])] * len(groups) + [ANY] * (len(after) + len(passing)),
        out_specs=(whole(out), *[ANY] * len(passing)),
        input_output_aliases={len(args) - len(passing) + i: 1 + i for i in range(len(passing))},
        scratch_shapes=scratch,
        compiler_params=params(),
        cost_estimate=cost(),
    )(*args)
    return result[0], result[1:]


def on_device(tokens, expert_ids, route_weights, w_gate, w_up, w_down):
    rows, width = tokens.shape
    top = expert_ids.shape[1]
    ring = lax.axis_size("expert")
    experts = ring * lax.axis_size("dp")
    capacity = min(rows, max(2, 3 * rows * top // (2 * experts)))
    parts = lax.axis_size("tensor")
    units = w_gate.shape[2] // parts
    core = lax.axis_index("dp")
    rank = lax.axis_index("tensor")
    hops = ring // 2

    def over_y(x):
        return lax.ppermute(x, "expert", [(i, i ^ 1) for i in range(ring)])

    def over_z(x):
        return lax.ppermute(x, "expert", [(i, (i + 2) % ring) for i in range(ring)])

    def over_core(x):
        return lax.ppermute(x, "dp", [(0, 1), (1, 0)])

    def over_x(x, step):
        return lax.ppermute(x, "tensor", [(i, (i + step) % parts) for i in range(parts)])

    first = lax.axis_index("expert") * 2
    scalars = [first + core, first + 1 - core, (rank + 1) % parts * units, rank * units]
    scalars += [(rank + parts - s) % parts * units for s in range(parts)]
    scalars = jnp.stack([jnp.asarray(s, jnp.int32) for s in scalars])
    gates = (w_gate[0], over_core(w_gate)[0])
    ups = (w_up[0], over_core(w_up)[0])
    split = parts == 2 and units % LANES == 0
    if split:
        away = home = tuple(zip(gates, ups))
    else:
        def unit_slice(w, offset):
            return lax.dynamic_slice_in_dim(w, (rank + offset) % parts * units, units, 1)

        away, home = [], []
        for gate, up in zip(gates, ups):
            pairs = [(unit_slice(gate, s), unit_slice(up, s)) for s in range(parts)]
            away.append((jnp.concatenate([w for pair in pairs[1:] for w in pair], axis=1),))
            home.append((jnp.concatenate(pairs[0], axis=1),))

    blocks, arrived = {(0, "s"): make_block(tokens, expert_ids, route_weights, experts)}, {}

    def send_on(hop):
        block = blocks[hop, "s"]
        if hop + 1 < hops:
            arrived[hop + 1] = over_z(block)
        blocks[hop, "b"] = over_y(block)

    both = ((0, (0, 1)), (1, (0, 1)))
    one = ((0, (0,)), (1, (0,)))
    plan = [([(0, "s")], ((0, (0,)),)), ([(0, "s"), (0, "b")], ((1, (0, 1)), (0, (1,)))), ([(1, "s")], one)]
    plan += [([(hop, "b"), (hop + 1, "s")], both) for hop in range(1, hops - 2)]
    plan += [([(hops - 2, "b"), (hops - 1, "b")], both), ([(hops - 1, "s")], one)]
    count = len(plan)
    chosen, parts_in, totals, hidden, returned = {}, {}, {}, {}, {}
    downs = [w_down[0]]
    order = [scalars]

    def pick(i):
        keys, groups = plan[i]
        mine = [blocks[k] for k in keys]
        copying = [w_down] if i == 1 else []
        chosen[i], part, *copies = pick_rows(
            scalars, groups, mine, away, split, copying, order, width, experts, capacity, units
        )
        downs.extend(over_core(c)[0] for c in copies)
        parts_in[i] = [over_x(part[:, 2 * units * (s - 1):2 * units * s], s) for s in range(1, parts)]
        order[:] = [part]

    def home_product(i, hop):
        passing = [arrived[hop]] if hop in arrived else []
        totals[i], passed = home_rows(scalars, plan[i][1], chosen[i], home, split, passing, order, capacity, units)
        order[:] = [totals[i]]
        if passing:
            blocks[hop, "s"] = passed[0]
            send_on(hop)

    def activate(i):
        total = totals[i]
        for piece in parts_in[i]:
            total = total + piece.astype(F32)
        value = (jax.nn.silu(total[:, :units]) * total[:, units:]).astype(BF16)
        hidden[i] = [value] + [over_x(value, s) for s in range(1, parts)]
        order.append(value)

    def down_product(i, hop):
        keys, groups = plan[i]
        mine = [blocks[k] for k in keys]
        passing = [arrived[hop]] if hop in arrived else []
        term, passed = down_rows(
            scalars, groups, hidden[i], mine, downs, passing, order, width, experts, capacity
        )
        order[:] = [term]
        if passing:
            blocks[hop, "s"] = passed[0]
            send_on(hop)
        for k, (at, kind) in enumerate(keys):
            piece = term[k * rows:(k + 1) * rows]
            if kind == "b":
                piece = over_y(piece)
            returned.setdefault(at, []).append(piece)

    arriving = []

    def add_hop(hop):
        total = sum(x.astype(F32) for x in returned[hop])
        if hop > 0:
            total = total.astype(BF16)
            arriving.append(lax.ppermute(total, "expert", [(i, (i - 2 * hop) % ring) for i in range(ring)]))
        else:
            arriving.append(total)
        order.append(total)

    send_on(0)
    added = 0
    for i in range(count + 2):
        if i == 1:
            activate(0)
        if i < count:
            pick(i)
        if 1 <= i - 1 < count:
            activate(i - 1)
        if i < count:
            home_product(i, {0: 1, 2: 2}.get(i))
        if (5 <= i < count or i > count) and added < hops - 2:
            add_hop(added)
            added += 1
        if 0 <= i - 2 < count:
            down_product(i - 2, i if i >= 3 else None)
    for hop in range(added, hops):
        add_hop(hop)
    return sum(x.astype(F32) for x in arriving).astype(BF16)


def solution(mesh):
    placed = (
        P(("group", "expert", "dp"), "tensor"),
        P(("group", "expert", "dp"), None),
        P(("group", "expert", "dp"), None),
        P(("expert", "dp"), "tensor", None),
        P(("expert", "dp"), "tensor", None),
        P(("expert", "dp"), None, "tensor"),
    )
    return jax.shard_map(
        on_device,
        mesh=mesh,
        in_specs=placed,
        out_specs=P(("group", "expert", "dp"), "tensor"),
        check_vma=False,
    )
```

```python
import functools

import jax
import jax.numpy as jnp
from jax import lax
from jax.experimental import pallas as pl
from jax.experimental.pallas import tpu as pltpu
from jax.sharding import PartitionSpec as P

F32 = jnp.float32
BF16 = jnp.bfloat16
LANES = 128
VMEM = 24 * 1024 * 1024
SMEM = pl.BlockSpec(memory_space=pltpu.SMEM)
ANY = pl.BlockSpec(memory_space=pl.ANY)
HBM = pl.BlockSpec(memory_space=pltpu.HBM)


def whole(x):
    return pl.BlockSpec(x.shape, lambda i: (0,) * len(x.shape))


def params():
    return pltpu.CompilerParams(vmem_limit_bytes=VMEM)


def cost():
    return pl.CostEstimate(flops=1, bytes_accessed=1, transcendentals=0)


def block_kernel(experts, tokens_ref, ids_ref, route_ref, out_ref, ids_buffer, route_buffer, sems):
    rows, width = tokens_ref.shape
    copies = [
        pltpu.make_async_copy(ids_ref, ids_buffer, sems.at[0]),
        pltpu.make_async_copy(route_ref, route_buffer, sems.at[1]),
        pltpu.make_async_copy(tokens_ref, out_ref.at[:, :width], sems.at[2]),
    ]
    for copy in copies:
        copy.start()
    copies[0].wait()
    copies[1].wait()
    ids = ids_buffer[...].T
    route = route_buffer[...].T
    column = lax.broadcasted_iota(jnp.int32, (rows, out_ref.shape[1] - width), 1)
    expert = jnp.where(column < experts, column, column - experts)
    value = jnp.zeros(column.shape, F32)
    for k in range(ids.shape[1]):
        value = value + jnp.where(expert == ids[:, k:k + 1], route[:, k:k + 1], 0.0)
    high = value.astype(BF16).astype(F32)
    out_ref[:, width:] = jnp.where(column < experts, high, value - high).astype(BF16)
    copies[2].wait()


def make_block(tokens, expert_ids, route_weights, experts):
    rows, width = tokens.shape
    padded = width + 2 * experts + (-(2 * experts)) % LANES
    args = (tokens, expert_ids.T, route_weights.T)
    return pl.pallas_call(
        functools.partial(block_kernel, experts),
        grid=(1,),
        out_shape=jax.ShapeDtypeStruct((rows, padded), BF16),
        in_specs=[HBM] * 3,
        out_specs=pl.BlockSpec((rows, padded), lambda i: (0, 0)),
        scratch_shapes=[
            pltpu.VMEM(args[1].shape, jnp.int32),
            pltpu.VMEM(args[2].shape, F32),
            pltpu.SemaphoreType.DMA((3,)),
        ],
        compiler_params=params(),
        cost_estimate=cost(),
    )(*args)


def layout(groups, capacity):
    offsets = [0]
    for _, members in groups:
        offsets.append(offsets[-1] + -(-len(members) * capacity // 16) * 16)
    return offsets


def slot_rows(tails, expert, experts, rows, capacity):
    total = tails.shape[0]
    column = lax.broadcasted_iota(jnp.int32, (8, tails.shape[1]), 1)
    mark = jnp.where((column == expert) | (column == experts + expert), 1.0, 0.0).astype(BF16)
    weight = lax.dot_general(mark, tails, (((1,), (1,)), ((), ())), preferred_element_type=F32)
    live = weight > 0.0
    number = lax.broadcasted_iota(jnp.int32, (8, total), 1) // rows
    above = lax.broadcasted_iota(jnp.int32, (total, total), 0)
    own = lax.broadcasted_iota(jnp.int32, (total, total), 1)
    ahead = jnp.where((above < own) & (above >= (number * rows)[0:1]), 1.0, 0.0).astype(BF16)
    before = jnp.dot(jnp.where(live, 1.0, 0.0).astype(BF16), ahead, preferred_element_type=F32)
    return jnp.where(live, before.astype(jnp.int32) + number * capacity, -1)[0:1]


def slot_columns(tails, expert, experts, rows, capacity):
    total = tails.shape[0]
    column = lax.broadcasted_iota(jnp.int32, tails.shape, 1)
    mine = (column == expert) | (column == experts + expert)
    weight = jnp.sum(jnp.where(mine, tails.astype(F32), 0.0), axis=1, keepdims=True)
    live = weight > 0.0
    number = lax.broadcasted_iota(jnp.int32, (total, 1), 0) // rows
    own = lax.broadcasted_iota(jnp.int32, (total, total), 0)
    above = lax.broadcasted_iota(jnp.int32, (total, total), 1)
    ahead = jnp.where((above < own) & (above >= number * rows), 1.0, 0.0).astype(BF16)
    flags = jnp.broadcast_to(jnp.where(live, 1.0, 0.0), (total, LANES)).astype(BF16)
    before = jnp.dot(ahead, flags, preferred_element_type=F32)[:, 0:1]
    return jnp.where(live, before.astype(jnp.int32) + number * capacity, -1), weight


def ordered_call(kernel, outs, specs, args, passing, after, copying=()):
    operands = (*args, *after, *copying, *passing)
    base = len(operands) - len(passing)
    kept, handed, copied = len(outs), len(passing), len(copying)
    token = jax.ShapeDtypeStruct((8, LANES), F32)

    def with_token(*refs):
        results = refs[len(operands):]
        sources = refs[base - copied:base]
        targets = results[kept + handed:kept + handed + copied]
        copies = [pltpu.make_async_copy(a, b, results[-1].at[i]) for i, (a, b) in enumerate(zip(sources, targets))]
        for copy in copies:
            copy.start()
        results[kept + handed + copied][...] = jnp.zeros(token.shape, token.dtype)
        kernel(*refs[:len(args)], *results[:kept])
        for copy in copies:
            copy.wait()

    results = pl.pallas_call(
        with_token,
        grid=(1,),
        out_shape=(*outs, *[jax.ShapeDtypeStruct(p.shape, p.dtype) for p in (*passing, *copying)], token),
        in_specs=specs + [ANY] * (len(after) + copied + handed),
        out_specs=(*[whole(o) for o in outs], *[ANY] * (handed + copied), whole(token)),
        input_output_aliases={base + i: kept + i for i in range(handed)},
        scratch_shapes=[pltpu.SemaphoreType.DMA((copied,))] if copied else [],
        compiler_params=params(),
        cost_estimate=cost(),
    )(*operands)
    return results[:kept], results[kept:kept + handed], results[kept + handed:-1], results[-1]


def select_kernel(width, experts, capacity, groups, count, scalars, *refs):
    blocks, outs = refs[:count], refs[count:]
    rows = blocks[0].shape[0]
    step = 512
    for (expert, members), out_ref in zip(groups, outs):
        tails = jnp.concatenate([blocks[m][:, width:] for m in members], axis=0)
        slot = slot_rows(tails, scalars[expert], experts, rows, capacity)
        place = lax.broadcasted_iota(jnp.int32, (out_ref.shape[0], len(members) * rows), 0)
        pick = jnp.where(place == slot, 1.0, 0.0).astype(BF16)
        for column in range(0, width, step):
            x = jnp.concatenate([blocks[m][:, column:column + step] for m in members], axis=0)
            out_ref[:, column:column + step] = jnp.dot(pick, x, preferred_element_type=F32).astype(BF16)


def select_rows(scalars, groups, blocks, copying, after, width, experts, capacity):
    kernel = functools.partial(select_kernel, width, experts, capacity, groups, len(blocks))
    offsets = layout(groups, capacity)
    outs = [jax.ShapeDtypeStruct((b - a, width), BF16) for a, b in zip(offsets, offsets[1:])]
    specs = [SMEM] + [whole(b) for b in blocks]
    return ordered_call(kernel, outs, specs, (scalars, *blocks), [], after, copying)


def round_kernel(count, scalars, *refs):
    out_ref = refs[-1]
    units = out_ref.shape[1] // 2
    columns = pl.ds(pl.multiple_of(scalars[2], LANES), units)
    start = 0
    for g in range(count):
        rows = slice(start, start + refs[2 * g].shape[0])
        start = rows.stop
        for half in range(2):
            out_ref[rows, half * units:(half + 1) * units] = refs[2 * g + half][:, columns].astype(BF16)


def away_part(scalars, products, units, after):
    total = sum(p.shape[0] for p in products[::2])
    out = jax.ShapeDtypeStruct((total, 2 * units), BF16)
    kernel = functools.partial(round_kernel, len(products) // 2)
    return ordered_call(kernel, [out], [SMEM] + [whole(p) for p in products], (scalars, *products), [], after)


def act_kernel(count, scalars, in_ref, *refs):
    out_ref = refs[-1]
    units = out_ref.shape[1]
    columns = pl.ds(pl.multiple_of(scalars[3], LANES), units)
    start = 0
    for g in range(count):
        rows = slice(start, start + refs[2 * g].shape[0])
        start = rows.stop
        gate = refs[2 * g][:, columns] + in_ref[rows, :units].astype(F32)
        up = refs[2 * g + 1][:, columns] + in_ref[rows, units:].astype(F32)
        out_ref[rows, :] = (gate / (1.0 + jnp.exp(-gate)) * up).astype(BF16)


def activated(scalars, products, part, passing, after):
    rows, columns = part.shape
    out = jax.ShapeDtypeStruct((rows, columns // 2), BF16)
    specs = [SMEM, whole(part)] + [whole(p) for p in products]
    kernel = functools.partial(act_kernel, len(products) // 2)
    return ordered_call(kernel, [out], specs, (scalars, part, *products), passing, after)


def join_kernel(scalars, own_ref, other_ref, *outs):
    units = own_ref.shape[1]
    start = 0
    for out_ref in outs:
        rows = slice(start, start + out_ref.shape[0])
        start = rows.stop
        for place, ref in ((scalars[3], own_ref), (scalars[2], other_ref)):
            out_ref[:, pl.ds(pl.multiple_of(place, LANES), units)] = ref[rows, :]


def joined(scalars, own, other, sizes, passing, after):
    outs = [jax.ShapeDtypeStruct((n, 2 * own.shape[1]), BF16) for n in sizes]
    specs = [SMEM, whole(own), whole(other)]
    return ordered_call(join_kernel, outs, specs, (scalars, own, other), passing, after)


def expand_kernel(experts, capacity, groups, count, scalars, *refs):
    results, tail_refs = refs[:len(groups)], refs[len(groups):len(groups) + count]
    out_ref = refs[-1]
    rows = tail_refs[0].shape[0]
    spreads, weights = [], []
    for (expert, members), ref in zip(groups, results):
        tails = jnp.concatenate([tail_refs[m][...] for m in members], axis=0)
        slot, weight = slot_columns(tails, scalars[expert], experts, rows, capacity)
        place = lax.broadcasted_iota(jnp.int32, (len(members) * rows, ref.shape[0]), 1)
        spreads.append(jnp.where(place == slot, 1.0, 0.0).astype(BF16))
        weights.append(weight)
    step = 512
    for column in range(0, out_ref.shape[1], step):
        sums = [None] * count
        for (_, members), ref, spread, weight in zip(groups, results, spreads, weights):
            value = ref[:, column:column + step].astype(BF16)
            value = jnp.dot(spread, value, preferred_element_type=F32) * weight
            for k, m in enumerate(members):
                piece = value[k * rows:(k + 1) * rows]
                sums[m] = piece if sums[m] is None else sums[m] + piece
        for m, value in enumerate(sums):
            out_ref[m * rows:(m + 1) * rows, column:column + step] = value.astype(BF16)


def expand_rows(scalars, groups, results, blocks, passing, after, experts, capacity):
    rows, padded = blocks[0].shape
    width = results[0].shape[1]
    tail = pl.BlockSpec((rows, padded - width), lambda i: (0, width // (padded - width)))
    kernel = functools.partial(expand_kernel, experts, capacity, groups, len(blocks))
    out = jax.ShapeDtypeStruct((len(blocks) * rows, width), BF16)
    specs = [SMEM] + [whole(r) for r in results] + [tail] * len(blocks)
    return ordered_call(kernel, [out], specs, (scalars, *results, *blocks), passing, after)


def add_kernel(*refs):
    out_ref = refs[-1]
    total = refs[0][...].astype(F32)
    for ref in refs[1:-1]:
        total = total + ref[...].astype(F32)
    out_ref[...] = total.astype(out_ref.dtype)


def added(terms, kind, after):
    out = jax.ShapeDtypeStruct(terms[0].shape, kind)
    return ordered_call(add_kernel, [out], [whole(t) for t in terms], tuple(terms), [], after)


def on_device(tokens, expert_ids, route_weights, w_gate, w_up, w_down):
    rows, width = tokens.shape
    top = expert_ids.shape[1]
    ring = lax.axis_size("expert")
    experts = ring * lax.axis_size("dp")
    capacity = min(rows, max(2, 3 * rows * top // (2 * experts)))
    parts = lax.axis_size("tensor")
    units = w_gate.shape[2] // parts
    core = lax.axis_index("dp")
    rank = lax.axis_index("tensor")
    hops = ring // 2
    aligned = parts == 2 and units % LANES == 0

    def over_y(x):
        return lax.ppermute(x, "expert", [(i, i ^ 1) for i in range(ring)])

    def over_z(x):
        return lax.ppermute(x, "expert", [(i, (i + 2) % ring) for i in range(ring)])

    def home_over_z(x, hop):
        return lax.ppermute(x, "expert", [(i, (i - 2 * hop) % ring) for i in range(ring)])

    def home_over_both(x, hop):
        return lax.ppermute(x, "expert", [(i, ((i - 2 * hop) % ring) ^ 1) for i in range(ring)])

    def over_core(x):
        return lax.ppermute(x, "dp", [(0, 1), (1, 0)])

    def over_x(x, step):
        return lax.ppermute(x, "tensor", [(i, (i + step) % parts) for i in range(parts)])

    first = lax.axis_index("expert") * 2
    scalars = jnp.stack([first + core, first + 1 - core, (rank + 1) % parts * units, rank * units]).astype(jnp.int32)
    gates = [w_gate[0], over_core(w_gate)[0]]
    ups = [w_up[0], over_core(w_up)[0]]
    downs = [w_down[0]]

    blocks, arrived = {(0, "s"): make_block(tokens, expert_ids, route_weights, experts)}, {}

    def send_on(hop):
        block = blocks[hop, "s"]
        if hop + 1 < hops:
            arrived[hop + 1] = over_z(block)
        blocks[hop, "b"] = over_y(block)

    def passing(hop):
        return [arrived[hop]] if hop in arrived else []

    def take_on(hop, passed):
        if passed:
            blocks[hop, "s"] = passed[0]
            send_on(hop)

    both = ((0, (0, 1)), (1, (0, 1)))
    plan = [([(0, "s")], ((0, (0,)),)), ([(0, "s"), (0, "b"), (1, "s")], ((1, (0, 1, 2)), (0, (1, 2))))]
    plan += [([(hop - 1, "b"), (hop, "s")], both) for hop in range(2, hops - 1)]
    plan += [([(hops - 2, "b"), (hops - 1, "b")], both), ([(hops - 1, "s")], ((0, (0,)), (1, (0,))))]
    count = len(plan)
    order = []
    rows_in, products, parts_in, hidden, results, own_part = {}, {}, {}, {}, {}, {}
    arriving, gathered = [], []

    def select(i):
        keys, groups = plan[i]
        copying = [w_down] if i == 1 else []
        rows_in[i], _, copies, token = select_rows(
            scalars, groups, [blocks[k] for k in keys], copying, order, width, experts, capacity
        )
        downs.extend(over_core(c)[0] for c in copies)
        order[:] = [token]

    def multiply(i):
        products[i] = []
        for (expert, _), x in zip(plan[i][1], rows_in[i]):
            for w in (gates[expert], ups[expert]):
                products[i].append(jnp.dot(x, w, preferred_element_type=F32))
        if aligned:
            (part,), _, _, token = away_part(scalars, products[i], units, order)
            parts_in[i] = [over_x(part, 1)]
            order[:] = [token]
            return
        gate, up = jnp.concatenate(products[i][::2], axis=0), jnp.concatenate(products[i][1::2], axis=0)
        parts_in[i] = []
        for step in range(parts):
            start = (rank + step) % parts * units
            part = jnp.concatenate([lax.dynamic_slice_in_dim(w, start, units, 1) for w in (gate, up)], axis=1)
            if step > 0:
                part = over_x(part.astype(BF16), step)
            parts_in[i].append(part)

    def activate(i, hop):
        if aligned:
            (value,), passed, _, token = activated(scalars, products[i], parts_in[i][0], passing(hop), order)
            order[:] = [token]
            take_on(hop, passed)
        else:
            total = sum(p.astype(F32) for p in parts_in[i])
            value = (jax.nn.silu(total[:, :units]) * total[:, units:]).astype(BF16)
            take_on(hop, passing(hop))
        hidden[i] = [value] + [over_x(value, s) for s in range(1, parts)]

    def down_product(i, hop):
        offsets = layout(plan[i][1], capacity)
        if aligned:
            sizes = [b - a for a, b in zip(offsets, offsets[1:])]
            values, passed, _, token = joined(scalars, *hidden[i], sizes, passing(hop), order)
            order[:] = [token]
            take_on(hop, passed)
        else:
            behind = (rank - jnp.arange(parts)) % parts
            value = jnp.moveaxis(jnp.stack(hidden[i])[behind], 0, 1).reshape(offsets[-1], -1)
            values = [value[a:b] for a, b in zip(offsets, offsets[1:])]
            take_on(hop, passing(hop))
        results[i] = []
        for (expert, _), value in zip(plan[i][1], values):
            results[i].append(jnp.dot(value, downs[expert], preferred_element_type=F32))

    def expand(i, hop):
        keys, groups = plan[i]
        (term,), passed, _, token = expand_rows(
            scalars, groups, results[i], [blocks[k] for k in keys], passing(hop), order, experts, capacity
        )
        order[:] = [token]
        take_on(hop, passed)
        for k, (at, kind) in enumerate(keys):
            piece = term[k * rows:(k + 1) * rows]
            direct = at >= hops - 2
            if kind == "s" and at == 0:
                gathered.append(piece)
            elif kind == "s" and direct:
                arriving.append((i, home_over_z(piece, at)))
            elif kind == "s":
                own_part[at] = piece
            elif direct:
                arriving.append((i, home_over_both(piece, at)))
            else:
                own_part[at, "b"] = over_y(piece)

    def add_hop(hop):
        if hop == 0:
            gathered.append(own_part[hop, "b"])
        elif hop < hops - 2:
            (total,), _, _, token = added([own_part[hop], own_part[hop, "b"]], BF16, order)
            order[:] = [token]
            arriving.append((hop + 2, home_over_z(total, hop)))

    def gather(unit):
        here = [x for i, x in arriving if i <= unit]
        arriving[:] = [(i, x) for i, x in arriving if i > unit]
        if len(gathered) + len(here) > 1:
            (total,), _, _, token = added(gathered + here, F32, order)
            gathered[:] = [total]
            order[:] = [token]

    send_on(0)
    select(0)
    multiply(0)
    activate(0, 1)
    for i in range(1, count + 1):
        if i > 2:
            activate(i - 1, None)
        if i < count:
            select(i)
            multiply(i)
        if i == 2:
            activate(1, None)
        if i >= 3:
            add_hop(i - 3)
            gather(i - 3)
        down_product(i - 1, i + 1 if i > 1 else None)
        expand(i - 1, 2 if i == 1 else None)
    for hop in range(count - 2, hops):
        add_hop(hop)
    return sum(x.astype(F32) for x in gathered + [x for _, x in arriving]).astype(BF16)


def solution(mesh):
    placed = (
        P(("group", "expert", "dp"), "tensor"),
        P(("group", "expert", "dp"), None),
        P(("group", "expert", "dp"), None),
        P(("expert", "dp"), "tensor", None),
        P(("expert", "dp"), "tensor", None),
        P(("expert", "dp"), None, "tensor"),
    )
    return jax.shard_map(
        on_device,
        mesh=mesh,
        in_specs=placed,
        out_specs=P(("group", "expert", "dp"), "tensor"),
        check_vma=False,
    )
```

```python
import functools

import jax
import jax.numpy as jnp
from jax import lax
from jax.experimental import pallas as pl
from jax.experimental.pallas import tpu as pltpu
from jax.sharding import PartitionSpec as P

F32 = jnp.float32
BF16 = jnp.bfloat16
LANES = 128
VMEM = 12 * 1024 * 1024
SMEM = pl.BlockSpec(memory_space=pltpu.SMEM)
ANY = pl.BlockSpec(memory_space=pl.ANY)
HBM = pl.BlockSpec(memory_space=pltpu.HBM)


def tile(extent, choices):
    for size in choices:
        if extent % size == 0:
            return size
    return extent


def whole(x):
    return pl.BlockSpec(x.shape, lambda i: (0,) * len(x.shape))


def params():
    return pltpu.CompilerParams(vmem_limit_bytes=VMEM)


def cost():
    return pl.CostEstimate(flops=1, bytes_accessed=1, transcendentals=0)


def block_kernel(experts, tokens_ref, ids_ref, route_ref, out_ref, ids_buffer, route_buffer, sems):
    rows, width = tokens_ref.shape
    copies = [
        pltpu.make_async_copy(ids_ref, ids_buffer, sems.at[0]),
        pltpu.make_async_copy(route_ref, route_buffer, sems.at[1]),
        pltpu.make_async_copy(tokens_ref, out_ref.at[:, :width], sems.at[2]),
    ]
    for copy in copies:
        copy.start()
    copies[0].wait()
    copies[1].wait()
    ids = ids_buffer[...].T
    route = route_buffer[...].T
    column = lax.broadcasted_iota(jnp.int32, (rows, out_ref.shape[1] - width), 1)
    expert = jnp.where(column < experts, column, column - experts)
    value = jnp.zeros(column.shape, F32)
    for k in range(ids.shape[1]):
        value = value + jnp.where(expert == ids[:, k:k + 1], route[:, k:k + 1], 0.0)
    high = value.astype(BF16).astype(F32)
    out_ref[:, width:] = jnp.where(column < experts, high, value - high).astype(BF16)
    copies[2].wait()


def make_block(tokens, expert_ids, route_weights, experts):
    rows, width = tokens.shape
    padded = width + 2 * experts + (-(2 * experts)) % LANES
    args = (tokens, expert_ids.T, route_weights.T)
    return pl.pallas_call(
        functools.partial(block_kernel, experts),
        grid=(1,),
        out_shape=jax.ShapeDtypeStruct((rows, padded), BF16),
        in_specs=[HBM] * 3,
        out_specs=pl.BlockSpec((rows, padded), lambda i: (0, 0)),
        scratch_shapes=[
            pltpu.VMEM(args[1].shape, jnp.int32),
            pltpu.VMEM(args[2].shape, F32),
            pltpu.SemaphoreType.DMA((3,)),
        ],
        compiler_params=params(),
        cost_estimate=cost(),
    )(*args)


def slot_row(tails, me, experts, rows, capacity):
    total = tails.shape[0]
    column = lax.broadcasted_iota(jnp.int32, (8, tails.shape[1]), 1)
    mark = jnp.where((column == me) | (column == experts + me), 1.0, 0.0).astype(BF16)
    weight = lax.dot_general(mark, tails, (((1,), (1,)), ((), ())), preferred_element_type=F32)
    live = weight > 0.0
    number = lax.broadcasted_iota(jnp.int32, (8, total), 1) // rows
    above = lax.broadcasted_iota(jnp.int32, (total, total), 0)
    own = lax.broadcasted_iota(jnp.int32, (total, total), 1)
    ahead = jnp.where((above < own) & (above >= (number * rows)[0:1]), 1.0, 0.0).astype(BF16)
    before = jnp.dot(jnp.where(live, 1.0, 0.0).astype(BF16), ahead, preferred_element_type=F32)
    return jnp.where(live, before.astype(jnp.int32) + number * capacity, -1)[0:1]


def slot_column(tails, me, experts, rows, capacity):
    total = tails.shape[0]
    column = lax.broadcasted_iota(jnp.int32, tails.shape, 1)
    mine = (column == me) | (column == experts + me)
    weight = jnp.sum(jnp.where(mine, tails.astype(F32), 0.0), axis=1, keepdims=True)
    live = weight > 0.0
    number = lax.broadcasted_iota(jnp.int32, (total, 1), 0) // rows
    own = lax.broadcasted_iota(jnp.int32, (total, total), 0)
    above = lax.broadcasted_iota(jnp.int32, (total, total), 1)
    ahead = jnp.where((above < own) & (above >= number * rows), 1.0, 0.0).astype(BF16)
    flags = jnp.broadcast_to(jnp.where(live, 1.0, 0.0), (total, LANES)).astype(BF16)
    before = jnp.dot(ahead, flags, preferred_element_type=F32)[:, 0:1]
    return jnp.where(live, before.astype(jnp.int32) + number * capacity, -1), weight


def layout(groups, capacity):
    offsets, total = [], 0
    for _, members in groups:
        offsets.append(total)
        total += -(-len(members) * capacity // 16) * 16
    return offsets + [total]


def multiply(x_ref, rows, weights, start, units, out_ref):
    def store(x, w, column, count):
        out_ref[rows, column:column + count] = jnp.dot(x, w, preferred_element_type=F32).astype(out_ref.dtype)

    x = x_ref[rows, :]
    if start is None:
        w_ref = weights[0]
        step = tile(w_ref.shape[1], (256, 384))
        for column in range(0, w_ref.shape[1], step):
            store(x, w_ref[:, column:column + step], column, step)
        return
    full = units // 256 * 256
    for i, ref in enumerate(weights):
        for column in range(0, full, 256):
            store(x, ref[:, pl.ds(pl.multiple_of(start + column, LANES), 256)], i * units + column, 256)
    if full < units:
        rest = pl.ds(pl.multiple_of(start + full, LANES), units - full)
        w = jnp.concatenate([ref[:, rest] for ref in weights], axis=1)
        y = jnp.dot(x, w, preferred_element_type=F32).astype(out_ref.dtype)
        out_ref[rows, full:units] = y[:, :units - full]
        out_ref[rows, units + full:] = y[:, units - full:]


def pick_kernel(width, experts, capacity, units, groups, count, kinds, split, scalars, *refs):
    blocks, weights = refs[:count], refs[count:]
    chosen_ref, part_ref = refs[-2:]
    rows = blocks[0].shape[0]
    offsets = layout(groups, capacity)
    step = tile(width, (512, 256))
    for g, (expert, members) in enumerate(groups):
        tails = jnp.concatenate([blocks[m][:, width:] for m in members], axis=0)
        slot = slot_row(tails, scalars[expert], experts, rows, capacity)
        here = offsets[g + 1] - offsets[g]
        place = lax.broadcasted_iota(jnp.int32, (here, len(members) * rows), 0)
        pick = jnp.where(place == slot, 1.0, 0.0).astype(BF16)
        for column in range(0, width, step):
            x = jnp.concatenate([blocks[m][:, column:column + step] for m in members], axis=0)
            value = jnp.dot(pick, x, preferred_element_type=F32).astype(BF16)
            chosen_ref[offsets[g]:offsets[g + 1], column:column + step] = value
    for g in range(len(groups)):
        mine = weights[kinds * g:kinds * (g + 1)]
        multiply(chosen_ref, slice(offsets[g], offsets[g + 1]), mine, scalars[2] if split else None, units, part_ref)


def pick_rows(scalars, groups, blocks, weights, split, after, width, experts, capacity, units):
    columns = 2 * units if split else weights[0][0].shape[1]
    taken = layout(groups, capacity)[-1]
    flat = [w for expert, _ in groups for w in weights[expert]]
    kernel = functools.partial(
        pick_kernel, width, experts, capacity, units, groups, len(blocks), len(weights[0]), split
    )
    out = (jax.ShapeDtypeStruct((taken, width), BF16), jax.ShapeDtypeStruct((taken, columns), BF16))
    return pl.pallas_call(
        kernel,
        grid=(1,),
        out_shape=out,
        in_specs=[SMEM] + [whole(x) for x in (*blocks, *flat)] + [ANY] * len(after),
        out_specs=tuple(whole(o) for o in out),
        compiler_params=params(),
        cost_estimate=cost(),
    )(scalars, *blocks, *flat, *after)


def home_kernel(capacity, units, groups, kinds, split, passed, scalars, x_ref, *refs):
    out_ref = refs[-1 - passed]
    offsets = layout(groups, capacity)
    for g in range(len(groups)):
        mine = refs[kinds * g:kinds * (g + 1)]
        multiply(x_ref, slice(offsets[g], offsets[g + 1]), mine, scalars[3] if split else None, units, out_ref)


def home_rows(scalars, groups, chosen, weights, split, passing, after, capacity, units):
    flat = [w for expert, _ in groups for w in weights[expert]]
    out = jax.ShapeDtypeStruct((chosen.shape[0], 2 * units), F32)
    args = (scalars, chosen, *flat, *after, *passing)
    result = pl.pallas_call(
        functools.partial(home_kernel, capacity, units, groups, len(weights[0]), split, len(passing)),
        grid=(1,),
        out_shape=(out, *[jax.ShapeDtypeStruct(p.shape, p.dtype) for p in passing]),
        in_specs=[SMEM, whole(chosen)] + [whole(w) for w in flat] + [ANY] * (len(after) + len(passing)),
        out_specs=(whole(out), *[ANY] * len(passing)),
        input_output_aliases={len(args) - len(passing) + i: 1 + i for i in range(len(passing))},
        compiler_params=params(),
        cost_estimate=cost(),
    )(*args)
    return result[0], result[1:]


def down_kernel(experts, capacity, groups, count, pieces, wide, passed, scalars, *refs):
    hiddens, refs = refs[:pieces], refs[pieces:]
    tail_refs, weights = refs[:count], refs[count:]
    scratch = refs[-2 * len(groups):]
    out_ref = refs[-2 * len(groups) - 1 - passed]
    rows = tail_refs[0].shape[0]
    units = hiddens[0].shape[1]
    offsets = layout(groups, capacity)
    starts = [scalars[4 + s] for s in range(pieces)]
    for g, (expert, members) in enumerate(groups):
        spread_ref, weight_ref = scratch[2 * g:2 * g + 2]
        tails = jnp.concatenate([tail_refs[m][...] for m in members], axis=0)
        slot, weight = slot_column(tails, scalars[expert], experts, rows, capacity)
        weight_ref[...] = weight
        place = lax.broadcasted_iota(jnp.int32, (len(members) * rows, offsets[g + 1] - offsets[g]), 1)
        spread = jnp.where(place == slot, 1.0, 0.0).astype(BF16)
        for s, ref in enumerate(hiddens):
            value = jnp.dot(spread, ref[offsets[g]:offsets[g + 1], :], preferred_element_type=F32).astype(BF16)
            if wide:
                spread_ref[:, pl.ds(pl.multiple_of(starts[s], LANES), units)] = value
            else:
                spread_ref[s] = value
    width = out_ref.shape[1]
    step = tile(width, (256,))

    @pl.loop(0, width // step)
    def _(i):
        span = pl.ds(pl.multiple_of(i * step, LANES), step)
        sums = [None] * count
        for g, (expert, members) in enumerate(groups):
            spread_ref, weight_ref = scratch[2 * g:2 * g + 2]
            w_ref = weights[g]
            if wide:
                result = jnp.dot(spread_ref[...], w_ref[:, span], preferred_element_type=F32)
            else:
                result = jnp.zeros((len(members) * rows, step), F32)
                for s in range(pieces):
                    w = w_ref[pl.ds(pl.multiple_of(starts[s], 16), units), span]
                    result = result + jnp.dot(spread_ref[s], w, preferred_element_type=F32)
            result = result * weight_ref[...]
            for k, m in enumerate(members):
                part = result[k * rows:(k + 1) * rows]
                sums[m] = part if sums[m] is None else sums[m] + part
        for m, value in enumerate(sums):
            out_ref[m * rows:(m + 1) * rows, span] = value.astype(BF16)


def down_rows(scalars, groups, hiddens, blocks, weights, passing, after, width, experts, capacity):
    rows, padded = blocks[0].shape
    units = hiddens[0].shape[1]
    pieces = len(hiddens)
    wide = units % LANES == 0
    tail = pl.BlockSpec((rows, padded - width), lambda i: (0, width // (padded - width)))
    scratch = []
    for _, members in groups:
        spread = (len(members) * rows, pieces * units) if wide else (pieces, len(members) * rows, units)
        scratch += [pltpu.VMEM(spread, BF16), pltpu.VMEM((len(members) * rows, 1), F32)]
    out = jax.ShapeDtypeStruct((len(blocks) * rows, width), BF16)
    args = (scalars, *hiddens, *blocks, *[weights[e] for e, _ in groups], *after, *passing)
    result = pl.pallas_call(
        functools.partial(down_kernel, experts, capacity, groups, len(blocks), pieces, wide, len(passing)),
        grid=(1,),
        out_shape=(out, *[jax.ShapeDtypeStruct(p.shape, p.dtype) for p in passing]),
        in_specs=[SMEM] + [whole(h) for h in hiddens] + [tail] * len(blocks)
        + [whole(weights[0])] * len(groups) + [ANY] * (len(after) + len(passing)),
        out_specs=(whole(out), *[ANY] * len(passing)),
        input_output_aliases={len(args) - len(passing) + i: 1 + i for i in range(len(passing))},
        scratch_shapes=scratch,
        compiler_params=params(),
        cost_estimate=cost(),
    )(*args)
    return result[0], result[1:]


def add_kernel(count, *refs):
    out_ref = refs[-1]
    total = refs[0][...].astype(F32)
    for ref in refs[1:count]:
        total = total + ref[...].astype(F32)
    out_ref[...] = total.astype(out_ref.dtype)


def added(terms, kind, after):
    out = jax.ShapeDtypeStruct(terms[0].shape, kind)
    return pl.pallas_call(
        functools.partial(add_kernel, len(terms)),
        grid=(1,),
        out_shape=out,
        in_specs=[whole(t) for t in terms] + [ANY] * len(after),
        out_specs=whole(out),
        compiler_params=params(),
        cost_estimate=cost(),
    )(*terms, *after)


def on_device(tokens, expert_ids, route_weights, w_gate, w_up, w_down):
    rows, width = tokens.shape
    top = expert_ids.shape[1]
    ring = lax.axis_size("expert")
    experts = ring * lax.axis_size("dp")
    capacity = min(rows, max(2, 3 * rows * top // (2 * experts)))
    parts = lax.axis_size("tensor")
    units = w_gate.shape[2] // parts
    core = lax.axis_index("dp")
    rank = lax.axis_index("tensor")
    hops = ring // 2

    def over_y(x):
        return lax.ppermute(x, "expert", [(i, i ^ 1) for i in range(ring)])

    def over_z(x):
        return lax.ppermute(x, "expert", [(i, (i + 2) % ring) for i in range(ring)])

    def over_core(x):
        return lax.ppermute(x, "dp", [(0, 1), (1, 0)])

    def over_x(x, step):
        return lax.ppermute(x, "tensor", [(i, (i + step) % parts) for i in range(parts)])

    first = lax.axis_index("expert") * 2
    scalars = [first + core, first + 1 - core, (rank + 1) % parts * units, rank * units]
    scalars += [(rank + parts - s) % parts * units for s in range(parts)]
    scalars = jnp.stack([jnp.asarray(s, jnp.int32) for s in scalars])
    gates = (w_gate[0], over_core(w_gate)[0])
    ups = (w_up[0], over_core(w_up)[0])
    split = parts == 2 and units % LANES == 0
    if split:
        away = home = tuple(zip(gates, ups))
    else:
        def unit_slice(w, offset):
            return lax.dynamic_slice_in_dim(w, (rank + offset) % parts * units, units, 1)

        away, home = [], []
        for gate, up in zip(gates, ups):
            pairs = [(unit_slice(gate, s), unit_slice(up, s)) for s in range(parts)]
            away.append((jnp.concatenate([w for pair in pairs[1:] for w in pair], axis=1),))
            home.append((jnp.concatenate(pairs[0], axis=1),))

    blocks, arrived = {(0, "s"): make_block(tokens, expert_ids, route_weights, experts)}, {}

    def send_on(hop):
        block = blocks[hop, "s"]
        if hop + 1 < hops:
            arrived[hop + 1] = over_z(block)
        blocks[hop, "b"] = over_y(block)

    both = ((0, (0, 1)), (1, (0, 1)))
    one = ((0, (0,)), (1, (0,)))
    plan = [([(0, "s")], ((0, (0,)),)), ([(0, "s"), (0, "b"), (1, "s")], ((1, (0, 1, 2)), (0, (1, 2))))]
    plan += [([(hop - 1, "b"), (hop, "s")], both) for hop in range(2, hops)]
    plan += [([(hops - 1, "b")], one)]
    count = len(plan)
    chosen, parts_in, totals, hidden, returned, carried, gathered = {}, {}, {}, {}, {}, {}, []
    downs = [w_down[0], over_core(w_down)[0]]
    order = [scalars]

    def passing(hop):
        return [arrived[hop]] if hop in arrived else []

    def take_on(hop, passed):
        if passed:
            blocks[hop, "s"] = passed[0]
            send_on(hop)

    def pick(i):
        keys, groups = plan[i]
        mine = [blocks[k] for k in keys]
        chosen[i], part = pick_rows(scalars, groups, mine, away, split, order, width, experts, capacity, units)
        parts_in[i] = [over_x(part[:, 2 * units * (s - 1):2 * units * s], s) for s in range(1, parts)]
        order[:] = [part]

    def home_product(i, hop=None):
        totals[i], passed = home_rows(
            scalars, plan[i][1], chosen[i], home, split, passing(hop), order, capacity, units
        )
        order[:] = [totals[i]]
        take_on(hop, passed)

    def activate(i):
        total = totals[i]
        for piece in parts_in[i]:
            total = total + piece.astype(F32)
        value = (jax.nn.silu(total[:, :units]) * total[:, units:]).astype(BF16)
        hidden[i] = [value] + [over_x(value, s) for s in range(1, parts)]
        order.append(value)

    def down_product(i, hop=None):
        keys, groups = plan[i]
        mine = [blocks[k] for k in keys]
        term, passed = down_rows(
            scalars, groups, hidden[i], mine, downs, passing(hop), order, width, experts, capacity
        )
        order[:] = [term]
        take_on(hop, passed)
        for k, (at, kind) in enumerate(keys):
            piece = term[k * rows:(k + 1) * rows]
            if kind == "b":
                returned[at, "b"] = over_y(piece)
            elif at == 0:
                gathered.append(piece)
            else:
                returned[at, "s"] = piece

    def add_hop(hop):
        if hop == 0:
            gathered[:] = [added(gathered + [returned[hop, "b"]], F32, order)]
            order[:] = [gathered[0]]
        else:
            terms = [returned[hop, "s"], returned[hop, "b"]] + ([carried[hop]] if hop in carried else [])
            total = added(terms, BF16, order)
            order[:] = [total]
            carried[hop + 1] = over_z(total)

    def await_beside(hop):
        if (hop, "b") in blocks:
            order.append(blocks[hop, "b"])

    send_on(0)
    if hops == 4:
        pick(0)
        order.extend([gates[1], ups[1]])
        home_product(0, 1)
        pick(1)
        activate(0)
        order.append(downs[1])
        home_product(1, 2)
        pick(2)
        activate(1)
        home_product(2, 3)
        order.append(blocks[2, "b"])
        down_product(0, None)
        activate(2)
        pick(3)
        home_product(3, None)
        down_product(1, None)
        down_product(2, None)
        pick(4)
        home_product(4, None)
        activate(3)
        down_product(3, None)
        add_hop(1)
        add_hop(0)
        activate(4)
        down_product(4, None)
        add_hop(2)
        add_hop(3)
    else:
        pick(0)
        home_product(0, 1)
        activate(0)
        for i in range(1, count):
            if i > 1:
                activate(i - 1)
            pick(i)
            home_product(i, i + 1)
            down_product(i - 1)
            if i >= 3:
                add_hop(i - 3)
        activate(count - 1)
        down_product(count - 1)
        for hop in range(count - 3, hops):
            add_hop(hop)
    return (gathered[0] + carried[hops].astype(F32)).astype(BF16)


def solution(mesh):
    placed = (
        P(("group", "expert", "dp"), "tensor"),
        P(("group", "expert", "dp"), None),
        P(("group", "expert", "dp"), None),
        P(("expert", "dp"), "tensor", None),
        P(("expert", "dp"), "tensor", None),
        P(("expert", "dp"), None, "tensor"),
    )
    return jax.shard_map(
        on_device,
        mesh=mesh,
        in_specs=placed,
        out_specs=P(("group", "expert", "dp"), "tensor"),
        check_vma=False,
    )
```

```python
import functools

import jax
import jax.numpy as jnp
from jax import lax
from jax.experimental import pallas as pl
from jax.experimental.pallas import tpu as pltpu
from jax.sharding import PartitionSpec as P

F32 = jnp.float32
BF16 = jnp.bfloat16
LANES = 128
VMEM = 10 * 1024 * 1024
ANY = pl.BlockSpec(memory_space=pl.ANY)
HBM = pl.BlockSpec(memory_space=pltpu.HBM)


def tile(extent, choices):
    for size in choices:
        if extent % size == 0:
            return size
    return extent


def whole(x):
    return pl.BlockSpec(x.shape, lambda i: (0,) * len(x.shape))


def params():
    return pltpu.CompilerParams(vmem_limit_bytes=VMEM)


def cost():
    return pl.CostEstimate(flops=1, bytes_accessed=1, transcendentals=0)


def block_kernel(experts, tokens_ref, ids_ref, route_ref, out_ref, ids_buffer, route_buffer, sems):
    rows, width = tokens_ref.shape
    copies = [
        pltpu.make_async_copy(ids_ref, ids_buffer, sems.at[0]),
        pltpu.make_async_copy(route_ref, route_buffer, sems.at[1]),
        pltpu.make_async_copy(tokens_ref, out_ref.at[:, :width], sems.at[2]),
    ]
    for copy in copies:
        copy.start()
    copies[0].wait()
    copies[1].wait()
    ids = ids_buffer[...].T
    route = route_buffer[...].T
    column = lax.broadcasted_iota(jnp.int32, (rows, out_ref.shape[1] - width), 1)
    expert = jnp.where(column < experts, column, column - experts)
    value = jnp.zeros(column.shape, F32)
    for k in range(ids.shape[1]):
        value = value + jnp.where(expert == ids[:, k:k + 1], route[:, k:k + 1], 0.0)
    high = value.astype(BF16).astype(F32)
    out_ref[:, width:] = jnp.where(column < experts, high, value - high).astype(BF16)
    copies[2].wait()


def make_block(tokens, expert_ids, route_weights, experts):
    rows, width = tokens.shape
    padded = width + 2 * experts + (-(2 * experts)) % LANES
    args = (tokens, expert_ids.T, route_weights.T)
    return pl.pallas_call(
        functools.partial(block_kernel, experts),
        grid=(1,),
        out_shape=jax.ShapeDtypeStruct((rows, padded), BF16),
        in_specs=[HBM] * 3,
        out_specs=pl.BlockSpec((rows, padded), lambda i: (0, 0)),
        scratch_shapes=[
            pltpu.VMEM(args[1].shape, jnp.int32),
            pltpu.VMEM(args[2].shape, F32),
            pltpu.SemaphoreType.DMA((3,)),
        ],
        compiler_params=params(),
        cost_estimate=cost(),
    )(*args)


def slot_row(tails, me, experts, rows, capacity):
    total = tails.shape[0]
    column = lax.broadcasted_iota(jnp.int32, (8, tails.shape[1]), 1)
    mark = jnp.where((column == me) | (column == experts + me), 1.0, 0.0).astype(BF16)
    weight = lax.dot_general(mark, tails, (((1,), (1,)), ((), ())), preferred_element_type=F32)
    live = weight > 0.0
    number = lax.broadcasted_iota(jnp.int32, (8, total), 1) // rows
    above = lax.broadcasted_iota(jnp.int32, (total, total), 0)
    own = lax.broadcasted_iota(jnp.int32, (total, total), 1)
    ahead = jnp.where((above < own) & (above >= (number * rows)[0:1]), 1.0, 0.0).astype(BF16)
    before = jnp.dot(jnp.where(live, 1.0, 0.0).astype(BF16), ahead, preferred_element_type=F32)
    return jnp.where(live, before.astype(jnp.int32) + number * capacity, -1)[0:1]


def slot_column(tails, me, experts, rows, capacity):
    total = tails.shape[0]
    column = lax.broadcasted_iota(jnp.int32, tails.shape, 1)
    mine = (column == me) | (column == experts + me)
    weight = jnp.sum(jnp.where(mine, tails.astype(F32), 0.0), axis=1, keepdims=True)
    live = weight > 0.0
    number = lax.broadcasted_iota(jnp.int32, (total, 1), 0) // rows
    own = lax.broadcasted_iota(jnp.int32, (total, total), 0)
    above = lax.broadcasted_iota(jnp.int32, (total, total), 1)
    ahead = jnp.where((above < own) & (above >= number * rows), 1.0, 0.0).astype(BF16)
    flags = jnp.broadcast_to(jnp.where(live, 1.0, 0.0), (total, LANES)).astype(BF16)
    before = jnp.dot(ahead, flags, preferred_element_type=F32)[:, 0:1]
    return jnp.where(live, before.astype(jnp.int32) + number * capacity, -1), weight


def layout(groups, capacity):
    offsets, total = [], 0
    for _, members in groups:
        offsets.append(total)
        total += -(-len(members) * capacity // 16) * 16
    return offsets + [total]


def multiply(x_ref, rows, weights, start, units, out_ref):
    def store(x, w, column, count):
        out_ref[rows, column:column + count] = jnp.dot(x, w, preferred_element_type=F32).astype(out_ref.dtype)

    x = x_ref[rows, :]
    if start is None:
        w_ref = weights[0]
        step = tile(w_ref.shape[1], (256, 384))
        for column in range(0, w_ref.shape[1], step):
            store(x, w_ref[:, column:column + step], column, step)
        return
    full = units // 256 * 256
    for i, ref in enumerate(weights):
        for column in range(0, full, 256):
            store(x, ref[:, pl.ds(pl.multiple_of(start + column, LANES), 256)], i * units + column, 256)
    if full < units:
        rest = pl.ds(pl.multiple_of(start + full, LANES), units - full)
        w = jnp.concatenate([ref[:, rest] for ref in weights], axis=1)
        y = jnp.dot(x, w, preferred_element_type=F32).astype(out_ref.dtype)
        out_ref[rows, full:units] = y[:, :units - full]
        out_ref[rows, units + full:] = y[:, units - full:]


def position(units):
    core, rank, parts = lax.axis_index("dp"), lax.axis_index("tensor"), lax.axis_size("tensor")
    first = lax.axis_index("expert") * 2
    places = [(rank + parts - s) % parts * units for s in range(parts)]
    return (first + core, first + 1 - core), (rank + 1) % parts * units, rank * units, places


def pick_kernel(width, experts, capacity, units, groups, count, kinds, split, *refs):
    blocks, weights = refs[:count], refs[count:]
    chosen_ref, part_ref = refs[-2:]
    rows = blocks[0].shape[0]
    mine_and_other, start, _, _ = position(units)
    offsets = layout(groups, capacity)
    step = tile(width, (512, 256))
    for g, (expert, members) in enumerate(groups):
        tails = jnp.concatenate([blocks[m][:, width:] for m in members], axis=0)
        slot = slot_row(tails, mine_and_other[expert], experts, rows, capacity)
        here = offsets[g + 1] - offsets[g]
        place = lax.broadcasted_iota(jnp.int32, (here, len(members) * rows), 0)
        pick = jnp.where(place == slot, 1.0, 0.0).astype(BF16)
        for column in range(0, width, step):
            x = jnp.concatenate([blocks[m][:, column:column + step] for m in members], axis=0)
            value = jnp.dot(pick, x, preferred_element_type=F32).astype(BF16)
            chosen_ref[offsets[g]:offsets[g + 1], column:column + step] = value
    for g in range(len(groups)):
        mine = weights[kinds * g:kinds * (g + 1)]
        multiply(chosen_ref, slice(offsets[g], offsets[g + 1]), mine, start if split else None, units, part_ref)


def pick_rows(groups, blocks, weights, split, after, width, experts, capacity, units):
    columns = 2 * units if split else weights[0][0].shape[1]
    taken = layout(groups, capacity)[-1]
    flat = [w for expert, _ in groups for w in weights[expert]]
    kernel = functools.partial(
        pick_kernel, width, experts, capacity, units, groups, len(blocks), len(weights[0]), split
    )
    out = (jax.ShapeDtypeStruct((taken, width), BF16), jax.ShapeDtypeStruct((taken, columns), BF16))
    return pl.pallas_call(
        kernel,
        grid=(1,),
        out_shape=out,
        in_specs=[whole(x) for x in (*blocks, *flat)] + [ANY] * len(after),
        out_specs=tuple(whole(o) for o in out),
        compiler_params=params(),
        cost_estimate=cost(),
    )(*blocks, *flat, *after)


def home_kernel(capacity, units, groups, kinds, split, passed, x_ref, *refs):
    _, _, start, _ = position(units)
    out_ref = refs[-1 - passed]
    offsets = layout(groups, capacity)
    for g in range(len(groups)):
        mine = refs[kinds * g:kinds * (g + 1)]
        multiply(x_ref, slice(offsets[g], offsets[g + 1]), mine, start if split else None, units, out_ref)


def home_rows(groups, chosen, weights, split, passing, after, capacity, units):
    flat = [w for expert, _ in groups for w in weights[expert]]
    out = jax.ShapeDtypeStruct((chosen.shape[0], 2 * units), F32)
    args = (chosen, *flat, *after, *passing)
    result = pl.pallas_call(
        functools.partial(home_kernel, capacity, units, groups, len(weights[0]), split, len(passing)),
        grid=(1,),
        out_shape=(out, *[jax.ShapeDtypeStruct(p.shape, p.dtype) for p in passing]),
        in_specs=[whole(chosen)] + [whole(w) for w in flat] + [ANY] * (len(after) + len(passing)),
        out_specs=(whole(out), *[ANY] * len(passing)),
        input_output_aliases={len(args) - len(passing) + i: 1 + i for i in range(len(passing))},
        compiler_params=params(),
        cost_estimate=cost(),
    )(*args)
    return result[0], result[1:]


def down_kernel(experts, capacity, groups, count, pieces, wide, passed, *refs):
    hiddens, refs = refs[:pieces], refs[pieces:]
    tail_refs, weights = refs[:count], refs[count:]
    scratch = refs[-len(groups):]
    out_ref = refs[-len(groups) - 1 - passed]
    rows = tail_refs[0].shape[0]
    units = hiddens[0].shape[1]
    mine_and_other, _, _, starts = position(units)
    offsets = layout(groups, capacity)
    width = out_ref.shape[1]
    step = tile(width, (256,))
    shares = []
    for g, (expert, members) in enumerate(groups):
        tails = jnp.concatenate([tail_refs[m][...] for m in members], axis=0)
        slot, weight = slot_column(tails, mine_and_other[expert], experts, rows, capacity)
        shares.append(jnp.broadcast_to(weight, (len(members) * rows, step)))
        place = lax.broadcasted_iota(jnp.int32, (len(members) * rows, offsets[g + 1] - offsets[g]), 1)
        spread = jnp.where(place == slot, 1.0, 0.0).astype(BF16)
        for s, ref in enumerate(hiddens):
            value = jnp.dot(spread, ref[offsets[g]:offsets[g + 1], :], preferred_element_type=F32).astype(BF16)
            if wide:
                scratch[g][:, pl.ds(pl.multiple_of(starts[s], LANES), units)] = value
            else:
                scratch[g][s] = value
    for column in range(0, width, step):
        sums = [None] * count
        for g, (expert, members) in enumerate(groups):
            w_ref = weights[g]
            if wide:
                result = jnp.dot(scratch[g][...], w_ref[:, column:column + step], preferred_element_type=F32)
            else:
                result = jnp.zeros((len(members) * rows, step), F32)
                for s in range(pieces):
                    w = w_ref[pl.ds(pl.multiple_of(starts[s], 16), units), column:column + step]
                    result = result + jnp.dot(scratch[g][s], w, preferred_element_type=F32)
            result = result * shares[g]
            for k, m in enumerate(members):
                part = result[k * rows:(k + 1) * rows]
                sums[m] = part if sums[m] is None else sums[m] + part
        for m, value in enumerate(sums):
            out_ref[m * rows:(m + 1) * rows, column:column + step] = value.astype(BF16)


def down_rows(groups, hiddens, blocks, weights, passing, after, width, experts, capacity):
    rows, padded = blocks[0].shape
    units = hiddens[0].shape[1]
    pieces = len(hiddens)
    wide = units % LANES == 0
    tail = pl.BlockSpec((rows, padded - width), lambda i: (0, width // (padded - width)))
    scratch = []
    for _, members in groups:
        spread = (len(members) * rows, pieces * units) if wide else (pieces, len(members) * rows, units)
        scratch.append(pltpu.VMEM(spread, BF16))
    out = jax.ShapeDtypeStruct((len(blocks) * rows, width), BF16)
    args = (*hiddens, *blocks, *[weights[e] for e, _ in groups], *after, *passing)
    result = pl.pallas_call(
        functools.partial(down_kernel, experts, capacity, groups, len(blocks), pieces, wide, len(passing)),
        grid=(1,),
        out_shape=(out, *[jax.ShapeDtypeStruct(p.shape, p.dtype) for p in passing]),
        in_specs=[whole(h) for h in hiddens] + [tail] * len(blocks)
        + [whole(weights[0])] * len(groups) + [ANY] * (len(after) + len(passing)),
        out_specs=(whole(out), *[ANY] * len(passing)),
        input_output_aliases={len(args) - len(passing) + i: 1 + i for i in range(len(passing))},
        scratch_shapes=scratch,
        compiler_params=params(),
        cost_estimate=cost(),
    )(*args)
    return result[0], result[1:]


def add_kernel(count, *refs):
    out_ref = refs[-1]
    total = refs[0][...].astype(F32)
    for ref in refs[1:count]:
        total = total + ref[...].astype(F32)
    out_ref[...] = total.astype(out_ref.dtype)


def added(terms, kind, after):
    out = jax.ShapeDtypeStruct(terms[0].shape, kind)
    return pl.pallas_call(
        functools.partial(add_kernel, len(terms)),
        grid=(1,),
        out_shape=out,
        in_specs=[whole(t) for t in terms] + [ANY] * len(after),
        out_specs=whole(out),
        compiler_params=params(),
        cost_estimate=cost(),
    )(*terms, *after)


def on_device(tokens, expert_ids, route_weights, w_gate, w_up, w_down):
    rows, width = tokens.shape
    top = expert_ids.shape[1]
    ring = lax.axis_size("expert")
    experts = ring * lax.axis_size("dp")
    capacity = min(rows, max(2, 3 * rows * top // (2 * experts)))
    parts = lax.axis_size("tensor")
    units = w_gate.shape[2] // parts
    rank = lax.axis_index("tensor")
    hops = ring // 2

    def over_y(x):
        return lax.ppermute(x, "expert", [(i, i ^ 1) for i in range(ring)])

    def over_z(x):
        return lax.ppermute(x, "expert", [(i, (i + 2) % ring) for i in range(ring)])

    def over_core(x):
        return lax.ppermute(x, "dp", [(0, 1), (1, 0)])

    def over_x(x, step):
        return lax.ppermute(x, "tensor", [(i, (i + step) % parts) for i in range(parts)])

    gates = (w_gate[0], over_core(w_gate)[0])
    ups = (w_up[0], over_core(w_up)[0])
    split = parts == 2 and units % LANES == 0
    if split:
        away = home = tuple(zip(gates, ups))
    else:
        def unit_slice(w, offset):
            return lax.dynamic_slice_in_dim(w, (rank + offset) % parts * units, units, 1)

        away, home = [], []
        for gate, up in zip(gates, ups):
            pairs = [(unit_slice(gate, s), unit_slice(up, s)) for s in range(parts)]
            away.append((jnp.concatenate([w for pair in pairs[1:] for w in pair], axis=1),))
            home.append((jnp.concatenate(pairs[0], axis=1),))

    blocks, arrived = {(0, "s"): make_block(tokens, expert_ids, route_weights, experts)}, {}

    def send_on(hop):
        block = blocks[hop, "s"]
        if hop + 1 < hops:
            arrived[hop + 1] = over_z(block)
        blocks[hop, "b"] = over_y(block)

    both = ((0, (0, 1)), (1, (0, 1)))
    one = ((0, (0,)), (1, (0,)))
    plan = [([(0, "s")], ((0, (0,)),)), ([(0, "s"), (0, "b"), (1, "s")], ((1, (0, 1, 2)), (0, (1, 2))))]
    plan += [([(hop - 1, "b"), (hop, "s")], both) for hop in range(2, hops)]
    plan += [([(hops - 1, "b")], one)]
    count = len(plan)
    chosen, parts_in, totals, hidden, returned, carried, gathered = {}, {}, {}, {}, {}, {}, []
    downs = [w_down[0], over_core(w_down)[0]]
    order = []

    def passing(hop):
        return [arrived[hop]] if hop in arrived else []

    def take_on(hop, passed):
        if passed:
            blocks[hop, "s"] = passed[0]
            send_on(hop)

    def pick(i):
        keys, groups = plan[i]
        mine = [blocks[k] for k in keys]
        chosen[i], part = pick_rows(groups, mine, away, split, order, width, experts, capacity, units)
        parts_in[i] = [over_x(part[:, 2 * units * (s - 1):2 * units * s], s) for s in range(1, parts)]
        order[:] = [part]

    def home_product(i, hop=None):
        totals[i], passed = home_rows(
            plan[i][1], chosen[i], home, split, passing(hop), order, capacity, units
        )
        order[:] = [totals[i]]
        take_on(hop, passed)

    def activate(i):
        total = totals[i]
        for piece in parts_in[i]:
            total = total + piece.astype(F32)
        value = (jax.nn.silu(total[:, :units]) * total[:, units:]).astype(BF16)
        hidden[i] = [value] + [over_x(value, s) for s in range(1, parts)]
        order.append(value)

    def down_product(i, hop=None):
        keys, groups = plan[i]
        mine = [blocks[k] for k in keys]
        term, passed = down_rows(
            groups, hidden[i], mine, downs, passing(hop), order, width, experts, capacity
        )
        order[:] = [term]
        take_on(hop, passed)
        for k, (at, kind) in enumerate(keys):
            piece = term[k * rows:(k + 1) * rows]
            if kind == "b":
                returned[at, "b"] = over_y(piece)
            elif at == 0:
                gathered.append(piece)
            else:
                returned[at, "s"] = piece

    def add_hop(hop):
        if hop == 0:
            gathered[:] = [added(gathered + [returned[hop, "b"]], F32, order)]
            order[:] = [gathered[0]]
        else:
            terms = [returned[hop, "s"], returned[hop, "b"]] + ([carried[hop]] if hop in carried else [])
            total = added(terms, BF16, order)
            order[:] = [total]
            carried[hop + 1] = over_z(total)

    def await_beside(hop):
        if (hop, "b") in blocks:
            order.append(blocks[hop, "b"])

    send_on(0)
    if hops == 4:
        pick(0)
        order.extend([gates[1], ups[1]])
        home_product(0, 1)
        pick(1)
        activate(0)
        order.append(downs[1])
        home_product(1, 2)
        pick(2)
        activate(1)
        home_product(2, 3)
        order.append(blocks[2, "b"])
        down_product(0, None)
        activate(2)
        pick(3)
        home_product(3, None)
        down_product(1, None)
        down_product(2, None)
        pick(4)
        home_product(4, None)
        activate(3)
        down_product(3, None)
        add_hop(1)
        add_hop(0)
        activate(4)
        down_product(4, None)
        add_hop(2)
        add_hop(3)
    else:
        pick(0)
        home_product(0, 1)
        activate(0)
        for i in range(1, count):
            if i > 1:
                activate(i - 1)
            pick(i)
            home_product(i, i + 1)
            down_product(i - 1)
            if i >= 3:
                add_hop(i - 3)
        activate(count - 1)
        down_product(count - 1)
        for hop in range(count - 3, hops):
            add_hop(hop)
    return (gathered[0] + carried[hops].astype(F32)).astype(BF16)


def solution(mesh):
    placed = (
        P(("group", "expert", "dp"), "tensor"),
        P(("group", "expert", "dp"), None),
        P(("group", "expert", "dp"), None),
        P(("expert", "dp"), "tensor", None),
        P(("expert", "dp"), "tensor", None),
        P(("expert", "dp"), None, "tensor"),
    )
    return jax.shard_map(
        on_device,
        mesh=mesh,
        in_specs=placed,
        out_specs=P(("group", "expert", "dp"), "tensor"),
        check_vma=False,
    )
```

```python
import functools

import jax
import jax.numpy as jnp
from jax import lax
from jax.experimental import pallas as pl
from jax.experimental.pallas import tpu as pltpu
from jax.sharding import PartitionSpec as P

F32 = jnp.float32
BF16 = jnp.bfloat16
LANES = 128
VMEM = 10 * 1024 * 1024
ANY = pl.BlockSpec(memory_space=pl.ANY)
HBM = pl.BlockSpec(memory_space=pltpu.HBM)


def tile(extent, choices):
    for size in choices:
        if extent % size == 0:
            return size
    return extent


def whole(x):
    return pl.BlockSpec(x.shape, lambda i: (0,) * len(x.shape))


def params():
    return pltpu.CompilerParams(vmem_limit_bytes=VMEM)


def cost():
    return pl.CostEstimate(flops=1, bytes_accessed=1, transcendentals=0)


def block_kernel(experts, tokens_ref, ids_ref, route_ref, out_ref, ids_buffer, route_buffer, sems):
    rows, width = tokens_ref.shape
    copies = [
        pltpu.make_async_copy(ids_ref, ids_buffer, sems.at[0]),
        pltpu.make_async_copy(route_ref, route_buffer, sems.at[1]),
        pltpu.make_async_copy(tokens_ref, out_ref.at[:, :width], sems.at[2]),
    ]
    for copy in copies:
        copy.start()
    copies[0].wait()
    copies[1].wait()
    ids = ids_buffer[...].T
    route = route_buffer[...].T
    column = lax.broadcasted_iota(jnp.int32, (rows, out_ref.shape[1] - width), 1)
    expert = jnp.where(column < experts, column, column - experts)
    value = jnp.zeros(column.shape, F32)
    for k in range(ids.shape[1]):
        value = value + jnp.where(expert == ids[:, k:k + 1], route[:, k:k + 1], 0.0)
    high = value.astype(BF16).astype(F32)
    out_ref[:, width:] = jnp.where(column < experts, high, value - high).astype(BF16)
    copies[2].wait()


def make_block(tokens, expert_ids, route_weights, experts):
    rows, width = tokens.shape
    padded = width + 2 * experts + (-(2 * experts)) % LANES
    args = (tokens, expert_ids.T, route_weights.T)
    return pl.pallas_call(
        functools.partial(block_kernel, experts),
        grid=(1,),
        out_shape=jax.ShapeDtypeStruct((rows, padded), BF16),
        in_specs=[HBM] * 3,
        out_specs=pl.BlockSpec((rows, padded), lambda i: (0, 0)),
        scratch_shapes=[
            pltpu.VMEM(args[1].shape, jnp.int32),
            pltpu.VMEM(args[2].shape, F32),
            pltpu.SemaphoreType.DMA((3,)),
        ],
        compiler_params=params(),
        cost_estimate=cost(),
    )(*args)


def slot_row(tails, me, experts, rows, capacity):
    total = tails.shape[0]
    column = lax.broadcasted_iota(jnp.int32, (8, tails.shape[1]), 1)
    mark = jnp.where((column == me) | (column == experts + me), 1.0, 0.0).astype(BF16)
    weight = lax.dot_general(mark, tails, (((1,), (1,)), ((), ())), preferred_element_type=F32)
    live = weight > 0.0
    number = lax.broadcasted_iota(jnp.int32, (8, total), 1) // rows
    above = lax.broadcasted_iota(jnp.int32, (total, total), 0)
    own = lax.broadcasted_iota(jnp.int32, (total, total), 1)
    ahead = jnp.where((above < own) & (above >= (number * rows)[0:1]), 1.0, 0.0).astype(BF16)
    before = jnp.dot(jnp.where(live, 1.0, 0.0).astype(BF16), ahead, preferred_element_type=F32)
    return jnp.where(live, before.astype(jnp.int32) + number * capacity, -1)[0:1]


def slot_column(tails, me, experts, rows, capacity):
    total = tails.shape[0]
    column = lax.broadcasted_iota(jnp.int32, tails.shape, 1)
    mine = (column == me) | (column == experts + me)
    weight = jnp.sum(jnp.where(mine, tails.astype(F32), 0.0), axis=1, keepdims=True)
    live = weight > 0.0
    number = lax.broadcasted_iota(jnp.int32, (total, 1), 0) // rows
    own = lax.broadcasted_iota(jnp.int32, (total, total), 0)
    above = lax.broadcasted_iota(jnp.int32, (total, total), 1)
    ahead = jnp.where((above < own) & (above >= number * rows), 1.0, 0.0).astype(BF16)
    flags = jnp.broadcast_to(jnp.where(live, 1.0, 0.0), (total, LANES)).astype(BF16)
    before = jnp.dot(ahead, flags, preferred_element_type=F32)[:, 0:1]
    return jnp.where(live, before.astype(jnp.int32) + number * capacity, -1), weight


def layout(groups, capacity):
    offsets, total = [], 0
    for _, members in groups:
        offsets.append(total)
        total += -(-len(members) * capacity // 16) * 16
    return offsets + [total]


def multiply(x_ref, rows, weights, start, units, out_ref):
    def store(x, w, column, count):
        out_ref[rows, column:column + count] = jnp.dot(x, w, preferred_element_type=F32).astype(out_ref.dtype)

    x = x_ref[rows, :]
    if start is None:
        w_ref = weights[0]
        step = tile(w_ref.shape[1], (256, 384))
        for column in range(0, w_ref.shape[1], step):
            store(x, w_ref[:, column:column + step], column, step)
        return
    full = units // 256 * 256
    for i, ref in enumerate(weights):
        for column in range(0, full, 256):
            store(x, ref[:, pl.ds(pl.multiple_of(start + column, LANES), 256)], i * units + column, 256)
    if full < units:
        rest = pl.ds(pl.multiple_of(start + full, LANES), units - full)
        w = jnp.concatenate([ref[:, rest] for ref in weights], axis=1)
        y = jnp.dot(x, w, preferred_element_type=F32).astype(out_ref.dtype)
        out_ref[rows, full:units] = y[:, :units - full]
        out_ref[rows, units + full:] = y[:, units - full:]


def position(units):
    core, rank, parts = lax.axis_index("dp"), lax.axis_index("tensor"), lax.axis_size("tensor")
    first = lax.axis_index("expert") * 2
    places = [(rank + parts - s) % parts * units for s in range(parts)]
    return (first + core, first + 1 - core), (rank + 1) % parts * units, rank * units, places


def pick_kernel(width, experts, capacity, units, groups, count, kinds, split, copied, *refs):
    blocks, weights = refs[:count], refs[count:]
    if copied:
        *_, source_ref, chosen_ref, part_ref, target_ref, sem = refs
        copy = pltpu.make_async_copy(source_ref, target_ref, sem)
        copy.start()
    else:
        chosen_ref, part_ref = refs[-2:]
    rows = blocks[0].shape[0]
    mine_and_other, start, _, _ = position(units)
    offsets = layout(groups, capacity)
    step = tile(width, (512, 256))
    for g, (expert, members) in enumerate(groups):
        tails = jnp.concatenate([blocks[m][:, width:] for m in members], axis=0)
        slot = slot_row(tails, mine_and_other[expert], experts, rows, capacity)
        here = offsets[g + 1] - offsets[g]
        place = lax.broadcasted_iota(jnp.int32, (here, len(members) * rows), 0)
        pick = jnp.where(place == slot, 1.0, 0.0).astype(BF16)
        for column in range(0, width, step):
            x = jnp.concatenate([blocks[m][:, column:column + step] for m in members], axis=0)
            value = jnp.dot(pick, x, preferred_element_type=F32).astype(BF16)
            chosen_ref[offsets[g]:offsets[g + 1], column:column + step] = value
    for g in range(len(groups)):
        mine = weights[kinds * g:kinds * (g + 1)]
        multiply(chosen_ref, slice(offsets[g], offsets[g + 1]), mine, start if split else None, units, part_ref)
    if copied:
        copy.wait()


def pick_rows(groups, blocks, weights, split, copying, after, width, experts, capacity, units):
    columns = 2 * units if split else weights[0][0].shape[1]
    taken = layout(groups, capacity)[-1]
    flat = [w for expert, _ in groups for w in weights[expert]]
    copied = len(copying)
    kernel = functools.partial(
        pick_kernel, width, experts, capacity, units, groups, len(blocks), len(weights[0]), split, copied
    )
    out = (jax.ShapeDtypeStruct((taken, width), BF16), jax.ShapeDtypeStruct((taken, columns), BF16))
    return pl.pallas_call(
        kernel,
        grid=(1,),
        out_shape=(*out, *[jax.ShapeDtypeStruct(a.shape, a.dtype) for a in copying]),
        in_specs=[whole(x) for x in (*blocks, *flat)] + [ANY] * (len(after) + copied),
        out_specs=(*[whole(o) for o in out], *[ANY] * copied),
        scratch_shapes=[pltpu.SemaphoreType.DMA] * copied,
        compiler_params=params(),
        cost_estimate=cost(),
    )(*blocks, *flat, *after, *copying)


def home_kernel(capacity, units, groups, kinds, split, passed, x_ref, *refs):
    _, _, start, _ = position(units)
    out_ref = refs[-1 - passed]
    offsets = layout(groups, capacity)
    for g in range(len(groups)):
        mine = refs[kinds * g:kinds * (g + 1)]
        multiply(x_ref, slice(offsets[g], offsets[g + 1]), mine, start if split else None, units, out_ref)


def home_rows(groups, chosen, weights, split, passing, after, capacity, units):
    flat = [w for expert, _ in groups for w in weights[expert]]
    out = jax.ShapeDtypeStruct((chosen.shape[0], 2 * units), F32)
    args = (chosen, *flat, *after, *passing)
    result = pl.pallas_call(
        functools.partial(home_kernel, capacity, units, groups, len(weights[0]), split, len(passing)),
        grid=(1,),
        out_shape=(out, *[jax.ShapeDtypeStruct(p.shape, p.dtype) for p in passing]),
        in_specs=[whole(chosen)] + [whole(w) for w in flat] + [ANY] * (len(after) + len(passing)),
        out_specs=(whole(out), *[ANY] * len(passing)),
        input_output_aliases={len(args) - len(passing) + i: 1 + i for i in range(len(passing))},
        compiler_params=params(),
        cost_estimate=cost(),
    )(*args)
    return result[0], result[1:]


def down_kernel(experts, capacity, groups, count, pieces, wide, passed, *refs):
    hiddens, refs = refs[:pieces], refs[pieces:]
    tail_refs, weights = refs[:count], refs[count:]
    scratch = refs[-len(groups):]
    out_ref = refs[-len(groups) - 1 - passed]
    rows = tail_refs[0].shape[0]
    units = hiddens[0].shape[1]
    mine_and_other, _, _, starts = position(units)
    offsets = layout(groups, capacity)
    width = out_ref.shape[1]
    step = tile(width, (256,))
    shares = []
    for g, (expert, members) in enumerate(groups):
        tails = jnp.concatenate([tail_refs[m][...] for m in members], axis=0)
        slot, weight = slot_column(tails, mine_and_other[expert], experts, rows, capacity)
        shares.append(jnp.broadcast_to(weight, (len(members) * rows, step)))
        place = lax.broadcasted_iota(jnp.int32, (len(members) * rows, offsets[g + 1] - offsets[g]), 1)
        spread = jnp.where(place == slot, 1.0, 0.0).astype(BF16)
        for s, ref in enumerate(hiddens):
            value = jnp.dot(spread, ref[offsets[g]:offsets[g + 1], :], preferred_element_type=F32).astype(BF16)
            if wide:
                scratch[g][:, pl.ds(pl.multiple_of(starts[s], LANES), units)] = value
            else:
                scratch[g][s] = value
    for column in range(0, width, step):
        sums = [None] * count
        for g, (expert, members) in enumerate(groups):
            w_ref = weights[g]
            if wide:
                result = jnp.dot(scratch[g][...], w_ref[:, column:column + step], preferred_element_type=F32)
            else:
                result = jnp.zeros((len(members) * rows, step), F32)
                for s in range(pieces):
                    w = w_ref[pl.ds(pl.multiple_of(starts[s], 16), units), column:column + step]
                    result = result + jnp.dot(scratch[g][s], w, preferred_element_type=F32)
            result = result * shares[g]
            for k, m in enumerate(members):
                part = result[k * rows:(k + 1) * rows]
                sums[m] = part if sums[m] is None else sums[m] + part
        for m, value in enumerate(sums):
            out_ref[m * rows:(m + 1) * rows, column:column + step] = value.astype(BF16)


def down_rows(groups, hiddens, blocks, weights, passing, after, width, experts, capacity):
    rows, padded = blocks[0].shape
    units = hiddens[0].shape[1]
    pieces = len(hiddens)
    wide = units % LANES == 0
    tail = pl.BlockSpec((rows, padded - width), lambda i: (0, width // (padded - width)))
    scratch = []
    for _, members in groups:
        spread = (len(members) * rows, pieces * units) if wide else (pieces, len(members) * rows, units)
        scratch.append(pltpu.VMEM(spread, BF16))
    out = jax.ShapeDtypeStruct((len(blocks) * rows, width), BF16)
    args = (*hiddens, *blocks, *[weights[e] for e, _ in groups], *after, *passing)
    result = pl.pallas_call(
        functools.partial(down_kernel, experts, capacity, groups, len(blocks), pieces, wide, len(passing)),
        grid=(1,),
        out_shape=(out, *[jax.ShapeDtypeStruct(p.shape, p.dtype) for p in passing]),
        in_specs=[whole(h) for h in hiddens] + [tail] * len(blocks)
        + [whole(weights[0])] * len(groups) + [ANY] * (len(after) + len(passing)),
        out_specs=(whole(out), *[ANY] * len(passing)),
        input_output_aliases={len(args) - len(passing) + i: 1 + i for i in range(len(passing))},
        scratch_shapes=scratch,
        compiler_params=params(),
        cost_estimate=cost(),
    )(*args)
    return result[0], result[1:]


def add_kernel(count, *refs):
    out_ref = refs[-1]
    total = refs[0][...].astype(F32)
    for ref in refs[1:count]:
        total = total + ref[...].astype(F32)
    out_ref[...] = total.astype(out_ref.dtype)


def added(terms, kind, after):
    out = jax.ShapeDtypeStruct(terms[0].shape, kind)
    return pl.pallas_call(
        functools.partial(add_kernel, len(terms)),
        grid=(1,),
        out_shape=out,
        in_specs=[whole(t) for t in terms] + [ANY] * len(after),
        out_specs=whole(out),
        compiler_params=params(),
        cost_estimate=cost(),
    )(*terms, *after)


def on_device(tokens, expert_ids, route_weights, w_gate, w_up, w_down):
    rows, width = tokens.shape
    top = expert_ids.shape[1]
    ring = lax.axis_size("expert")
    experts = ring * lax.axis_size("dp")
    capacity = min(rows, max(2, 3 * rows * top // (2 * experts)))
    parts = lax.axis_size("tensor")
    units = w_gate.shape[2] // parts
    rank = lax.axis_index("tensor")
    hops = ring // 2

    def over_y(x):
        return lax.ppermute(x, "expert", [(i, i ^ 1) for i in range(ring)])

    def over_z(x):
        return lax.ppermute(x, "expert", [(i, (i + 2) % ring) for i in range(ring)])

    def home_over_both(x, hop):
        return lax.ppermute(x, "expert", [(i, ((i - 2 * hop) % ring) ^ 1) for i in range(ring)])

    def over_core(x):
        return lax.ppermute(x, "dp", [(0, 1), (1, 0)])

    def over_x(x, step):
        return lax.ppermute(x, "tensor", [(i, (i + step) % parts) for i in range(parts)])

    gates = (w_gate[0], over_core(w_gate)[0])
    ups = (w_up[0], over_core(w_up)[0])
    split = parts == 2 and units % LANES == 0
    if split:
        away = home = tuple(zip(gates, ups))
    else:
        def unit_slice(w, offset):
            return lax.dynamic_slice_in_dim(w, (rank + offset) % parts * units, units, 1)

        away, home = [], []
        for gate, up in zip(gates, ups):
            pairs = [(unit_slice(gate, s), unit_slice(up, s)) for s in range(parts)]
            away.append((jnp.concatenate([w for pair in pairs[1:] for w in pair], axis=1),))
            home.append((jnp.concatenate(pairs[0], axis=1),))

    blocks, arrived = {(0, "s"): make_block(tokens, expert_ids, route_weights, experts)}, {}
    blocks[0, "c"] = over_core(blocks[0, "s"])

    def send_on(hop):
        block = blocks[hop, "s"]
        if hop + 1 < hops:
            arrived[hop + 1] = over_z(block)
        blocks[hop, "b"] = over_y(block)

    both = ((0, (0, 1)), (1, (0, 1)))
    one = ((0, (0,)), (1, (0,)))
    plan = [([(0, "s")], ((0, (0,)),)), ([(0, "s"), (0, "b"), (1, "s")], ((1, (0, 1, 2)), (0, (1, 2))))]
    plan += [([(1, "b")], one)] + [([(hop, "b"), (hop, "s")], both) for hop in range(2, hops - 1)]
    plan += [([(hops - 1, "b")], one), ([(hops - 1, "s")], one)]
    count = len(plan)
    straight = ()
    chosen, parts_in, totals, hidden, returned, carried, gathered = {}, {}, {}, {}, {}, {}, []
    downs = [w_down[0]]
    order = []

    def passing(hop):
        return [arrived[hop]] if hop in arrived else []

    def take_on(hop, passed):
        if passed:
            blocks[hop, "s"] = passed[0]
            send_on(hop)

    def pick(i):
        keys, groups = plan[i]
        mine = [blocks[k] for k in keys]
        copying = [w_down] if i == 1 else []
        chosen[i], part, *copies = pick_rows(
            groups, mine, away, split, copying, order, width, experts, capacity, units
        )
        downs.extend(over_core(c)[0] for c in copies)
        parts_in[i] = [over_x(part[:, 2 * units * (s - 1):2 * units * s], s) for s in range(1, parts)]
        order[:] = [part]

    def home_product(i, hop=None):
        totals[i], passed = home_rows(
            plan[i][1], chosen[i], home, split, passing(hop), order, capacity, units
        )
        order[:] = [totals[i]]
        take_on(hop, passed)

    def activate(i):
        total = totals[i]
        for piece in parts_in[i]:
            total = total + piece.astype(F32)
        value = (jax.nn.silu(total[:, :units]) * total[:, units:]).astype(BF16)
        hidden[i] = [value] + [over_x(value, s) for s in range(1, parts)]
        order.append(value)

    def down_product(i, hop=None):
        keys, groups = plan[i]
        mine = [blocks[k] for k in keys]
        term, passed = down_rows(
            groups, hidden[i], mine, downs, passing(hop), order, width, experts, capacity
        )
        order[:] = [term]
        take_on(hop, passed)
        for k, (at, kind) in enumerate(keys):
            piece = term[k * rows:(k + 1) * rows]
            if kind == "b" and at in straight:
                gathered.append(home_over_both(piece, at))
            elif kind == "b":
                returned[at, "b"] = over_y(piece)
            elif kind == "c":
                gathered.append(over_core(piece))
            elif at == 0:
                gathered.append(piece)
            else:
                returned[at, "s"] = piece

    def add_hop(hop):
        if hop == 0:
            gathered[:] = [added(gathered + [returned[hop, "b"]], F32, order)]
            order[:] = [gathered[0]]
        else:
            terms = [returned[hop, "s"]] + ([returned[hop, "b"]] if hop not in straight else [])
            terms += [carried[hop]] if hop in carried else []
            total = added(terms, BF16, order)
            order[:] = [total]
            carried[hop + 1] = over_z(total)

    def await_beside(hop):
        if (hop, "b") in blocks:
            order.append(blocks[hop, "b"])

    send_on(0)
    if hops == 4:
        pick(0)
        order.append(blocks[0, "b"])
        home_product(0, 1)
        activate(0)
        pick(1)
        order.extend(downs[1:])
        home_product(1, 2)
        pick(2)
        home_product(2, 3)
        down_product(0)
        activate(2)
        pick(3)
        activate(1)
        down_product(1)
        down_product(2)
        pick(4)
        home_product(3)
        home_product(4)
        activate(3)
        pick(5)
        home_product(5)
        order.append(blocks[2, "b"])
        add_hop(0)
        down_product(3)
        add_hop(1)
        order.append(blocks[2, "b"])
        activate(4)
        down_product(4)
        activate(5)
        add_hop(2)
        down_product(5)
        add_hop(3)
    else:
        for i in range(count):
            pick(i)
            home_product(i, i + 1)
            if i > 0:
                activate(i - 1)
                down_product(i - 1)
        activate(count - 1)
        down_product(count - 1)
        for hop in range(hops):
            add_hop(hop)
    return sum(x.astype(F32) for x in gathered + [carried[hops]]).astype(BF16)


def solution(mesh):
    placed = (
        P(("group", "expert", "dp"), "tensor"),
        P(("group", "expert", "dp"), None),
        P(("group", "expert", "dp"), None),
        P(("expert", "dp"), "tensor", None),
        P(("expert", "dp"), "tensor", None),
        P(("expert", "dp"), None, "tensor"),
    )
    return jax.shard_map(
        on_device,
        mesh=mesh,
        in_specs=placed,
        out_specs=P(("group", "expert", "dp"), "tensor"),
        check_vma=False,
    )
```

```python
import functools

import jax
import jax.numpy as jnp
from jax import lax
from jax.experimental import pallas as pl
from jax.experimental.pallas import tpu as pltpu
from jax.sharding import PartitionSpec as P

F32 = jnp.float32
BF16 = jnp.bfloat16
LANES = 128
VMEM = 10 * 1024 * 1024
ANY = pl.BlockSpec(memory_space=pl.ANY)
HBM = pl.BlockSpec(memory_space=pltpu.HBM)


def tile(extent, choices):
    for size in choices:
        if extent % size == 0:
            return size
    return extent


def whole(x):
    return pl.BlockSpec(x.shape, lambda i: (0,) * len(x.shape))


def params():
    return pltpu.CompilerParams(vmem_limit_bytes=VMEM)


def cost():
    return pl.CostEstimate(flops=1, bytes_accessed=1, transcendentals=0)


def block_kernel(experts, tokens_ref, ids_ref, route_ref, out_ref, ids_buffer, route_buffer, sems):
    rows, width = tokens_ref.shape
    copies = [
        pltpu.make_async_copy(ids_ref, ids_buffer, sems.at[0]),
        pltpu.make_async_copy(route_ref, route_buffer, sems.at[1]),
        pltpu.make_async_copy(tokens_ref, out_ref.at[:, :width], sems.at[2]),
    ]
    for copy in copies:
        copy.start()
    copies[0].wait()
    copies[1].wait()
    ids = ids_buffer[...].T
    route = route_buffer[...].T
    column = lax.broadcasted_iota(jnp.int32, (rows, out_ref.shape[1] - width), 1)
    expert = jnp.where(column < experts, column, column - experts)
    value = jnp.zeros(column.shape, F32)
    for k in range(ids.shape[1]):
        value = value + jnp.where(expert == ids[:, k:k + 1], route[:, k:k + 1], 0.0)
    high = value.astype(BF16).astype(F32)
    out_ref[:, width:] = jnp.where(column < experts, high, value - high).astype(BF16)
    copies[2].wait()


def make_block(tokens, expert_ids, route_weights, experts):
    rows, width = tokens.shape
    padded = width + 2 * experts + (-(2 * experts)) % LANES
    args = (tokens, expert_ids.T, route_weights.T)
    return pl.pallas_call(
        functools.partial(block_kernel, experts),
        grid=(1,),
        out_shape=jax.ShapeDtypeStruct((rows, padded), BF16),
        in_specs=[HBM] * 3,
        out_specs=pl.BlockSpec((rows, padded), lambda i: (0, 0)),
        scratch_shapes=[
            pltpu.VMEM(args[1].shape, jnp.int32),
            pltpu.VMEM(args[2].shape, F32),
            pltpu.SemaphoreType.DMA((3,)),
        ],
        compiler_params=params(),
        cost_estimate=cost(),
    )(*args)


def slot_row(tails, me, experts, rows, capacity):
    total = tails.shape[0]
    column = lax.broadcasted_iota(jnp.int32, (8, tails.shape[1]), 1)
    mark = jnp.where((column == me) | (column == experts + me), 1.0, 0.0).astype(BF16)
    weight = lax.dot_general(mark, tails, (((1,), (1,)), ((), ())), preferred_element_type=F32)
    live = weight > 0.0
    number = lax.broadcasted_iota(jnp.int32, (8, total), 1) // rows
    above = lax.broadcasted_iota(jnp.int32, (total, total), 0)
    own = lax.broadcasted_iota(jnp.int32, (total, total), 1)
    ahead = jnp.where((above < own) & (above >= (number * rows)[0:1]), 1.0, 0.0).astype(BF16)
    before = jnp.dot(jnp.where(live, 1.0, 0.0).astype(BF16), ahead, preferred_element_type=F32)
    return jnp.where(live, before.astype(jnp.int32) + number * capacity, -1)[0:1]


def slot_column(tails, me, experts, rows, capacity):
    total = tails.shape[0]
    column = lax.broadcasted_iota(jnp.int32, tails.shape, 1)
    mine = (column == me) | (column == experts + me)
    weight = jnp.sum(jnp.where(mine, tails.astype(F32), 0.0), axis=1, keepdims=True)
    live = weight > 0.0
    number = lax.broadcasted_iota(jnp.int32, (total, 1), 0) // rows
    own = lax.broadcasted_iota(jnp.int32, (total, total), 0)
    above = lax.broadcasted_iota(jnp.int32, (total, total), 1)
    ahead = jnp.where((above < own) & (above >= number * rows), 1.0, 0.0).astype(BF16)
    flags = jnp.broadcast_to(jnp.where(live, 1.0, 0.0), (total, LANES)).astype(BF16)
    before = jnp.dot(ahead, flags, preferred_element_type=F32)[:, 0:1]
    return jnp.where(live, before.astype(jnp.int32) + number * capacity, -1), weight


def layout(groups, capacity):
    offsets, total = [], 0
    for _, members in groups:
        offsets.append(total)
        total += -(-len(members) * capacity // 16) * 16
    return offsets + [total]


def multiply(x_ref, rows, weights, start, units, out_ref):
    def store(x, w, column, count):
        out_ref[rows, column:column + count] = jnp.dot(x, w, preferred_element_type=F32).astype(out_ref.dtype)

    x = x_ref[rows, :]
    if start is None:
        w_ref = weights[0]
        step = tile(w_ref.shape[1], (256, 384))
        for column in range(0, w_ref.shape[1], step):
            store(x, w_ref[:, column:column + step], column, step)
        return
    full = units // 256 * 256
    for i, ref in enumerate(weights):
        for column in range(0, full, 256):
            store(x, ref[:, pl.ds(pl.multiple_of(start + column, LANES), 256)], i * units + column, 256)
    if full < units:
        rest = pl.ds(pl.multiple_of(start + full, LANES), units - full)
        w = jnp.concatenate([ref[:, rest] for ref in weights], axis=1)
        y = jnp.dot(x, w, preferred_element_type=F32).astype(out_ref.dtype)
        out_ref[rows, full:units] = y[:, :units - full]
        out_ref[rows, units + full:] = y[:, units - full:]


def position(units):
    core, rank, parts = lax.axis_index("dp"), lax.axis_index("tensor"), lax.axis_size("tensor")
    first = lax.axis_index("expert") * 2
    places = [(rank + parts - s) % parts * units for s in range(parts)]
    return (first + core, first + 1 - core), (rank + 1) % parts * units, rank * units, places


def pick_kernel(width, experts, capacity, units, groups, count, kinds, split, *refs):
    blocks, weights = refs[:count], refs[count:]
    chosen_ref, part_ref = refs[-2:]
    rows = blocks[0].shape[0]
    mine_and_other, start, _, _ = position(units)
    offsets = layout(groups, capacity)
    step = tile(width, (512, 256))
    for g, (expert, members) in enumerate(groups):
        tails = jnp.concatenate([blocks[m][:, width:] for m in members], axis=0)
        slot = slot_row(tails, mine_and_other[expert], experts, rows, capacity)
        here = offsets[g + 1] - offsets[g]
        place = lax.broadcasted_iota(jnp.int32, (here, len(members) * rows), 0)
        pick = jnp.where(place == slot, 1.0, 0.0).astype(BF16)
        for column in range(0, width, step):
            x = jnp.concatenate([blocks[m][:, column:column + step] for m in members], axis=0)
            value = jnp.dot(pick, x, preferred_element_type=F32).astype(BF16)
            chosen_ref[offsets[g]:offsets[g + 1], column:column + step] = value
    for g in range(len(groups)):
        mine = weights[kinds * g:kinds * (g + 1)]
        multiply(chosen_ref, slice(offsets[g], offsets[g + 1]), mine, start if split else None, units, part_ref)


def pick_rows(groups, blocks, weights, split, after, width, experts, capacity, units):
    columns = 2 * units if split else weights[0][0].shape[1]
    taken = layout(groups, capacity)[-1]
    flat = [w for expert, _ in groups for w in weights[expert]]
    kernel = functools.partial(
        pick_kernel, width, experts, capacity, units, groups, len(blocks), len(weights[0]), split
    )
    out = (jax.ShapeDtypeStruct((taken, width), BF16), jax.ShapeDtypeStruct((taken, columns), BF16))
    return pl.pallas_call(
        kernel,
        grid=(1,),
        out_shape=out,
        in_specs=[whole(x) for x in (*blocks, *flat)] + [ANY] * len(after),
        out_specs=tuple(whole(o) for o in out),
        compiler_params=params(),
        cost_estimate=cost(),
    )(*blocks, *flat, *after)


def home_kernel(capacity, units, groups, kinds, split, passed, copied, x_ref, *refs):
    if copied:
        source_ref, target_ref, sem = refs[-4 - 2 * passed], refs[-2], refs[-1]
        copy = pltpu.make_async_copy(source_ref, target_ref, sem)
        copy.start()
        refs = refs[:-2]
    _, _, start, _ = position(units)
    out_ref = refs[-1 - passed]
    offsets = layout(groups, capacity)
    for g in range(len(groups)):
        mine = refs[kinds * g:kinds * (g + 1)]
        multiply(x_ref, slice(offsets[g], offsets[g + 1]), mine, start if split else None, units, out_ref)
    if copied:
        copy.wait()


def home_rows(groups, chosen, weights, split, passing, copying, after, capacity, units):
    flat = [w for expert, _ in groups for w in weights[expert]]
    out = jax.ShapeDtypeStruct((chosen.shape[0], 2 * units), F32)
    args = (chosen, *flat, *after, *copying, *passing)
    count, copied = len(passing), len(copying)
    result = pl.pallas_call(
        functools.partial(home_kernel, capacity, units, groups, len(weights[0]), split, count, copied),
        grid=(1,),
        out_shape=(out, *[jax.ShapeDtypeStruct(p.shape, p.dtype) for p in (*passing, *copying)]),
        in_specs=[whole(chosen)] + [whole(w) for w in flat] + [ANY] * (len(after) + copied + count),
        out_specs=(whole(out), *[ANY] * (count + copied)),
        input_output_aliases={len(args) - count + i: 1 + i for i in range(count)},
        scratch_shapes=[pltpu.SemaphoreType.DMA] * copied,
        compiler_params=params(),
        cost_estimate=cost(),
    )(*args)
    return result[0], result[1:1 + count], result[1 + count:]


def down_kernel(experts, capacity, groups, count, pieces, wide, passed, *refs):
    hiddens, refs = refs[:pieces], refs[pieces:]
    tail_refs, weights = refs[:count], refs[count:]
    scratch = refs[-len(groups):]
    out_ref = refs[-len(groups) - 1 - passed]
    rows = tail_refs[0].shape[0]
    units = hiddens[0].shape[1]
    mine_and_other, _, _, starts = position(units)
    offsets = layout(groups, capacity)
    width = out_ref.shape[1]
    step = tile(width, (256,))
    shares = []
    for g, (expert, members) in enumerate(groups):
        tails = jnp.concatenate([tail_refs[m][...] for m in members], axis=0)
        slot, weight = slot_column(tails, mine_and_other[expert], experts, rows, capacity)
        shares.append(jnp.broadcast_to(weight, (len(members) * rows, step)))
        place = lax.broadcasted_iota(jnp.int32, (len(members) * rows, offsets[g + 1] - offsets[g]), 1)
        spread = jnp.where(place == slot, 1.0, 0.0).astype(BF16)
        for s, ref in enumerate(hiddens):
            value = jnp.dot(spread, ref[offsets[g]:offsets[g + 1], :], preferred_element_type=F32).astype(BF16)
            if wide:
                scratch[g][:, pl.ds(pl.multiple_of(starts[s], LANES), units)] = value
            else:
                scratch[g][s] = value
    for column in range(0, width, step):
        sums = [None] * count
        for g, (expert, members) in enumerate(groups):
            w_ref = weights[g]
            if wide:
                result = jnp.dot(scratch[g][...], w_ref[:, column:column + step], preferred_element_type=F32)
            else:
                result = jnp.zeros((len(members) * rows, step), F32)
                for s in range(pieces):
                    w = w_ref[pl.ds(pl.multiple_of(starts[s], 16), units), column:column + step]
                    result = result + jnp.dot(scratch[g][s], w, preferred_element_type=F32)
            result = result * shares[g]
            for k, m in enumerate(members):
                part = result[k * rows:(k + 1) * rows]
                sums[m] = part if sums[m] is None else sums[m] + part
        for m, value in enumerate(sums):
            out_ref[m * rows:(m + 1) * rows, column:column + step] = value.astype(BF16)


def down_rows(groups, hiddens, blocks, weights, passing, after, width, experts, capacity):
    rows, padded = blocks[0].shape
    units = hiddens[0].shape[1]
    pieces = len(hiddens)
    wide = units % LANES == 0
    tail = pl.BlockSpec((rows, padded - width), lambda i: (0, width // (padded - width)))
    scratch = []
    for _, members in groups:
        spread = (len(members) * rows, pieces * units) if wide else (pieces, len(members) * rows, units)
        scratch.append(pltpu.VMEM(spread, BF16))
    out = jax.ShapeDtypeStruct((len(blocks) * rows, width), BF16)
    args = (*hiddens, *blocks, *[weights[e] for e, _ in groups], *after, *passing)
    result = pl.pallas_call(
        functools.partial(down_kernel, experts, capacity, groups, len(blocks), pieces, wide, len(passing)),
        grid=(1,),
        out_shape=(out, *[jax.ShapeDtypeStruct(p.shape, p.dtype) for p in passing]),
        in_specs=[whole(h) for h in hiddens] + [tail] * len(blocks)
        + [whole(weights[0])] * len(groups) + [ANY] * (len(after) + len(passing)),
        out_specs=(whole(out), *[ANY] * len(passing)),
        input_output_aliases={len(args) - len(passing) + i: 1 + i for i in range(len(passing))},
        scratch_shapes=scratch,
        compiler_params=params(),
        cost_estimate=cost(),
    )(*args)
    return result[0], result[1:]


def add_kernel(count, *refs):
    out_ref = refs[-1]
    total = refs[0][...].astype(F32)
    for ref in refs[1:count]:
        total = total + ref[...].astype(F32)
    out_ref[...] = total.astype(out_ref.dtype)


def added(terms, kind, after):
    out = jax.ShapeDtypeStruct(terms[0].shape, kind)
    return pl.pallas_call(
        functools.partial(add_kernel, len(terms)),
        grid=(1,),
        out_shape=out,
        in_specs=[whole(t) for t in terms] + [ANY] * len(after),
        out_specs=whole(out),
        compiler_params=params(),
        cost_estimate=cost(),
    )(*terms, *after)


def on_device(tokens, expert_ids, route_weights, w_gate, w_up, w_down):
    rows, width = tokens.shape
    top = expert_ids.shape[1]
    ring = lax.axis_size("expert")
    experts = ring * lax.axis_size("dp")
    capacity = min(rows, max(2, 3 * rows * top // (2 * experts)))
    parts = lax.axis_size("tensor")
    units = w_gate.shape[2] // parts
    rank = lax.axis_index("tensor")
    hops = ring // 2

    def over_y(x):
        return lax.ppermute(x, "expert", [(i, i ^ 1) for i in range(ring)])

    def over_z(x):
        return lax.ppermute(x, "expert", [(i, (i + 2) % ring) for i in range(ring)])

    def home_over_both(x, hop):
        return lax.ppermute(x, "expert", [(i, ((i - 2 * hop) % ring) ^ 1) for i in range(ring)])

    def over_core(x):
        return lax.ppermute(x, "dp", [(0, 1), (1, 0)])

    def over_x(x, step):
        return lax.ppermute(x, "tensor", [(i, (i + step) % parts) for i in range(parts)])

    gates = (w_gate[0], over_core(w_gate)[0])
    ups = (w_up[0], over_core(w_up)[0])
    split = parts == 2 and units % LANES == 0
    if split:
        away = home = tuple(zip(gates, ups))
    else:
        def unit_slice(w, offset):
            return lax.dynamic_slice_in_dim(w, (rank + offset) % parts * units, units, 1)

        away, home = [], []
        for gate, up in zip(gates, ups):
            pairs = [(unit_slice(gate, s), unit_slice(up, s)) for s in range(parts)]
            away.append((jnp.concatenate([w for pair in pairs[1:] for w in pair], axis=1),))
            home.append((jnp.concatenate(pairs[0], axis=1),))

    blocks, arrived = {(0, "s"): make_block(tokens, expert_ids, route_weights, experts)}, {}
    blocks[0, "c"] = over_core(blocks[0, "s"])

    def send_on(hop):
        block = blocks[hop, "s"]
        if hop + 1 < hops:
            arrived[hop + 1] = over_z(block)
        blocks[hop, "b"] = over_y(block)

    both = ((0, (0, 1)), (1, (0, 1)))
    one = ((0, (0,)), (1, (0,)))
    plan = [([(0, "s")], ((0, (0,)),)), ([(0, "s"), (0, "b"), (1, "s")], ((1, (0, 1, 2)), (0, (1, 2))))]
    plan += [([(1, "b")], one)] + [([(hop, "b"), (hop, "s")], both) for hop in range(2, hops - 1)]
    plan += [([(hops - 1, "b")], one), ([(hops - 1, "s")], one)]
    count = len(plan)
    straight = ()
    chosen, parts_in, totals, hidden, returned, carried, gathered = {}, {}, {}, {}, {}, {}, []
    downs = [w_down[0]]
    order = []

    def passing(hop):
        return [arrived[hop]] if hop in arrived else []

    def take_on(hop, passed):
        if passed:
            blocks[hop, "s"] = passed[0]
            send_on(hop)

    def pick(i):
        keys, groups = plan[i]
        mine = [blocks[k] for k in keys]
        chosen[i], part = pick_rows(groups, mine, away, split, order, width, experts, capacity, units)
        cut = units if i == 1 else 2 * units
        parts_in[i] = []
        for step in range(1, parts):
            columns = range(2 * units * (step - 1), 2 * units * step, cut)
            parts_in[i].append([over_x(part[:, c:c + cut], step) for c in columns])
        order[:] = [part]

    def home_product(i, hop=None):
        copying = [w_down] if i == 0 else []
        totals[i], passed, copies = home_rows(
            plan[i][1], chosen[i], home, split, passing(hop), copying, order, capacity, units
        )
        downs.extend(over_core(c)[0] for c in copies)
        order[:] = [totals[i]]
        take_on(hop, passed)

    def activate(i):
        total = totals[i]
        for pieces in parts_in[i]:
            total = total + jnp.concatenate(pieces, axis=1).astype(F32)
        value = (jax.nn.silu(total[:, :units]) * total[:, units:]).astype(BF16)
        hidden[i] = [value] + [over_x(value, s) for s in range(1, parts)]
        order.append(value)

    def down_product(i, hop=None):
        keys, groups = plan[i]
        mine = [blocks[k] for k in keys]
        term, passed = down_rows(
            groups, hidden[i], mine, downs, passing(hop), order, width, experts, capacity
        )
        order[:] = [term]
        take_on(hop, passed)
        for k, (at, kind) in enumerate(keys):
            piece = term[k * rows:(k + 1) * rows]
            if kind == "b" and at in straight:
                gathered.append(home_over_both(piece, at))
            elif kind == "b":
                returned[at, "b"] = over_y(piece)
            elif kind == "c":
                gathered.append(over_core(piece))
            elif at == 0:
                gathered.append(piece)
            else:
                returned[at, "s"] = piece

    def add_hop(hop):
        if hop == 0:
            gathered[:] = [added(gathered + [returned[hop, "b"]], F32, order)]
            order[:] = [gathered[0]]
        else:
            terms = [returned[hop, "s"]] + ([returned[hop, "b"]] if hop not in straight else [])
            terms += [carried[hop]] if hop in carried else []
            total = added(terms, BF16, order)
            order[:] = [total]
            carried[hop + 1] = over_z(total)

    def await_beside(hop):
        if (hop, "b") in blocks:
            order.append(blocks[hop, "b"])

    send_on(0)
    if hops == 4:
        pick(0)
        order.append(blocks[0, "b"])
        home_product(0, 1)
        pick(1)
        activate(0)
        order.extend(downs[1:])
        home_product(1, 2)
        pick(2)
        down_product(0)
        home_product(2, 3)
        activate(2)
        activate(1)
        pick(3)
        down_product(1)
        down_product(2)
        pick(4)
        home_product(3)
        activate(3)
        home_product(4)
        pick(5)
        order.append(blocks[2, "b"])
        order.extend(downs[1:])
        activate(4)
        home_product(5)
        add_hop(1)
        order.append(blocks[2, "b"])
        down_product(3)
        down_product(4)
        activate(5)
        add_hop(2)
        order.append(blocks[1, "b"])
        down_product(5)
        add_hop(3)
        add_hop(0)
    else:
        for i in range(count):
            pick(i)
            home_product(i, i + 1)
            if i > 0:
                activate(i - 1)
                down_product(i - 1)
        activate(count - 1)
        down_product(count - 1)
        for hop in range(hops):
            add_hop(hop)
    return sum(x.astype(F32) for x in gathered + [carried[hops]]).astype(BF16)


def solution(mesh):
    placed = (
        P(("group", "expert", "dp"), "tensor"),
        P(("group", "expert", "dp"), None),
        P(("group", "expert", "dp"), None),
        P(("expert", "dp"), "tensor", None),
        P(("expert", "dp"), "tensor", None),
        P(("expert", "dp"), None, "tensor"),
    )
    return jax.shard_map(
        on_device,
        mesh=mesh,
        in_specs=placed,
        out_specs=P(("group", "expert", "dp"), "tensor"),
        check_vma=False,
    )
```

```python
import functools

import jax
import jax.numpy as jnp
from jax import lax
from jax.experimental import pallas as pl
from jax.experimental.pallas import tpu as pltpu
from jax.sharding import PartitionSpec as P

F32 = jnp.float32
BF16 = jnp.bfloat16
LANES = 128
VMEM = 10 * 1024 * 1024
ANY = pl.BlockSpec(memory_space=pl.ANY)
HBM = pl.BlockSpec(memory_space=pltpu.HBM)


def tile(extent, choices):
    for size in choices:
        if extent % size == 0:
            return size
    return extent


def whole(x):
    return pl.BlockSpec(x.shape, lambda i: (0,) * len(x.shape))


def params():
    return pltpu.CompilerParams(vmem_limit_bytes=VMEM)


def cost():
    return pl.CostEstimate(flops=1, bytes_accessed=1, transcendentals=0)


def block_kernel(experts, tokens_ref, routes_ref, out_ref, sem):
    rows, width = tokens_ref.shape
    copy = pltpu.make_async_copy(tokens_ref, out_ref.at[:, :width], sem)
    copy.start()
    routes = routes_ref[...].T
    top = routes.shape[1] // 2
    column = lax.broadcasted_iota(jnp.int32, (rows, out_ref.shape[1] - width), 1)
    expert = jnp.where(column < experts, column, column - experts).astype(F32)
    value = jnp.zeros(column.shape, F32)
    for k in range(top):
        value = value + jnp.where(expert == routes[:, k:k + 1], routes[:, top + k:top + k + 1], 0.0)
    high = value.astype(BF16).astype(F32)
    out_ref[:, width:] = jnp.where(column < experts, high, value - high).astype(BF16)
    copy.wait()


def make_block(tokens, expert_ids, route_weights, experts):
    rows, width = tokens.shape
    padded = width + 2 * experts + (-(2 * experts)) % LANES
    routes = jnp.concatenate([expert_ids.T.astype(F32), route_weights.T], axis=0)
    return pl.pallas_call(
        functools.partial(block_kernel, experts),
        grid=(1,),
        out_shape=jax.ShapeDtypeStruct((rows, padded), BF16),
        in_specs=[HBM, whole(routes)],
        out_specs=pl.BlockSpec((rows, padded), lambda i: (0, 0)),
        scratch_shapes=[pltpu.SemaphoreType.DMA],
        compiler_params=params(),
        cost_estimate=cost(),
    )(tokens, routes)


def slot_row(tails, me, experts, rows, capacity):
    total = tails.shape[0]
    column = lax.broadcasted_iota(jnp.int32, (8, tails.shape[1]), 1)
    mark = jnp.where((column == me) | (column == experts + me), 1.0, 0.0).astype(BF16)
    weight = lax.dot_general(mark, tails, (((1,), (1,)), ((), ())), preferred_element_type=F32)
    live = weight > 0.0
    number = lax.broadcasted_iota(jnp.int32, (8, total), 1) // rows
    above = lax.broadcasted_iota(jnp.int32, (total, total), 0)
    own = lax.broadcasted_iota(jnp.int32, (total, total), 1)
    ahead = jnp.where((above < own) & (above >= (number * rows)[0:1]), 1.0, 0.0).astype(BF16)
    before = jnp.dot(jnp.where(live, 1.0, 0.0).astype(BF16), ahead, preferred_element_type=F32)
    return jnp.where(live, before.astype(jnp.int32) + number * capacity, -1)[0:1]


def slot_column(tails, me, experts, rows, capacity):
    total = tails.shape[0]
    column = lax.broadcasted_iota(jnp.int32, tails.shape, 1)
    mine = (column == me) | (column == experts + me)
    weight = jnp.sum(jnp.where(mine, tails.astype(F32), 0.0), axis=1, keepdims=True)
    live = weight > 0.0
    number = lax.broadcasted_iota(jnp.int32, (total, 1), 0) // rows
    own = lax.broadcasted_iota(jnp.int32, (total, total), 0)
    above = lax.broadcasted_iota(jnp.int32, (total, total), 1)
    ahead = jnp.where((above < own) & (above >= number * rows), 1.0, 0.0).astype(BF16)
    flags = jnp.broadcast_to(jnp.where(live, 1.0, 0.0), (total, LANES)).astype(BF16)
    before = jnp.dot(ahead, flags, preferred_element_type=F32)[:, 0:1]
    return jnp.where(live, before.astype(jnp.int32) + number * capacity, -1), weight


def layout(groups, capacity):
    offsets, total = [], 0
    for _, members in groups:
        offsets.append(total)
        total += -(-len(members) * capacity // 16) * 16
    return offsets + [total]


def multiply(x_ref, rows, weights, start, units, out_ref):
    def store(x, w, column, count):
        out_ref[rows, column:column + count] = jnp.dot(x, w, preferred_element_type=F32).astype(out_ref.dtype)

    x = x_ref[rows, :]
    if start is None:
        w_ref = weights[0]
        step = tile(w_ref.shape[1], (256, 384))
        for column in range(0, w_ref.shape[1], step):
            store(x, w_ref[:, column:column + step], column, step)
        return
    full = units // 256 * 256
    for i, ref in enumerate(weights):
        for column in range(0, full, 256):
            store(x, ref[:, pl.ds(pl.multiple_of(start + column, LANES), 256)], i * units + column, 256)
    if full < units:
        rest = pl.ds(pl.multiple_of(start + full, LANES), units - full)
        w = jnp.concatenate([ref[:, rest] for ref in weights], axis=1)
        y = jnp.dot(x, w, preferred_element_type=F32).astype(out_ref.dtype)
        out_ref[rows, full:units] = y[:, :units - full]
        out_ref[rows, units + full:] = y[:, units - full:]


def position(units):
    core, rank, parts = lax.axis_index("dp"), lax.axis_index("tensor"), lax.axis_size("tensor")
    first = lax.axis_index("expert") * 2
    places = [(rank + parts - s) % parts * units for s in range(parts)]
    return (first + core, first + 1 - core), (rank + 1) % parts * units, rank * units, places


def pick_kernel(width, experts, capacity, units, groups, count, kinds, split, copied, *refs):
    blocks, weights = refs[:count], refs[count:]
    if copied:
        *_, source_ref, chosen_ref, part_ref, target_ref, sem = refs
        copy = pltpu.make_async_copy(source_ref, target_ref, sem)
        copy.start()
    else:
        chosen_ref, part_ref = refs[-2:]
    rows = blocks[0].shape[0]
    mine_and_other, start, _, _ = position(units)
    offsets = layout(groups, capacity)
    step = tile(width, (512, 256))
    for g, (expert, members) in enumerate(groups):
        tails = jnp.concatenate([blocks[m][:, width:] for m in members], axis=0)
        slot = slot_row(tails, mine_and_other[expert], experts, rows, capacity)
        here = offsets[g + 1] - offsets[g]
        place = lax.broadcasted_iota(jnp.int32, (here, len(members) * rows), 0)
        pick = jnp.where(place == slot, 1.0, 0.0).astype(BF16)
        for column in range(0, width, step):
            x = jnp.concatenate([blocks[m][:, column:column + step] for m in members], axis=0)
            value = jnp.dot(pick, x, preferred_element_type=F32).astype(BF16)
            chosen_ref[offsets[g]:offsets[g + 1], column:column + step] = value
    for g in range(len(groups)):
        mine = weights[kinds * g:kinds * (g + 1)]
        multiply(chosen_ref, slice(offsets[g], offsets[g + 1]), mine, start if split else None, units, part_ref)
    if copied:
        copy.wait()


def pick_rows(groups, blocks, weights, split, copying, after, width, experts, capacity, units):
    columns = 2 * units if split else weights[0][0].shape[1]
    taken = layout(groups, capacity)[-1]
    flat = [w for expert, _ in groups for w in weights[expert]]
    copied = len(copying)
    kernel = functools.partial(
        pick_kernel, width, experts, capacity, units, groups, len(blocks), len(weights[0]), split, copied
    )
    out = (jax.ShapeDtypeStruct((taken, width), BF16), jax.ShapeDtypeStruct((taken, columns), BF16))
    return pl.pallas_call(
        kernel,
        grid=(1,),
        out_shape=(*out, *[jax.ShapeDtypeStruct(a.shape, a.dtype) for a in copying]),
        in_specs=[whole(x) for x in (*blocks, *flat)] + [ANY] * (len(after) + copied),
        out_specs=(*[whole(o) for o in out], *[ANY] * copied),
        scratch_shapes=[pltpu.SemaphoreType.DMA] * copied,
        compiler_params=params(),
        cost_estimate=cost(),
    )(*blocks, *flat, *after, *copying)


def home_kernel(capacity, units, groups, kinds, split, passed, x_ref, *refs):
    _, _, start, _ = position(units)
    out_ref = refs[-1 - passed]
    offsets = layout(groups, capacity)
    for g in range(len(groups)):
        mine = refs[kinds * g:kinds * (g + 1)]
        multiply(x_ref, slice(offsets[g], offsets[g + 1]), mine, start if split else None, units, out_ref)


def home_rows(groups, chosen, weights, split, passing, after, capacity, units):
    flat = [w for expert, _ in groups for w in weights[expert]]
    out = jax.ShapeDtypeStruct((chosen.shape[0], 2 * units), F32)
    args = (chosen, *flat, *after, *passing)
    result = pl.pallas_call(
        functools.partial(home_kernel, capacity, units, groups, len(weights[0]), split, len(passing)),
        grid=(1,),
        out_shape=(out, *[jax.ShapeDtypeStruct(p.shape, p.dtype) for p in passing]),
        in_specs=[whole(chosen)] + [whole(w) for w in flat] + [ANY] * (len(after) + len(passing)),
        out_specs=(whole(out), *[ANY] * len(passing)),
        input_output_aliases={len(args) - len(passing) + i: 1 + i for i in range(len(passing))},
        compiler_params=params(),
        cost_estimate=cost(),
    )(*args)
    return result[0], result[1:]


def down_kernel(experts, capacity, groups, count, pieces, wide, passed, *refs):
    hiddens, refs = refs[:pieces], refs[pieces:]
    tail_refs, weights = refs[:count], refs[count:]
    scratch = refs[-len(groups):]
    out_ref = refs[-len(groups) - 1 - passed]
    rows = tail_refs[0].shape[0]
    units = hiddens[0].shape[1]
    mine_and_other, _, _, starts = position(units)
    offsets = layout(groups, capacity)
    width = out_ref.shape[1]
    step = tile(width, (256,))
    shares = []
    for g, (expert, members) in enumerate(groups):
        tails = jnp.concatenate([tail_refs[m][...] for m in members], axis=0)
        slot, weight = slot_column(tails, mine_and_other[expert], experts, rows, capacity)
        shares.append(jnp.broadcast_to(weight, (len(members) * rows, step)))
        place = lax.broadcasted_iota(jnp.int32, (len(members) * rows, offsets[g + 1] - offsets[g]), 1)
        spread = jnp.where(place == slot, 1.0, 0.0).astype(BF16)
        for s, ref in enumerate(hiddens):
            value = jnp.dot(spread, ref[offsets[g]:offsets[g + 1], :], preferred_element_type=F32).astype(BF16)
            if wide:
                scratch[g][:, pl.ds(pl.multiple_of(starts[s], LANES), units)] = value
            else:
                scratch[g][s] = value
    for column in range(0, width, step):
        sums = [None] * count
        for g, (expert, members) in enumerate(groups):
            w_ref = weights[g]
            if wide:
                result = jnp.dot(scratch[g][...], w_ref[:, column:column + step], preferred_element_type=F32)
            else:
                result = jnp.zeros((len(members) * rows, step), F32)
                for s in range(pieces):
                    w = w_ref[pl.ds(pl.multiple_of(starts[s], 16), units), column:column + step]
                    result = result + jnp.dot(scratch[g][s], w, preferred_element_type=F32)
            result = result * shares[g]
            for k, m in enumerate(members):
                part = result[k * rows:(k + 1) * rows]
                sums[m] = part if sums[m] is None else sums[m] + part
        for m, value in enumerate(sums):
            out_ref[m * rows:(m + 1) * rows, column:column + step] = value.astype(BF16)


def down_rows(groups, hiddens, blocks, weights, passing, after, width, experts, capacity):
    rows, padded = blocks[0].shape
    units = hiddens[0].shape[1]
    pieces = len(hiddens)
    wide = units % LANES == 0
    tail = pl.BlockSpec((rows, padded - width), lambda i: (0, width // (padded - width)))
    scratch = []
    for _, members in groups:
        spread = (len(members) * rows, pieces * units) if wide else (pieces, len(members) * rows, units)
        scratch.append(pltpu.VMEM(spread, BF16))
    out = jax.ShapeDtypeStruct((len(blocks) * rows, width), BF16)
    args = (*hiddens, *blocks, *[weights[e] for e, _ in groups], *after, *passing)
    result = pl.pallas_call(
        functools.partial(down_kernel, experts, capacity, groups, len(blocks), pieces, wide, len(passing)),
        grid=(1,),
        out_shape=(out, *[jax.ShapeDtypeStruct(p.shape, p.dtype) for p in passing]),
        in_specs=[whole(h) for h in hiddens] + [tail] * len(blocks)
        + [whole(weights[0])] * len(groups) + [ANY] * (len(after) + len(passing)),
        out_specs=(whole(out), *[ANY] * len(passing)),
        input_output_aliases={len(args) - len(passing) + i: 1 + i for i in range(len(passing))},
        scratch_shapes=scratch,
        compiler_params=params(),
        cost_estimate=cost(),
    )(*args)
    return result[0], result[1:]


def add_kernel(count, *refs):
    out_ref = refs[-1]
    total = refs[0][...].astype(F32)
    for ref in refs[1:count]:
        total = total + ref[...].astype(F32)
    out_ref[...] = total.astype(out_ref.dtype)


def added(terms, kind, after):
    out = jax.ShapeDtypeStruct(terms[0].shape, kind)
    return pl.pallas_call(
        functools.partial(add_kernel, len(terms)),
        grid=(1,),
        out_shape=out,
        in_specs=[whole(t) for t in terms] + [ANY] * len(after),
        out_specs=whole(out),
        compiler_params=params(),
        cost_estimate=cost(),
    )(*terms, *after)


def on_device(tokens, expert_ids, route_weights, w_gate, w_up, w_down):
    rows, width = tokens.shape
    top = expert_ids.shape[1]
    ring = lax.axis_size("expert")
    experts = ring * lax.axis_size("dp")
    capacity = min(rows, max(2, 3 * rows * top // (2 * experts)))
    parts = lax.axis_size("tensor")
    units = w_gate.shape[2] // parts
    rank = lax.axis_index("tensor")
    hops = ring // 2

    def over_y(x):
        return lax.ppermute(x, "expert", [(i, i ^ 1) for i in range(ring)])

    def over_z(x):
        return lax.ppermute(x, "expert", [(i, (i + 2) % ring) for i in range(ring)])

    def home_over_both(x, hop):
        return lax.ppermute(x, "expert", [(i, ((i - 2 * hop) % ring) ^ 1) for i in range(ring)])

    def over_core(x):
        return lax.ppermute(x, "dp", [(0, 1), (1, 0)])

    def over_x(x, step):
        return lax.ppermute(x, "tensor", [(i, (i + step) % parts) for i in range(parts)])

    gates = (w_gate[0], over_core(w_gate)[0])
    ups = (w_up[0], over_core(w_up)[0])
    split = parts == 2 and units % LANES == 0
    if split:
        away = home = tuple(zip(gates, ups))
    else:
        def unit_slice(w, offset):
            return lax.dynamic_slice_in_dim(w, (rank + offset) % parts * units, units, 1)

        away, home = [], []
        for gate, up in zip(gates, ups):
            pairs = [(unit_slice(gate, s), unit_slice(up, s)) for s in range(parts)]
            away.append((jnp.concatenate([w for pair in pairs[1:] for w in pair], axis=1),))
            home.append((jnp.concatenate(pairs[0], axis=1),))

    blocks, arrived = {(0, "s"): make_block(tokens, expert_ids, route_weights, experts)}, {}
    blocks[0, "c"] = over_core(blocks[0, "s"])

    def send_on(hop):
        block = blocks[hop, "s"]
        if hop + 1 < hops:
            arrived[hop + 1] = over_z(block)
        blocks[hop, "b"] = over_y(block)

    both = ((0, (0, 1)), (1, (0, 1)))
    one = ((0, (0,)), (1, (0,)))
    plan = [([(0, "s")], ((0, (0,)),)), ([(0, "s"), (0, "b"), (1, "s")], ((1, (0, 1, 2)), (0, (1, 2))))]
    plan += [([(1, "b")], one)] + [([(hop, "b"), (hop, "s")], both) for hop in range(2, hops - 1)]
    plan += [([(hops - 1, "b")], one), ([(hops - 1, "s")], one)]
    count = len(plan)
    straight = ()
    chosen, parts_in, totals, hidden, returned, carried, gathered = {}, {}, {}, {}, {}, {}, []
    downs = [w_down[0]]
    order = []

    def passing(hop):
        return [arrived[hop]] if hop in arrived else []

    def take_on(hop, passed):
        if passed:
            blocks[hop, "s"] = passed[0]
            send_on(hop)

    def pick(i):
        keys, groups = plan[i]
        mine = [blocks[k] for k in keys]
        copying = [w_down] if i == 1 else []
        chosen[i], part, *copies = pick_rows(
            groups, mine, away, split, copying, order, width, experts, capacity, units
        )
        downs.extend(over_core(c)[0] for c in copies)
        parts_in[i] = [over_x(part[:, 2 * units * (s - 1):2 * units * s], s) for s in range(1, parts)]
        order[:] = [part]

    def home_product(i, hop=None):
        totals[i], passed = home_rows(
            plan[i][1], chosen[i], home, split, passing(hop), order, capacity, units
        )
        order[:] = [totals[i]]
        take_on(hop, passed)

    def activate(i):
        total = totals[i]
        for piece in parts_in[i]:
            total = total + piece.astype(F32)
        value = (jax.nn.silu(total[:, :units]) * total[:, units:]).astype(BF16)
        hidden[i] = [value] + [over_x(value, s) for s in range(1, parts)]
        order.append(value)

    def down_product(i, hop=None):
        keys, groups = plan[i]
        mine = [blocks[k] for k in keys]
        term, passed = down_rows(
            groups, hidden[i], mine, downs, passing(hop), order, width, experts, capacity
        )
        order[:] = [term]
        take_on(hop, passed)
        for k, (at, kind) in enumerate(keys):
            piece = term[k * rows:(k + 1) * rows]
            if kind == "b" and at in straight:
                gathered.append(home_over_both(piece, at))
            elif kind == "b":
                returned[at, "b"] = over_y(piece)
            elif kind == "c":
                gathered.append(over_core(piece))
            elif at == 0:
                gathered.append(piece)
            else:
                returned[at, "s"] = piece

    def add_hop(hop):
        if hop == 0:
            gathered[:] = [added(gathered + [returned[hop, "b"]], F32, order)]
            order[:] = [gathered[0]]
        else:
            terms = [returned[hop, "s"]] + ([returned[hop, "b"]] if hop not in straight else [])
            terms += [carried[hop]] if hop in carried else []
            total = added(terms, BF16, order)
            order[:] = [total]
            carried[hop + 1] = over_z(total)

    def await_beside(hop):
        if (hop, "b") in blocks:
            order.append(blocks[hop, "b"])

    send_on(0)
    if hops == 4:
        pick(0)
        order.append(blocks[0, "b"])
        home_product(0, 1)
        activate(0)
        pick(1)
        order.extend(downs[1:])
        home_product(1, 2)
        pick(2)
        down_product(0)
        home_product(2, 3)
        activate(2)
        pick(3)
        activate(1)
        down_product(1)
        down_product(2)
        pick(4)
        home_product(3)
        home_product(4)
        activate(3)
        pick(5)
        home_product(5)
        order.append(blocks[2, "b"])
        add_hop(0)
        add_hop(1)
        order.append(blocks[0, "b"])
        down_product(3)
        order.append(blocks[2, "b"])
        activate(4)
        down_product(4)
        activate(5)
        add_hop(2)
        down_product(5)
        add_hop(3)
    else:
        for i in range(count):
            pick(i)
            home_product(i, i + 1)
            if i > 0:
                activate(i - 1)
                down_product(i - 1)
        activate(count - 1)
        down_product(count - 1)
        for hop in range(hops):
            add_hop(hop)
    return sum(x.astype(F32) for x in gathered + [carried[hops]]).astype(BF16)


def solution(mesh):
    placed = (
        P(("group", "expert", "dp"), "tensor"),
        P(("group", "expert", "dp"), None),
        P(("group", "expert", "dp"), None),
        P(("expert", "dp"), "tensor", None),
        P(("expert", "dp"), "tensor", None),
        P(("expert", "dp"), None, "tensor"),
    )
    return jax.shard_map(
        on_device,
        mesh=mesh,
        in_specs=placed,
        out_specs=P(("group", "expert", "dp"), "tensor"),
        check_vma=False,
    )
```

```python
import functools

import jax
import jax.numpy as jnp
from jax import lax
from jax.experimental import pallas as pl
from jax.experimental.pallas import tpu as pltpu
from jax.sharding import PartitionSpec as P

F32 = jnp.float32
BF16 = jnp.bfloat16
LANES = 128
VMEM = 10 * 1024 * 1024
ANY = pl.BlockSpec(memory_space=pl.ANY)
HBM = pl.BlockSpec(memory_space=pltpu.HBM)


def tile(extent, choices):
    for size in choices:
        if extent % size == 0:
            return size
    return extent


def whole(x):
    return pl.BlockSpec(x.shape, lambda i: (0,) * len(x.shape))


def params():
    return pltpu.CompilerParams(vmem_limit_bytes=VMEM)


def cost():
    return pl.CostEstimate(flops=1, bytes_accessed=1, transcendentals=0)


def block_kernel(experts, tokens_ref, ids_ref, route_ref, out_ref, ids_buffer, route_buffer, sems):
    rows, width = tokens_ref.shape
    copies = [
        pltpu.make_async_copy(ids_ref, ids_buffer, sems.at[0]),
        pltpu.make_async_copy(route_ref, route_buffer, sems.at[1]),
        pltpu.make_async_copy(tokens_ref, out_ref.at[:, :width], sems.at[2]),
    ]
    for copy in copies:
        copy.start()
    copies[0].wait()
    copies[1].wait()
    ids = ids_buffer[...].T
    route = route_buffer[...].T
    column = lax.broadcasted_iota(jnp.int32, (rows, out_ref.shape[1] - width), 1)
    expert = jnp.where(column < experts, column, column - experts)
    value = jnp.zeros(column.shape, F32)
    for k in range(ids.shape[1]):
        value = value + jnp.where(expert == ids[:, k:k + 1], route[:, k:k + 1], 0.0)
    high = value.astype(BF16).astype(F32)
    out_ref[:, width:] = jnp.where(column < experts, high, value - high).astype(BF16)
    copies[2].wait()


def make_block(tokens, expert_ids, route_weights, experts):
    rows, width = tokens.shape
    padded = width + 2 * experts + (-(2 * experts)) % LANES
    args = (tokens, expert_ids.T, route_weights.T)
    return pl.pallas_call(
        functools.partial(block_kernel, experts),
        grid=(1,),
        out_shape=jax.ShapeDtypeStruct((rows, padded), BF16),
        in_specs=[HBM] * 3,
        out_specs=pl.BlockSpec((rows, padded), lambda i: (0, 0)),
        scratch_shapes=[
            pltpu.VMEM(args[1].shape, jnp.int32),
            pltpu.VMEM(args[2].shape, F32),
            pltpu.SemaphoreType.DMA((3,)),
        ],
        compiler_params=params(),
        cost_estimate=cost(),
    )(*args)


def slot_row(tails, me, experts, rows, capacity):
    total = tails.shape[0]
    column = lax.broadcasted_iota(jnp.int32, (8, tails.shape[1]), 1)
    mark = jnp.where((column == me) | (column == experts + me), 1.0, 0.0).astype(BF16)
    weight = lax.dot_general(mark, tails, (((1,), (1,)), ((), ())), preferred_element_type=F32)
    live = weight > 0.0
    number = lax.broadcasted_iota(jnp.int32, (8, total), 1) // rows
    above = lax.broadcasted_iota(jnp.int32, (total, total), 0)
    own = lax.broadcasted_iota(jnp.int32, (total, total), 1)
    ahead = jnp.where((above < own) & (above >= (number * rows)[0:1]), 1.0, 0.0).astype(BF16)
    before = jnp.dot(jnp.where(live, 1.0, 0.0).astype(BF16), ahead, preferred_element_type=F32)
    return jnp.where(live, before.astype(jnp.int32) + number * capacity, -1)[0:1]


def slot_column(tails, me, experts, rows, capacity):
    total = tails.shape[0]
    column = lax.broadcasted_iota(jnp.int32, tails.shape, 1)
    mine = (column == me) | (column == experts + me)
    weight = jnp.sum(jnp.where(mine, tails.astype(F32), 0.0), axis=1, keepdims=True)
    live = weight > 0.0
    number = lax.broadcasted_iota(jnp.int32, (total, 1), 0) // rows
    own = lax.broadcasted_iota(jnp.int32, (total, total), 0)
    above = lax.broadcasted_iota(jnp.int32, (total, total), 1)
    ahead = jnp.where((above < own) & (above >= number * rows), 1.0, 0.0).astype(BF16)
    flags = jnp.broadcast_to(jnp.where(live, 1.0, 0.0), (total, LANES)).astype(BF16)
    before = jnp.dot(ahead, flags, preferred_element_type=F32)[:, 0:1]
    return jnp.where(live, before.astype(jnp.int32) + number * capacity, -1), weight


def layout(groups, capacity):
    offsets, total = [], 0
    for _, members in groups:
        offsets.append(total)
        total += -(-len(members) * capacity // 16) * 16
    return offsets + [total]


def multiply(x_ref, rows, weights, start, units, out_ref):
    def store(x, w, column, count):
        out_ref[rows, column:column + count] = jnp.dot(x, w, preferred_element_type=F32).astype(out_ref.dtype)

    x = x_ref[rows, :]
    if start is None:
        w_ref = weights[0]
        step = tile(w_ref.shape[1], (256, 384))
        for column in range(0, w_ref.shape[1], step):
            store(x, w_ref[:, column:column + step], column, step)
        return
    full = units // 256 * 256
    for i, ref in enumerate(weights):
        for column in range(0, full, 256):
            store(x, ref[:, pl.ds(pl.multiple_of(start + column, LANES), 256)], i * units + column, 256)
    if full < units:
        rest = pl.ds(pl.multiple_of(start + full, LANES), units - full)
        w = jnp.concatenate([ref[:, rest] for ref in weights], axis=1)
        y = jnp.dot(x, w, preferred_element_type=F32).astype(out_ref.dtype)
        out_ref[rows, full:units] = y[:, :units - full]
        out_ref[rows, units + full:] = y[:, units - full:]


def position(units):
    core, rank, parts = lax.axis_index("dp"), lax.axis_index("tensor"), lax.axis_size("tensor")
    first = lax.axis_index("expert") * 2
    places = [(rank + parts - s) % parts * units for s in range(parts)]
    return (first + core, first + 1 - core), (rank + 1) % parts * units, rank * units, places


def pick_kernel(width, experts, capacity, units, groups, count, kinds, split, copied, *refs):
    blocks, weights = refs[:count], refs[count:]
    if copied:
        *_, source_ref, chosen_ref, part_ref, target_ref, sem = refs
        copy = pltpu.make_async_copy(source_ref, target_ref, sem)
        copy.start()
    else:
        chosen_ref, part_ref = refs[-2:]
    rows = blocks[0].shape[0]
    mine_and_other, start, _, _ = position(units)
    offsets = layout(groups, capacity)
    step = tile(width, (512, 256))
    for g, (expert, members) in enumerate(groups):
        tails = jnp.concatenate([blocks[m][:, width:] for m in members], axis=0)
        slot = slot_row(tails, mine_and_other[expert], experts, rows, capacity)
        here = offsets[g + 1] - offsets[g]
        place = lax.broadcasted_iota(jnp.int32, (here, len(members) * rows), 0)
        pick = jnp.where(place == slot, 1.0, 0.0).astype(BF16)
        for column in range(0, width, step):
            x = jnp.concatenate([blocks[m][:, column:column + step] for m in members], axis=0)
            value = jnp.dot(pick, x, preferred_element_type=F32).astype(BF16)
            chosen_ref[offsets[g]:offsets[g + 1], column:column + step] = value
    for g in range(len(groups)):
        mine = weights[kinds * g:kinds * (g + 1)]
        multiply(chosen_ref, slice(offsets[g], offsets[g + 1]), mine, start if split else None, units, part_ref)
    if copied:
        copy.wait()


def pick_rows(groups, blocks, weights, split, copying, after, width, experts, capacity, units):
    columns = 2 * units if split else weights[0][0].shape[1]
    taken = layout(groups, capacity)[-1]
    flat = [w for expert, _ in groups for w in weights[expert]]
    copied = len(copying)
    kernel = functools.partial(
        pick_kernel, width, experts, capacity, units, groups, len(blocks), len(weights[0]), split, copied
    )
    out = (jax.ShapeDtypeStruct((taken, width), BF16), jax.ShapeDtypeStruct((taken, columns), BF16))
    return pl.pallas_call(
        kernel,
        grid=(1,),
        out_shape=(*out, *[jax.ShapeDtypeStruct(a.shape, a.dtype) for a in copying]),
        in_specs=[whole(x) for x in (*blocks, *flat)] + [ANY] * (len(after) + copied),
        out_specs=(*[whole(o) for o in out], *[ANY] * copied),
        scratch_shapes=[pltpu.SemaphoreType.DMA] * copied,
        compiler_params=params(),
        cost_estimate=cost(),
    )(*blocks, *flat, *after, *copying)


def home_kernel(capacity, units, groups, kinds, split, passed, x_ref, *refs):
    _, _, start, _ = position(units)
    out_ref = refs[-1 - passed]
    offsets = layout(groups, capacity)
    for g in range(len(groups)):
        mine = refs[kinds * g:kinds * (g + 1)]
        multiply(x_ref, slice(offsets[g], offsets[g + 1]), mine, start if split else None, units, out_ref)


def home_rows(groups, chosen, weights, split, passing, after, capacity, units):
    flat = [w for expert, _ in groups for w in weights[expert]]
    out = jax.ShapeDtypeStruct((chosen.shape[0], 2 * units), F32)
    args = (chosen, *flat, *after, *passing)
    result = pl.pallas_call(
        functools.partial(home_kernel, capacity, units, groups, len(weights[0]), split, len(passing)),
        grid=(1,),
        out_shape=(out, *[jax.ShapeDtypeStruct(p.shape, p.dtype) for p in passing]),
        in_specs=[whole(chosen)] + [whole(w) for w in flat] + [ANY] * (len(after) + len(passing)),
        out_specs=(whole(out), *[ANY] * len(passing)),
        input_output_aliases={len(args) - len(passing) + i: 1 + i for i in range(len(passing))},
        compiler_params=params(),
        cost_estimate=cost(),
    )(*args)
    return result[0], result[1:]


def down_kernel(experts, capacity, groups, count, pieces, wide, passed, *refs):
    hiddens, refs = refs[:pieces], refs[pieces:]
    tail_refs, weights = refs[:count], refs[count:]
    scratch = refs[-len(groups):]
    out_ref = refs[-len(groups) - 1 - passed]
    rows = tail_refs[0].shape[0]
    units = hiddens[0].shape[1]
    mine_and_other, _, _, starts = position(units)
    offsets = layout(groups, capacity)
    width = out_ref.shape[1]
    step = tile(width, (256,))
    shares = []
    for g, (expert, members) in enumerate(groups):
        tails = jnp.concatenate([tail_refs[m][...] for m in members], axis=0)
        slot, weight = slot_column(tails, mine_and_other[expert], experts, rows, capacity)
        shares.append(jnp.broadcast_to(weight, (len(members) * rows, step)))
        place = lax.broadcasted_iota(jnp.int32, (len(members) * rows, offsets[g + 1] - offsets[g]), 1)
        spread = jnp.where(place == slot, 1.0, 0.0).astype(BF16)
        for s, ref in enumerate(hiddens):
            value = jnp.dot(spread, ref[offsets[g]:offsets[g + 1], :], preferred_element_type=F32).astype(BF16)
            if wide:
                scratch[g][:, pl.ds(pl.multiple_of(starts[s], LANES), units)] = value
            else:
                scratch[g][s] = value
    for column in range(0, width, step):
        sums = [None] * count
        for g, (expert, members) in enumerate(groups):
            w_ref = weights[g]
            if wide:
                result = jnp.dot(scratch[g][...], w_ref[:, column:column + step], preferred_element_type=F32)
            else:
                result = jnp.zeros((len(members) * rows, step), F32)
                for s in range(pieces):
                    w = w_ref[pl.ds(pl.multiple_of(starts[s], 16), units), column:column + step]
                    result = result + jnp.dot(scratch[g][s], w, preferred_element_type=F32)
            result = result * shares[g]
            for k, m in enumerate(members):
                part = result[k * rows:(k + 1) * rows]
                sums[m] = part if sums[m] is None else sums[m] + part
        for m, value in enumerate(sums):
            out_ref[m * rows:(m + 1) * rows, column:column + step] = value.astype(BF16)


def down_rows(groups, hiddens, blocks, weights, passing, after, width, experts, capacity):
    rows, padded = blocks[0].shape
    units = hiddens[0].shape[1]
    pieces = len(hiddens)
    wide = units % LANES == 0
    tail = pl.BlockSpec((rows, padded - width), lambda i: (0, width // (padded - width)))
    scratch = []
    for _, members in groups:
        spread = (len(members) * rows, pieces * units) if wide else (pieces, len(members) * rows, units)
        scratch.append(pltpu.VMEM(spread, BF16))
    out = jax.ShapeDtypeStruct((len(blocks) * rows, width), BF16)
    args = (*hiddens, *blocks, *[weights[e] for e, _ in groups], *after, *passing)
    result = pl.pallas_call(
        functools.partial(down_kernel, experts, capacity, groups, len(blocks), pieces, wide, len(passing)),
        grid=(1,),
        out_shape=(out, *[jax.ShapeDtypeStruct(p.shape, p.dtype) for p in passing]),
        in_specs=[whole(h) for h in hiddens] + [tail] * len(blocks)
        + [whole(weights[0])] * len(groups) + [ANY] * (len(after) + len(passing)),
        out_specs=(whole(out), *[ANY] * len(passing)),
        input_output_aliases={len(args) - len(passing) + i: 1 + i for i in range(len(passing))},
        scratch_shapes=scratch,
        compiler_params=params(),
        cost_estimate=cost(),
    )(*args)
    return result[0], result[1:]


def add_kernel(count, *refs):
    out_ref = refs[-1]
    total = refs[0][...].astype(F32)
    for ref in refs[1:count]:
        total = total + ref[...].astype(F32)
    out_ref[...] = total.astype(out_ref.dtype)


def added(terms, kind, after):
    out = jax.ShapeDtypeStruct(terms[0].shape, kind)
    return pl.pallas_call(
        functools.partial(add_kernel, len(terms)),
        grid=(1,),
        out_shape=out,
        in_specs=[whole(t) for t in terms] + [ANY] * len(after),
        out_specs=whole(out),
        compiler_params=params(),
        cost_estimate=cost(),
    )(*terms, *after)


def on_device(tokens, expert_ids, route_weights, w_gate, w_up, w_down):
    rows, width = tokens.shape
    top = expert_ids.shape[1]
    ring = lax.axis_size("expert")
    experts = ring * lax.axis_size("dp")
    capacity = min(rows, max(2, 3 * rows * top // (2 * experts)))
    parts = lax.axis_size("tensor")
    units = w_gate.shape[2] // parts
    rank = lax.axis_index("tensor")
    hops = ring // 2

    def over_y(x):
        return lax.ppermute(x, "expert", [(i, i ^ 1) for i in range(ring)])

    def over_z(x):
        return lax.ppermute(x, "expert", [(i, (i + 2) % ring) for i in range(ring)])

    def home_over_both(x, hop):
        return lax.ppermute(x, "expert", [(i, ((i - 2 * hop) % ring) ^ 1) for i in range(ring)])

    def over_core(x):
        return lax.ppermute(x, "dp", [(0, 1), (1, 0)])

    def over_x(x, step):
        return lax.ppermute(x, "tensor", [(i, (i + step) % parts) for i in range(parts)])

    gates = (w_gate[0], over_core(w_gate)[0])
    ups = (w_up[0], over_core(w_up)[0])
    split = parts == 2 and units % LANES == 0
    if split:
        away = home = tuple(zip(gates, ups))
    else:
        def unit_slice(w, offset):
            return lax.dynamic_slice_in_dim(w, (rank + offset) % parts * units, units, 1)

        away, home = [], []
        for gate, up in zip(gates, ups):
            pairs = [(unit_slice(gate, s), unit_slice(up, s)) for s in range(parts)]
            away.append((jnp.concatenate([w for pair in pairs[1:] for w in pair], axis=1),))
            home.append((jnp.concatenate(pairs[0], axis=1),))

    blocks, arrived = {(0, "s"): make_block(tokens, expert_ids, route_weights, experts)}, {}
    blocks[0, "c"] = over_core(blocks[0, "s"])

    def send_on(hop):
        block = blocks[hop, "s"]
        if hop + 1 < hops:
            arrived[hop + 1] = over_z(block)
        blocks[hop, "b"] = over_y(block)

    both = ((0, (0, 1)), (1, (0, 1)))
    one = ((0, (0,)), (1, (0,)))
    plan = [([(0, "s")], ((0, (0,)),)), ([(0, "s"), (0, "b"), (1, "s")], ((1, (0, 1, 2)), (0, (1, 2))))]
    plan += [([(1, "b")], one)] + [([(hop, "b"), (hop, "s")], both) for hop in range(2, hops - 1)]
    plan += [([(hops - 1, "b")], one), ([(hops - 1, "s")], one)]
    count = len(plan)
    straight = ()
    chosen, parts_in, totals, hidden, returned, carried, gathered = {}, {}, {}, {}, {}, {}, []
    downs = [w_down[0]]
    order = []

    def passing(hop):
        return [arrived[hop]] if hop in arrived else []

    def take_on(hop, passed):
        if passed:
            blocks[hop, "s"] = passed[0]
            send_on(hop)

    def pick(i):
        keys, groups = plan[i]
        mine = [blocks[k] for k in keys]
        chosen[i], part = pick_rows(
            groups, mine, away, split, [], order, width, experts, capacity, units
        )
        if i == 1:
            later, _ = lax.optimization_barrier((w_down, part))
            downs.append(over_core(later)[0])
        parts_in[i] = [over_x(part[:, 2 * units * (s - 1):2 * units * s], s) for s in range(1, parts)]
        order[:] = [part]

    def home_product(i, hop=None):
        totals[i], passed = home_rows(
            plan[i][1], chosen[i], home, split, passing(hop), order, capacity, units
        )
        order[:] = [totals[i]]
        take_on(hop, passed)

    def activate(i):
        total = totals[i]
        for piece in parts_in[i]:
            total = total + piece.astype(F32)
        value = (jax.nn.silu(total[:, :units]) * total[:, units:]).astype(BF16)
        hidden[i] = [value] + [over_x(value, s) for s in range(1, parts)]
        order.append(value)

    def down_product(i, hop=None):
        keys, groups = plan[i]
        mine = [blocks[k] for k in keys]
        term, passed = down_rows(
            groups, hidden[i], mine, downs, passing(hop), order, width, experts, capacity
        )
        order[:] = [term]
        take_on(hop, passed)
        for k, (at, kind) in enumerate(keys):
            piece = term[k * rows:(k + 1) * rows]
            if kind == "b" and at in straight:
                gathered.append(home_over_both(piece, at))
            elif kind == "b":
                returned[at, "b"] = over_y(piece)
            elif kind == "c":
                gathered.append(over_core(piece))
            elif at == 0:
                gathered.append(piece)
            else:
                returned[at, "s"] = piece

    def add_hop(hop):
        if hop == 0:
            gathered[:] = [added(gathered + [returned[hop, "b"]], F32, order)]
            order[:] = [gathered[0]]
        else:
            terms = [returned[hop, "s"]] + ([returned[hop, "b"]] if hop not in straight else [])
            terms += [carried[hop]] if hop in carried else []
            total = added(terms, BF16, order)
            order[:] = [total]
            carried[hop + 1] = over_z(total)

    def await_beside(hop):
        if (hop, "b") in blocks:
            order.append(blocks[hop, "b"])

    send_on(0)
    if hops == 4:
        pick(0)
        order.append(blocks[0, "b"])
        home_product(0, 1)
        activate(0)
        pick(1)
        order.extend(downs[1:])
        home_product(1, 2)
        pick(2)
        home_product(2, 3)
        down_product(0)
        activate(2)
        pick(3)
        activate(1)
        down_product(1)
        down_product(2)
        pick(4)
        home_product(3)
        home_product(4)
        activate(3)
        pick(5)
        home_product(5)
        order.append(blocks[2, "b"])
        add_hop(0)
        down_product(3)
        add_hop(1)
        order.append(blocks[2, "b"])
        activate(4)
        down_product(4)
        activate(5)
        add_hop(2)
        down_product(5)
        add_hop(3)
    else:
        for i in range(count):
            pick(i)
            home_product(i, i + 1)
            if i > 0:
                activate(i - 1)
                down_product(i - 1)
        activate(count - 1)
        down_product(count - 1)
        for hop in range(hops):
            add_hop(hop)
    return sum(x.astype(F32) for x in gathered + [carried[hops]]).astype(BF16)


def solution(mesh):
    placed = (
        P(("group", "expert", "dp"), "tensor"),
        P(("group", "expert", "dp"), None),
        P(("group", "expert", "dp"), None),
        P(("expert", "dp"), "tensor", None),
        P(("expert", "dp"), "tensor", None),
        P(("expert", "dp"), None, "tensor"),
    )
    return jax.shard_map(
        on_device,
        mesh=mesh,
        in_specs=placed,
        out_specs=P(("group", "expert", "dp"), "tensor"),
        check_vma=False,
    )
```

```python
import functools

import jax
import jax.numpy as jnp
from jax import lax
from jax.experimental import pallas as pl
from jax.experimental.pallas import tpu as pltpu
from jax.sharding import PartitionSpec as P

F32 = jnp.float32
BF16 = jnp.bfloat16
LANES = 128
VMEM = 10 * 1024 * 1024
ANY = pl.BlockSpec(memory_space=pl.ANY)
HBM = pl.BlockSpec(memory_space=pltpu.HBM)


def tile(extent, choices):
    for size in choices:
        if extent % size == 0:
            return size
    return extent


def whole(x):
    return pl.BlockSpec(x.shape, lambda i: (0,) * len(x.shape))


def params():
    return pltpu.CompilerParams(vmem_limit_bytes=VMEM)


def cost():
    return pl.CostEstimate(flops=1, bytes_accessed=1, transcendentals=0)


def block_kernel(experts, tokens_ref, routes_ref, out_ref, sem):
    rows, width = tokens_ref.shape
    copy = pltpu.make_async_copy(tokens_ref, out_ref.at[:, :width], sem)
    copy.start()
    routes = routes_ref[...].T
    top = routes.shape[1] // 2
    column = lax.broadcasted_iota(jnp.int32, (rows, out_ref.shape[1] - width), 1)
    expert = jnp.where(column < experts, column, column - experts).astype(F32)
    value = jnp.zeros(column.shape, F32)
    for k in range(top):
        value = value + jnp.where(expert == routes[:, k:k + 1], routes[:, top + k:top + k + 1], 0.0)
    high = value.astype(BF16).astype(F32)
    out_ref[:, width:] = jnp.where(column < experts, high, value - high).astype(BF16)
    copy.wait()


def make_block(tokens, expert_ids, route_weights, experts):
    rows, width = tokens.shape
    padded = width + 2 * experts + (-(2 * experts)) % LANES
    routes = jnp.concatenate([expert_ids.T.astype(F32), route_weights.T], axis=0)
    return pl.pallas_call(
        functools.partial(block_kernel, experts),
        grid=(1,),
        out_shape=jax.ShapeDtypeStruct((rows, padded), BF16),
        in_specs=[HBM, whole(routes)],
        out_specs=pl.BlockSpec((rows, padded), lambda i: (0, 0)),
        scratch_shapes=[pltpu.SemaphoreType.DMA],
        compiler_params=params(),
        cost_estimate=cost(),
    )(tokens, routes)


def slot_row(tails, me, experts, rows, capacity):
    total = tails.shape[0]
    column = lax.broadcasted_iota(jnp.int32, (8, tails.shape[1]), 1)
    mark = jnp.where((column == me) | (column == experts + me), 1.0, 0.0).astype(BF16)
    weight = lax.dot_general(mark, tails, (((1,), (1,)), ((), ())), preferred_element_type=F32)
    live = weight > 0.0
    number = lax.broadcasted_iota(jnp.int32, (8, total), 1) // rows
    above = lax.broadcasted_iota(jnp.int32, (total, total), 0)
    own = lax.broadcasted_iota(jnp.int32, (total, total), 1)
    ahead = jnp.where((above < own) & (above >= (number * rows)[0:1]), 1.0, 0.0).astype(BF16)
    before = jnp.dot(jnp.where(live, 1.0, 0.0).astype(BF16), ahead, preferred_element_type=F32)
    return jnp.where(live, before.astype(jnp.int32) + number * capacity, -1)[0:1]


def slot_column(tails, me, experts, rows, capacity):
    total = tails.shape[0]
    column = lax.broadcasted_iota(jnp.int32, tails.shape, 1)
    mine = (column == me) | (column == experts + me)
    weight = jnp.sum(jnp.where(mine, tails.astype(F32), 0.0), axis=1, keepdims=True)
    live = weight > 0.0
    number = lax.broadcasted_iota(jnp.int32, (total, 1), 0) // rows
    own = lax.broadcasted_iota(jnp.int32, (total, total), 0)
    above = lax.broadcasted_iota(jnp.int32, (total, total), 1)
    ahead = jnp.where((above < own) & (above >= number * rows), 1.0, 0.0).astype(BF16)
    flags = jnp.broadcast_to(jnp.where(live, 1.0, 0.0), (total, LANES)).astype(BF16)
    before = jnp.dot(ahead, flags, preferred_element_type=F32)[:, 0:1]
    return jnp.where(live, before.astype(jnp.int32) + number * capacity, -1), weight


def layout(groups, capacity):
    offsets, total = [], 0
    for _, members in groups:
        offsets.append(total)
        total += -(-len(members) * capacity // 16) * 16
    return offsets + [total]


def multiply(x_ref, rows, weights, start, units, out_ref):
    def store(x, w, column, count):
        out_ref[rows, column:column + count] = jnp.dot(x, w, preferred_element_type=F32).astype(out_ref.dtype)

    x = x_ref[rows, :]
    if start is None:
        w_ref = weights[0]
        step = tile(w_ref.shape[1], (256, 384))
        for column in range(0, w_ref.shape[1], step):
            store(x, w_ref[:, column:column + step], column, step)
        return
    full = units // 256 * 256
    for i, ref in enumerate(weights):
        for column in range(0, full, 256):
            store(x, ref[:, pl.ds(pl.multiple_of(start + column, LANES), 256)], i * units + column, 256)
    if full < units:
        rest = pl.ds(pl.multiple_of(start + full, LANES), units - full)
        w = jnp.concatenate([ref[:, rest] for ref in weights], axis=1)
        y = jnp.dot(x, w, preferred_element_type=F32).astype(out_ref.dtype)
        out_ref[rows, full:units] = y[:, :units - full]
        out_ref[rows, units + full:] = y[:, units - full:]


def position(units):
    core, rank, parts = lax.axis_index("dp"), lax.axis_index("tensor"), lax.axis_size("tensor")
    first = lax.axis_index("expert") * 2
    places = [(rank + parts - s) % parts * units for s in range(parts)]
    return (first + core, first + 1 - core), (rank + 1) % parts * units, rank * units, places


def pick_kernel(width, experts, capacity, units, groups, count, kinds, split, copied, *refs):
    blocks, weights = refs[:count], refs[count:]
    if copied:
        *_, source_ref, chosen_ref, part_ref, target_ref, sem = refs
        copy = pltpu.make_async_copy(source_ref, target_ref, sem)
        copy.start()
    else:
        chosen_ref, part_ref = refs[-2:]
    rows = blocks[0].shape[0]
    mine_and_other, start, _, _ = position(units)
    offsets = layout(groups, capacity)
    step = tile(width, (512, 256))
    for g, (expert, members) in enumerate(groups):
        tails = jnp.concatenate([blocks[m][:, width:] for m in members], axis=0)
        slot = slot_row(tails, mine_and_other[expert], experts, rows, capacity)
        here = offsets[g + 1] - offsets[g]
        place = lax.broadcasted_iota(jnp.int32, (here, len(members) * rows), 0)
        pick = jnp.where(place == slot, 1.0, 0.0).astype(BF16)
        for column in range(0, width, step):
            x = jnp.concatenate([blocks[m][:, column:column + step] for m in members], axis=0)
            value = jnp.dot(pick, x, preferred_element_type=F32).astype(BF16)
            chosen_ref[offsets[g]:offsets[g + 1], column:column + step] = value
    for g in range(len(groups)):
        mine = weights[kinds * g:kinds * (g + 1)]
        multiply(chosen_ref, slice(offsets[g], offsets[g + 1]), mine, start if split else None, units, part_ref)
    if copied:
        copy.wait()


def pick_rows(groups, blocks, weights, split, copying, after, width, experts, capacity, units):
    columns = 2 * units if split else weights[0][0].shape[1]
    taken = layout(groups, capacity)[-1]
    flat = [w for expert, _ in groups for w in weights[expert]]
    copied = len(copying)
    kernel = functools.partial(
        pick_kernel, width, experts, capacity, units, groups, len(blocks), len(weights[0]), split, copied
    )
    out = (jax.ShapeDtypeStruct((taken, width), BF16), jax.ShapeDtypeStruct((taken, columns), BF16))
    return pl.pallas_call(
        kernel,
        grid=(1,),
        out_shape=(*out, *[jax.ShapeDtypeStruct(a.shape, a.dtype) for a in copying]),
        in_specs=[whole(x) for x in (*blocks, *flat)] + [ANY] * (len(after) + copied),
        out_specs=(*[whole(o) for o in out], *[ANY] * copied),
        scratch_shapes=[pltpu.SemaphoreType.DMA] * copied,
        compiler_params=params(),
        cost_estimate=cost(),
    )(*blocks, *flat, *after, *copying)


def home_kernel(capacity, units, groups, kinds, split, passed, x_ref, *refs):
    _, _, start, _ = position(units)
    out_ref = refs[-1 - passed]
    offsets = layout(groups, capacity)
    for g in range(len(groups)):
        mine = refs[kinds * g:kinds * (g + 1)]
        multiply(x_ref, slice(offsets[g], offsets[g + 1]), mine, start if split else None, units, out_ref)


def home_rows(groups, chosen, weights, split, passing, after, capacity, units):
    flat = [w for expert, _ in groups for w in weights[expert]]
    out = jax.ShapeDtypeStruct((chosen.shape[0], 2 * units), F32)
    args = (chosen, *flat, *after, *passing)
    result = pl.pallas_call(
        functools.partial(home_kernel, capacity, units, groups, len(weights[0]), split, len(passing)),
        grid=(1,),
        out_shape=(out, *[jax.ShapeDtypeStruct(p.shape, p.dtype) for p in passing]),
        in_specs=[whole(chosen)] + [whole(w) for w in flat] + [ANY] * (len(after) + len(passing)),
        out_specs=(whole(out), *[ANY] * len(passing)),
        input_output_aliases={len(args) - len(passing) + i: 1 + i for i in range(len(passing))},
        compiler_params=params(),
        cost_estimate=cost(),
    )(*args)
    return result[0], result[1:]


def down_kernel(experts, capacity, groups, count, pieces, wide, passed, *refs):
    hiddens, refs = refs[:pieces], refs[pieces:]
    tail_refs, weights = refs[:count], refs[count:]
    scratch = refs[-len(groups):]
    out_ref = refs[-len(groups) - 1 - passed]
    rows = tail_refs[0].shape[0]
    units = hiddens[0].shape[1]
    mine_and_other, _, _, starts = position(units)
    offsets = layout(groups, capacity)
    width = out_ref.shape[1]
    step = tile(width, (256,))
    shares = []
    for g, (expert, members) in enumerate(groups):
        tails = jnp.concatenate([tail_refs[m][...] for m in members], axis=0)
        slot, weight = slot_column(tails, mine_and_other[expert], experts, rows, capacity)
        shares.append(jnp.broadcast_to(weight, (len(members) * rows, step)))
        place = lax.broadcasted_iota(jnp.int32, (len(members) * rows, offsets[g + 1] - offsets[g]), 1)
        spread = jnp.where(place == slot, 1.0, 0.0).astype(BF16)
        for s, ref in enumerate(hiddens):
            value = jnp.dot(spread, ref[offsets[g]:offsets[g + 1], :], preferred_element_type=F32).astype(BF16)
            if wide:
                scratch[g][:, pl.ds(pl.multiple_of(starts[s], LANES), units)] = value
            else:
                scratch[g][s] = value
    for column in range(0, width, step):
        sums = [None] * count
        for g, (expert, members) in enumerate(groups):
            w_ref = weights[g]
            if wide:
                result = jnp.dot(scratch[g][...], w_ref[:, column:column + step], preferred_element_type=F32)
            else:
                result = jnp.zeros((len(members) * rows, step), F32)
                for s in range(pieces):
                    w = w_ref[pl.ds(pl.multiple_of(starts[s], 16), units), column:column + step]
                    result = result + jnp.dot(scratch[g][s], w, preferred_element_type=F32)
            result = result * shares[g]
            for k, m in enumerate(members):
                part = result[k * rows:(k + 1) * rows]
                sums[m] = part if sums[m] is None else sums[m] + part
        for m, value in enumerate(sums):
            out_ref[m * rows:(m + 1) * rows, column:column + step] = value.astype(BF16)


def down_rows(groups, hiddens, blocks, weights, passing, after, width, experts, capacity):
    rows, padded = blocks[0].shape
    units = hiddens[0].shape[1]
    pieces = len(hiddens)
    wide = units % LANES == 0
    tail = pl.BlockSpec((rows, padded - width), lambda i: (0, width // (padded - width)))
    scratch = []
    for _, members in groups:
        spread = (len(members) * rows, pieces * units) if wide else (pieces, len(members) * rows, units)
        scratch.append(pltpu.VMEM(spread, BF16))
    out = jax.ShapeDtypeStruct((len(blocks) * rows, width), BF16)
    args = (*hiddens, *blocks, *[weights[e] for e, _ in groups], *after, *passing)
    result = pl.pallas_call(
        functools.partial(down_kernel, experts, capacity, groups, len(blocks), pieces, wide, len(passing)),
        grid=(1,),
        out_shape=(out, *[jax.ShapeDtypeStruct(p.shape, p.dtype) for p in passing]),
        in_specs=[whole(h) for h in hiddens] + [tail] * len(blocks)
        + [whole(weights[0])] * len(groups) + [ANY] * (len(after) + len(passing)),
        out_specs=(whole(out), *[ANY] * len(passing)),
        input_output_aliases={len(args) - len(passing) + i: 1 + i for i in range(len(passing))},
        scratch_shapes=scratch,
        compiler_params=params(),
        cost_estimate=cost(),
    )(*args)
    return result[0], result[1:]


def add_kernel(count, *refs):
    out_ref = refs[-1]
    total = refs[0][...].astype(F32)
    for ref in refs[1:count]:
        total = total + ref[...].astype(F32)
    out_ref[...] = total.astype(out_ref.dtype)


def added(terms, kind, after):
    out = jax.ShapeDtypeStruct(terms[0].shape, kind)
    return pl.pallas_call(
        functools.partial(add_kernel, len(terms)),
        grid=(1,),
        out_shape=out,
        in_specs=[whole(t) for t in terms] + [ANY] * len(after),
        out_specs=whole(out),
        compiler_params=params(),
        cost_estimate=cost(),
    )(*terms, *after)


def on_device(tokens, expert_ids, route_weights, w_gate, w_up, w_down):
    rows, width = tokens.shape
    top = expert_ids.shape[1]
    ring = lax.axis_size("expert")
    experts = ring * lax.axis_size("dp")
    capacity = min(rows, max(2, 3 * rows * top // (2 * experts)))
    parts = lax.axis_size("tensor")
    units = w_gate.shape[2] // parts
    rank = lax.axis_index("tensor")
    hops = ring // 2

    def over_y(x):
        return lax.ppermute(x, "expert", [(i, i ^ 1) for i in range(ring)])

    def over_z(x):
        return lax.ppermute(x, "expert", [(i, (i + 2) % ring) for i in range(ring)])

    def home_over_both(x, hop):
        return lax.ppermute(x, "expert", [(i, ((i - 2 * hop) % ring) ^ 1) for i in range(ring)])

    def over_core(x):
        return lax.ppermute(x, "dp", [(0, 1), (1, 0)])

    def over_x(x, step):
        return lax.ppermute(x, "tensor", [(i, (i + step) % parts) for i in range(parts)])

    gates = (w_gate[0], over_core(w_gate)[0])
    ups = (w_up[0], over_core(w_up)[0])
    split = parts == 2 and units % LANES == 0
    if split:
        away = home = tuple(zip(gates, ups))
    else:
        def unit_slice(w, offset):
            return lax.dynamic_slice_in_dim(w, (rank + offset) % parts * units, units, 1)

        away, home = [], []
        for gate, up in zip(gates, ups):
            pairs = [(unit_slice(gate, s), unit_slice(up, s)) for s in range(parts)]
            away.append((jnp.concatenate([w for pair in pairs[1:] for w in pair], axis=1),))
            home.append((jnp.concatenate(pairs[0], axis=1),))

    blocks, arrived = {(0, "s"): make_block(tokens, expert_ids, route_weights, experts)}, {}
    blocks[0, "c"] = over_core(blocks[0, "s"])

    def send_on(hop):
        block = blocks[hop, "s"]
        if hop + 1 < hops:
            arrived[hop + 1] = over_z(block)
        blocks[hop, "b"] = over_y(block)

    both = ((0, (0, 1)), (1, (0, 1)))
    one = ((0, (0,)), (1, (0,)))
    plan = [([(0, "s")], ((0, (0,)),)), ([(0, "s"), (0, "b"), (1, "s")], ((1, (0, 1, 2)), (0, (1, 2))))]
    plan += [([(1, "b")], one)] + [([(hop, "b"), (hop, "s")], both) for hop in range(2, hops - 1)]
    plan += [([(hops - 1, "b")], one), ([(hops - 1, "s")], one)]
    count = len(plan)
    straight = ()
    chosen, parts_in, totals, hidden, returned, carried, gathered = {}, {}, {}, {}, {}, {}, []
    downs = [w_down[0]]
    order = []

    def passing(hop):
        return [arrived[hop]] if hop in arrived else []

    def take_on(hop, passed):
        if passed:
            blocks[hop, "s"] = passed[0]
            send_on(hop)

    def pick(i):
        keys, groups = plan[i]
        mine = [blocks[k] for k in keys]
        chosen[i], part = pick_rows(
            groups, mine, away, split, [], order, width, experts, capacity, units
        )
        if i == 1:
            later, _ = lax.optimization_barrier((w_down, part))
            downs.append(over_core(later)[0])
        cut = units if i == 1 else 2 * units
        parts_in[i] = []
        for step in range(1, parts):
            columns = range(2 * units * (step - 1), 2 * units * step, cut)
            parts_in[i].append([over_x(part[:, c:c + cut], step) for c in columns])
        order[:] = [part]

    def home_product(i, hop=None):
        totals[i], passed = home_rows(
            plan[i][1], chosen[i], home, split, passing(hop), order, capacity, units
        )
        order[:] = [totals[i]]
        take_on(hop, passed)

    def activate(i):
        total = totals[i]
        for pieces in parts_in[i]:
            total = total + jnp.concatenate(pieces, axis=1).astype(F32)
        value = (jax.nn.silu(total[:, :units]) * total[:, units:]).astype(BF16)
        hidden[i] = [value] + [over_x(value, s) for s in range(1, parts)]
        order.append(value)

    def down_product(i, hop=None):
        keys, groups = plan[i]
        mine = [blocks[k] for k in keys]
        term, passed = down_rows(
            groups, hidden[i], mine, downs, passing(hop), order, width, experts, capacity
        )
        order[:] = [term]
        take_on(hop, passed)
        for k, (at, kind) in enumerate(keys):
            piece = term[k * rows:(k + 1) * rows]
            if kind == "b" and at in straight:
                gathered.append(home_over_both(piece, at))
            elif kind == "b":
                returned[at, "b"] = over_y(piece)
            elif kind == "c":
                gathered.append(over_core(piece))
            elif at == 0:
                gathered.append(piece)
            else:
                returned[at, "s"] = piece

    def add_hop(hop):
        if hop == 0:
            gathered[:] = [added(gathered + [returned[hop, "b"]], F32, order)]
            order[:] = [gathered[0]]
        else:
            terms = [returned[hop, "s"]] + ([returned[hop, "b"]] if hop not in straight else [])
            terms += [carried[hop]] if hop in carried else []
            total = added(terms, BF16, order)
            order[:] = [total]
            carried[hop + 1] = over_z(total)

    def await_beside(hop):
        if (hop, "b") in blocks:
            order.append(blocks[hop, "b"])

    send_on(0)
    if hops == 4:
        pick(0)
        order.append(blocks[0, "b"])
        home_product(0, 1)
        activate(0)
        pick(1)
        order.extend(downs[1:])
        pick(2)
        home_product(1, 2)
        home_product(2, 3)
        down_product(0)
        pick(3)
        activate(2)
        activate(1)
        down_product(1)
        down_product(2)
        pick(4)
        home_product(3)
        home_product(4)
        activate(3)
        pick(5)
        home_product(5)
        order.append(blocks[2, "b"])
        add_hop(0)
        down_product(3)
        add_hop(1)
        order.append(blocks[2, "b"])
        activate(4)
        down_product(4)
        activate(5)
        add_hop(2)
        down_product(5)
        add_hop(3)
    else:
        for i in range(count):
            pick(i)
            home_product(i, i + 1)
            if i > 0:
                activate(i - 1)
                down_product(i - 1)
        activate(count - 1)
        down_product(count - 1)
        for hop in range(hops):
            add_hop(hop)
    return sum(x.astype(F32) for x in gathered + [carried[hops]]).astype(BF16)


def solution(mesh):
    placed = (
        P(("group", "expert", "dp"), "tensor"),
        P(("group", "expert", "dp"), None),
        P(("group", "expert", "dp"), None),
        P(("expert", "dp"), "tensor", None),
        P(("expert", "dp"), "tensor", None),
        P(("expert", "dp"), None, "tensor"),
    )
    return jax.shard_map(
        on_device,
        mesh=mesh,
        in_specs=placed,
        out_specs=P(("group", "expert", "dp"), "tensor"),
        check_vma=False,
    )
```

```python
import functools

import jax
import jax.numpy as jnp
from jax import lax
from jax.experimental import pallas as pl
from jax.experimental.pallas import tpu as pltpu
from jax.sharding import PartitionSpec as P

F32 = jnp.float32
BF16 = jnp.bfloat16
LANES = 128
VMEM = 10 * 1024 * 1024
ANY = pl.BlockSpec(memory_space=pl.ANY)
HBM = pl.BlockSpec(memory_space=pltpu.HBM)


def tile(extent, choices):
    for size in choices:
        if extent % size == 0:
            return size
    return extent


def whole(x):
    return pl.BlockSpec(x.shape, lambda i: (0,) * len(x.shape))


def params():
    return pltpu.CompilerParams(vmem_limit_bytes=VMEM)


def cost():
    return pl.CostEstimate(flops=1, bytes_accessed=1, transcendentals=0)


def block_kernel(experts, tokens_ref, routes_ref, out_ref, sem):
    rows, width = tokens_ref.shape
    copy = pltpu.make_async_copy(tokens_ref, out_ref.at[:, :width], sem)
    copy.start()
    routes = routes_ref[...].T
    top = routes.shape[1] // 2
    column = lax.broadcasted_iota(jnp.int32, (rows, out_ref.shape[1] - width), 1)
    expert = jnp.where(column < experts, column, column - experts).astype(F32)
    value = jnp.zeros(column.shape, F32)
    for k in range(top):
        value = value + jnp.where(expert == routes[:, k:k + 1], routes[:, top + k:top + k + 1], 0.0)
    high = value.astype(BF16).astype(F32)
    out_ref[:, width:] = jnp.where(column < experts, high, value - high).astype(BF16)
    copy.wait()


def make_block(tokens, expert_ids, route_weights, experts):
    rows, width = tokens.shape
    padded = width + 2 * experts + (-(2 * experts)) % LANES
    routes = jnp.concatenate([expert_ids.T.astype(F32), route_weights.T], axis=0)
    return pl.pallas_call(
        functools.partial(block_kernel, experts),
        grid=(1,),
        out_shape=jax.ShapeDtypeStruct((rows, padded), BF16),
        in_specs=[HBM, whole(routes)],
        out_specs=pl.BlockSpec((rows, padded), lambda i: (0, 0)),
        scratch_shapes=[pltpu.SemaphoreType.DMA],
        compiler_params=params(),
        cost_estimate=cost(),
    )(tokens, routes)


def slot_row(tails, me, experts, rows, capacity):
    total = tails.shape[0]
    column = lax.broadcasted_iota(jnp.int32, (8, tails.shape[1]), 1)
    mark = jnp.where((column == me) | (column == experts + me), 1.0, 0.0).astype(BF16)
    weight = lax.dot_general(mark, tails, (((1,), (1,)), ((), ())), preferred_element_type=F32)
    live = weight > 0.0
    number = lax.broadcasted_iota(jnp.int32, (8, total), 1) // rows
    above = lax.broadcasted_iota(jnp.int32, (total, total), 0)
    own = lax.broadcasted_iota(jnp.int32, (total, total), 1)
    ahead = jnp.where((above < own) & (above >= (number * rows)[0:1]), 1.0, 0.0).astype(BF16)
    before = jnp.dot(jnp.where(live, 1.0, 0.0).astype(BF16), ahead, preferred_element_type=F32)
    return jnp.where(live, before.astype(jnp.int32) + number * capacity, -1)[0:1]


def slot_column(tails, me, experts, rows, capacity):
    total = tails.shape[0]
    column = lax.broadcasted_iota(jnp.int32, tails.shape, 1)
    mine = (column == me) | (column == experts + me)
    weight = jnp.sum(jnp.where(mine, tails.astype(F32), 0.0), axis=1, keepdims=True)
    live = weight > 0.0
    number = lax.broadcasted_iota(jnp.int32, (total, 1), 0) // rows
    own = lax.broadcasted_iota(jnp.int32, (total, total), 0)
    above = lax.broadcasted_iota(jnp.int32, (total, total), 1)
    ahead = jnp.where((above < own) & (above >= number * rows), 1.0, 0.0).astype(BF16)
    flags = jnp.broadcast_to(jnp.where(live, 1.0, 0.0), (total, LANES)).astype(BF16)
    before = jnp.dot(ahead, flags, preferred_element_type=F32)[:, 0:1]
    return jnp.where(live, before.astype(jnp.int32) + number * capacity, -1), weight


def tight(groups, capacity):
    return len(groups) == 2 and capacity % 8 == 0 and all(len(members) == 1 for _, members in groups)


def layout(groups, capacity):
    if tight(groups, capacity):
        return [0, capacity, -(-2 * capacity // 16) * 16]
    offsets = [0]
    for _, members in groups:
        offsets.append(offsets[-1] + -(-len(members) * capacity // 16) * 16)
    return offsets


def multiply(x_ref, rows, weights, start, units, out_ref):
    def store(x, w, column, count):
        out_ref[rows, column:column + count] = jnp.dot(x, w, preferred_element_type=F32).astype(out_ref.dtype)

    x = x_ref[rows, :]
    if start is None:
        w_ref = weights[0]
        step = tile(w_ref.shape[1], (256, 384))
        for column in range(0, w_ref.shape[1], step):
            store(x, w_ref[:, column:column + step], column, step)
        return
    full = units // 256 * 256
    for i, ref in enumerate(weights):
        for column in range(0, full, 256):
            store(x, ref[:, pl.ds(pl.multiple_of(start + column, LANES), 256)], i * units + column, 256)
    if full < units:
        rest = pl.ds(pl.multiple_of(start + full, LANES), units - full)
        w = jnp.concatenate([ref[:, rest] for ref in weights], axis=1)
        y = jnp.dot(x, w, preferred_element_type=F32).astype(out_ref.dtype)
        out_ref[rows, full:units] = y[:, :units - full]
        out_ref[rows, units + full:] = y[:, units - full:]


def multiply_both(x_ref, bound, first, second, start, units, out_ref):
    x = x_ref[...]
    for (column, count, v), (_, _, w) in zip(tiles(first, start, units), tiles(second, start, units)):
        upper = lax.broadcasted_iota(jnp.int32, (x.shape[0], count), 0) < bound
        a = jnp.dot(x, v(), preferred_element_type=F32)
        b = jnp.dot(x, w(), preferred_element_type=F32)
        out_ref[:, column:column + count] = jnp.where(upper, a, b).astype(out_ref.dtype)


def tiles(weights, start, units):
    if start is None:
        ref = weights[0]
        step = tile(ref.shape[1], (256, 384))
        return [(c, step, lambda c=c: ref[:, c:c + step]) for c in range(0, ref.shape[1], step)]
    parts = []
    step = tile(units, (384, 256, LANES))
    for i, ref in enumerate(weights):
        for c in range(0, units, step):
            span = pl.ds(pl.multiple_of(start + c, LANES), step)
            parts.append((i * units + c, step, lambda ref=ref, span=span: ref[:, span]))
    return parts


def position(units):
    core, rank, parts = lax.axis_index("dp"), lax.axis_index("tensor"), lax.axis_size("tensor")
    first = lax.axis_index("expert") * 2
    places = [(rank + parts - s) % parts * units for s in range(parts)]
    return (first + core, first + 1 - core), (rank + 1) % parts * units, rank * units, places


def pick_kernel(width, experts, capacity, units, groups, count, kinds, split, copied, *refs):
    blocks, weights = refs[:count], refs[count:]
    if copied:
        *_, source_ref, chosen_ref, part_ref, target_ref, sem = refs
        copy = pltpu.make_async_copy(source_ref, target_ref, sem)
        copy.start()
    else:
        chosen_ref, part_ref = refs[-2:]
    rows = blocks[0].shape[0]
    mine_and_other, start, _, _ = position(units)
    offsets = layout(groups, capacity)
    step = tile(width, (512, 256))
    if tight(groups, capacity):
        taken = offsets[-1]
        place = lax.broadcasted_iota(jnp.int32, (taken, rows), 0)
        pick = jnp.zeros((taken, rows), F32)
        for g, (expert, _) in enumerate(groups):
            slot = slot_row(blocks[0][:, width:], mine_and_other[expert], experts, rows, capacity)
            pick = pick + jnp.where((place == slot + offsets[g]) & (slot >= 0), 1.0, 0.0)
        pick = pick.astype(BF16)
        for column in range(0, width, step):
            value = jnp.dot(pick, blocks[0][:, column:column + step], preferred_element_type=F32)
            chosen_ref[:, column:column + step] = value.astype(BF16)
        first, second = weights[:kinds], weights[kinds:2 * kinds]
        multiply_both(chosen_ref, offsets[1], first, second, start if split else None, units, part_ref)
        return
    for g, (expert, members) in enumerate(groups):
        tails = jnp.concatenate([blocks[m][:, width:] for m in members], axis=0)
        slot = slot_row(tails, mine_and_other[expert], experts, rows, capacity)
        here = offsets[g + 1] - offsets[g]
        place = lax.broadcasted_iota(jnp.int32, (here, len(members) * rows), 0)
        pick = jnp.where(place == slot, 1.0, 0.0).astype(BF16)
        for column in range(0, width, step):
            x = jnp.concatenate([blocks[m][:, column:column + step] for m in members], axis=0)
            value = jnp.dot(pick, x, preferred_element_type=F32).astype(BF16)
            chosen_ref[offsets[g]:offsets[g + 1], column:column + step] = value
    for g in range(len(groups)):
        mine = weights[kinds * g:kinds * (g + 1)]
        multiply(chosen_ref, slice(offsets[g], offsets[g + 1]), mine, start if split else None, units, part_ref)
    if copied:
        copy.wait()


def pick_rows(groups, blocks, weights, split, copying, after, width, experts, capacity, units):
    columns = 2 * units if split else weights[0][0].shape[1]
    taken = layout(groups, capacity)[-1]
    flat = [w for expert, _ in groups for w in weights[expert]]
    copied = len(copying)
    kernel = functools.partial(
        pick_kernel, width, experts, capacity, units, groups, len(blocks), len(weights[0]), split, copied
    )
    out = (jax.ShapeDtypeStruct((taken, width), BF16), jax.ShapeDtypeStruct((taken, columns), BF16))
    return pl.pallas_call(
        kernel,
        grid=(1,),
        out_shape=(*out, *[jax.ShapeDtypeStruct(a.shape, a.dtype) for a in copying]),
        in_specs=[whole(x) for x in (*blocks, *flat)] + [ANY] * (len(after) + copied),
        out_specs=(*[whole(o) for o in out], *[ANY] * copied),
        scratch_shapes=[pltpu.SemaphoreType.DMA] * copied,
        compiler_params=params(),
        cost_estimate=cost(),
    )(*blocks, *flat, *after, *copying)


def home_kernel(capacity, units, groups, kinds, split, passed, x_ref, *refs):
    _, _, start, _ = position(units)
    out_ref = refs[-1 - passed]
    offsets = layout(groups, capacity)
    if tight(groups, capacity):
        first, second = refs[:kinds], refs[kinds:2 * kinds]
        multiply_both(x_ref, offsets[1], first, second, start if split else None, units, out_ref)
        return
    for g in range(len(groups)):
        mine = refs[kinds * g:kinds * (g + 1)]
        multiply(x_ref, slice(offsets[g], offsets[g + 1]), mine, start if split else None, units, out_ref)


def home_rows(groups, chosen, weights, split, passing, after, capacity, units):
    flat = [w for expert, _ in groups for w in weights[expert]]
    out = jax.ShapeDtypeStruct((chosen.shape[0], 2 * units), F32)
    args = (chosen, *flat, *after, *passing)
    result = pl.pallas_call(
        functools.partial(home_kernel, capacity, units, groups, len(weights[0]), split, len(passing)),
        grid=(1,),
        out_shape=(out, *[jax.ShapeDtypeStruct(p.shape, p.dtype) for p in passing]),
        in_specs=[whole(chosen)] + [whole(w) for w in flat] + [ANY] * (len(after) + len(passing)),
        out_specs=(whole(out), *[ANY] * len(passing)),
        input_output_aliases={len(args) - len(passing) + i: 1 + i for i in range(len(passing))},
        compiler_params=params(),
        cost_estimate=cost(),
    )(*args)
    return result[0], result[1:]


def down_kernel(experts, capacity, groups, count, pieces, wide, passed, *refs):
    hiddens, refs = refs[:pieces], refs[pieces:]
    tail_refs, weights = refs[:count], refs[count:]
    scratch = refs[-len(groups):]
    out_ref = refs[-len(groups) - 1 - passed]
    rows = tail_refs[0].shape[0]
    units = hiddens[0].shape[1]
    mine_and_other, _, _, starts = position(units)
    offsets = layout(groups, capacity)
    width = out_ref.shape[1]
    step = tile(width, (256,))
    shares = []
    for g, (expert, members) in enumerate(groups):
        tails = jnp.concatenate([tail_refs[m][...] for m in members], axis=0)
        slot, weight = slot_column(tails, mine_and_other[expert], experts, rows, capacity)
        shares.append(jnp.broadcast_to(weight, (len(members) * rows, step)))
        low, high = (0, offsets[-1]) if tight(groups, capacity) else (offsets[g], offsets[g + 1])
        place = lax.broadcasted_iota(jnp.int32, (len(members) * rows, high - low), 1) - (offsets[g] - low)
        spread = jnp.where((place == slot) & (slot >= 0), 1.0, 0.0).astype(BF16)
        for s, ref in enumerate(hiddens):
            value = jnp.dot(spread, ref[low:high, :], preferred_element_type=F32).astype(BF16)
            if wide:
                scratch[g][:, pl.ds(pl.multiple_of(starts[s], LANES), units)] = value
            else:
                scratch[g][s] = value
    for column in range(0, width, step):
        sums = [None] * count
        for g, (expert, members) in enumerate(groups):
            w_ref = weights[g]
            if wide:
                result = jnp.dot(scratch[g][...], w_ref[:, column:column + step], preferred_element_type=F32)
            else:
                result = jnp.zeros((len(members) * rows, step), F32)
                for s in range(pieces):
                    w = w_ref[pl.ds(pl.multiple_of(starts[s], 16), units), column:column + step]
                    result = result + jnp.dot(scratch[g][s], w, preferred_element_type=F32)
            result = result * shares[g]
            for k, m in enumerate(members):
                part = result[k * rows:(k + 1) * rows]
                sums[m] = part if sums[m] is None else sums[m] + part
        for m, value in enumerate(sums):
            out_ref[m * rows:(m + 1) * rows, column:column + step] = value.astype(BF16)


def down_rows(groups, hiddens, blocks, weights, passing, after, width, experts, capacity):
    rows, padded = blocks[0].shape
    units = hiddens[0].shape[1]
    pieces = len(hiddens)
    wide = units % LANES == 0
    tail = pl.BlockSpec((rows, padded - width), lambda i: (0, width // (padded - width)))
    scratch = []
    for _, members in groups:
        spread = (len(members) * rows, pieces * units) if wide else (pieces, len(members) * rows, units)
        scratch.append(pltpu.VMEM(spread, BF16))
    out = jax.ShapeDtypeStruct((len(blocks) * rows, width), BF16)
    args = (*hiddens, *blocks, *[weights[e] for e, _ in groups], *after, *passing)
    result = pl.pallas_call(
        functools.partial(down_kernel, experts, capacity, groups, len(blocks), pieces, wide, len(passing)),
        grid=(1,),
        out_shape=(out, *[jax.ShapeDtypeStruct(p.shape, p.dtype) for p in passing]),
        in_specs=[whole(h) for h in hiddens] + [tail] * len(blocks)
        + [whole(weights[0])] * len(groups) + [ANY] * (len(after) + len(passing)),
        out_specs=(whole(out), *[ANY] * len(passing)),
        input_output_aliases={len(args) - len(passing) + i: 1 + i for i in range(len(passing))},
        scratch_shapes=scratch,
        compiler_params=params(),
        cost_estimate=cost(),
    )(*args)
    return result[0], result[1:]


def add_kernel(count, *refs):
    out_ref = refs[-1]
    total = refs[0][...].astype(F32)
    for ref in refs[1:count]:
        total = total + ref[...].astype(F32)
    out_ref[...] = total.astype(out_ref.dtype)


def added(terms, kind, after):
    out = jax.ShapeDtypeStruct(terms[0].shape, kind)
    return pl.pallas_call(
        functools.partial(add_kernel, len(terms)),
        grid=(1,),
        out_shape=out,
        in_specs=[whole(t) for t in terms] + [ANY] * len(after),
        out_specs=whole(out),
        compiler_params=params(),
        cost_estimate=cost(),
    )(*terms, *after)


def on_device(tokens, expert_ids, route_weights, w_gate, w_up, w_down):
    rows, width = tokens.shape
    top = expert_ids.shape[1]
    ring = lax.axis_size("expert")
    experts = ring * lax.axis_size("dp")
    capacity = min(rows, max(2, 3 * rows * top // (2 * experts)))
    parts = lax.axis_size("tensor")
    units = w_gate.shape[2] // parts
    rank = lax.axis_index("tensor")
    hops = ring // 2

    def over_y(x):
        return lax.ppermute(x, "expert", [(i, i ^ 1) for i in range(ring)])

    def over_z(x):
        return lax.ppermute(x, "expert", [(i, (i + 2) % ring) for i in range(ring)])

    def home_over_both(x, hop):
        return lax.ppermute(x, "expert", [(i, ((i - 2 * hop) % ring) ^ 1) for i in range(ring)])

    def over_core(x):
        return lax.ppermute(x, "dp", [(0, 1), (1, 0)])

    def over_x(x, step):
        return lax.ppermute(x, "tensor", [(i, (i + step) % parts) for i in range(parts)])

    gates = (w_gate[0], over_core(w_gate)[0])
    ups = (w_up[0], over_core(w_up)[0])
    split = parts == 2 and units % LANES == 0
    if split:
        away = home = tuple(zip(gates, ups))
    else:
        def unit_slice(w, offset):
            return lax.dynamic_slice_in_dim(w, (rank + offset) % parts * units, units, 1)

        away, home = [], []
        for gate, up in zip(gates, ups):
            pairs = [(unit_slice(gate, s), unit_slice(up, s)) for s in range(parts)]
            away.append((jnp.concatenate([w for pair in pairs[1:] for w in pair], axis=1),))
            home.append((jnp.concatenate(pairs[0], axis=1),))

    blocks, arrived = {(0, "s"): make_block(tokens, expert_ids, route_weights, experts)}, {}
    blocks[0, "c"] = over_core(blocks[0, "s"])

    def send_on(hop):
        block = blocks[hop, "s"]
        if hop + 1 < hops:
            arrived[hop + 1] = over_z(block)
        blocks[hop, "b"] = over_y(block)

    both = ((0, (0, 1)), (1, (0, 1)))
    one = ((0, (0,)), (1, (0,)))
    plan = [([(0, "s")], ((0, (0,)),)), ([(0, "s"), (0, "b"), (1, "s")], ((1, (0, 1, 2)), (0, (1, 2))))]
    plan += [([(1, "b")], one)] + [([(hop, "b"), (hop, "s")], both) for hop in range(2, hops - 1)]
    plan += [([(hops - 1, "b")], one), ([(hops - 1, "s")], one)]
    count = len(plan)
    straight = ()
    chosen, parts_in, totals, hidden, returned, carried, gathered = {}, {}, {}, {}, {}, {}, []
    downs = [w_down[0]]
    order = []

    def passing(hop):
        return [arrived[hop]] if hop in arrived else []

    def take_on(hop, passed):
        if passed:
            blocks[hop, "s"] = passed[0]
            send_on(hop)

    def pick(i):
        keys, groups = plan[i]
        mine = [blocks[k] for k in keys]
        chosen[i], part = pick_rows(
            groups, mine, away, split, [], order, width, experts, capacity, units
        )
        if i == 1:
            later, _ = lax.optimization_barrier((w_down, part))
            downs.append(over_core(later)[0])
        cut = units if i == 1 else 2 * units
        parts_in[i] = []
        for step in range(1, parts):
            columns = range(2 * units * (step - 1), 2 * units * step, cut)
            parts_in[i].append([over_x(part[:, c:c + cut], step) for c in columns])
        order[:] = [part]

    def home_product(i, hop=None):
        totals[i], passed = home_rows(
            plan[i][1], chosen[i], home, split, passing(hop), order, capacity, units
        )
        order[:] = [totals[i]]
        take_on(hop, passed)

    def activate(i):
        total = totals[i]
        for pieces in parts_in[i]:
            total = total + jnp.concatenate(pieces, axis=1).astype(F32)
        value = (jax.nn.silu(total[:, :units]) * total[:, units:]).astype(BF16)
        hidden[i] = [value] + [over_x(value, s) for s in range(1, parts)]
        order.append(value)

    def down_product(i, hop=None):
        keys, groups = plan[i]
        mine = [blocks[k] for k in keys]
        term, passed = down_rows(
            groups, hidden[i], mine, downs, passing(hop), order, width, experts, capacity
        )
        order[:] = [term]
        take_on(hop, passed)
        for k, (at, kind) in enumerate(keys):
            piece = term[k * rows:(k + 1) * rows]
            if kind == "b" and at in straight:
                gathered.append(home_over_both(piece, at))
            elif kind == "b":
                returned[at, "b"] = over_y(piece)
            elif kind == "c":
                gathered.append(over_core(piece))
            elif at == 0:
                gathered.append(piece)
            else:
                returned[at, "s"] = piece

    def add_hop(hop):
        if hop == 0:
            gathered[:] = [added(gathered + [returned[hop, "b"]], F32, order)]
            order[:] = [gathered[0]]
        else:
            terms = [returned[hop, "s"]] + ([returned[hop, "b"]] if hop not in straight else [])
            terms += [carried[hop]] if hop in carried else []
            total = added(terms, BF16, order)
            order[:] = [total]
            carried[hop + 1] = over_z(total)

    def await_beside(hop):
        if (hop, "b") in blocks:
            order.append(blocks[hop, "b"])

    send_on(0)
    if hops == 4:
        pick(0)
        order.append(blocks[0, "b"])
        home_product(0, 1)
        activate(0)
        pick(1)
        order.extend(downs[1:])
        pick(2)
        home_product(1, 2)
        home_product(2, 3)
        down_product(0)
        pick(3)
        activate(1)
        activate(2)
        down_product(1)
        down_product(2)
        pick(4)
        home_product(3)
        home_product(4)
        activate(3)
        pick(5)
        add_hop(0)
        order.append(blocks[2, "b"])
        home_product(5)
        down_product(3)
        activate(4)
        add_hop(1)
        down_product(4)
        add_hop(2)
        activate(5)
        down_product(5)
        add_hop(3)
    else:
        for i in range(count):
            pick(i)
            home_product(i, i + 1)
            if i > 0:
                activate(i - 1)
                down_product(i - 1)
        activate(count - 1)
        down_product(count - 1)
        for hop in range(hops):
            add_hop(hop)
    return sum(x.astype(F32) for x in gathered + [carried[hops]]).astype(BF16)


def solution(mesh):
    placed = (
        P(("group", "expert", "dp"), "tensor"),
        P(("group", "expert", "dp"), None),
        P(("group", "expert", "dp"), None),
        P(("expert", "dp"), "tensor", None),
        P(("expert", "dp"), "tensor", None),
        P(("expert", "dp"), None, "tensor"),
    )
    return jax.shard_map(
        on_device,
        mesh=mesh,
        in_specs=placed,
        out_specs=P(("group", "expert", "dp"), "tensor"),
        check_vma=False,
    )
```

```python
import functools

import jax
import jax.numpy as jnp
from jax import lax
from jax.experimental import pallas as pl
from jax.experimental.pallas import tpu as pltpu
from jax.sharding import PartitionSpec as P

F32 = jnp.float32
BF16 = jnp.bfloat16
LANES = 128
VMEM = 10 * 1024 * 1024
ANY = pl.BlockSpec(memory_space=pl.ANY)
HBM = pl.BlockSpec(memory_space=pltpu.HBM)


def tile(extent, choices):
    for size in choices:
        if extent % size == 0:
            return size
    return extent


def whole(x):
    return pl.BlockSpec(x.shape, lambda i: (0,) * len(x.shape))


def params():
    return pltpu.CompilerParams(vmem_limit_bytes=VMEM)


def cost():
    return pl.CostEstimate(flops=1, bytes_accessed=1, transcendentals=0)


def block_kernel(experts, tokens_ref, routes_ref, out_ref, sem):
    rows, width = tokens_ref.shape
    copy = pltpu.make_async_copy(tokens_ref, out_ref.at[:, :width], sem)
    copy.start()
    routes = routes_ref[...].T
    top = routes.shape[1] // 2
    column = lax.broadcasted_iota(jnp.int32, (rows, out_ref.shape[1] - width), 1)
    expert = jnp.where(column < experts, column, column - experts).astype(F32)
    value = jnp.zeros(column.shape, F32)
    for k in range(top):
        value = value + jnp.where(expert == routes[:, k:k + 1], routes[:, top + k:top + k + 1], 0.0)
    high = value.astype(BF16).astype(F32)
    out_ref[:, width:] = jnp.where(column < experts, high, value - high).astype(BF16)
    copy.wait()


def make_block(tokens, expert_ids, route_weights, experts):
    rows, width = tokens.shape
    padded = width + 2 * experts + (-(2 * experts)) % LANES
    routes = jnp.concatenate([expert_ids.T.astype(F32), route_weights.T], axis=0)
    return pl.pallas_call(
        functools.partial(block_kernel, experts),
        grid=(1,),
        out_shape=jax.ShapeDtypeStruct((rows, padded), BF16),
        in_specs=[HBM, whole(routes)],
        out_specs=pl.BlockSpec((rows, padded), lambda i: (0, 0)),
        scratch_shapes=[pltpu.SemaphoreType.DMA],
        compiler_params=params(),
        cost_estimate=cost(),
    )(tokens, routes)


def slot_row(tails, me, experts, rows, capacity):
    total = tails.shape[0]
    column = lax.broadcasted_iota(jnp.int32, (8, tails.shape[1]), 1)
    mark = jnp.where((column == me) | (column == experts + me), 1.0, 0.0).astype(BF16)
    weight = lax.dot_general(mark, tails, (((1,), (1,)), ((), ())), preferred_element_type=F32)
    live = weight > 0.0
    number = lax.broadcasted_iota(jnp.int32, (8, total), 1) // rows
    above = lax.broadcasted_iota(jnp.int32, (total, total), 0)
    own = lax.broadcasted_iota(jnp.int32, (total, total), 1)
    ahead = jnp.where((above < own) & (above >= (number * rows)[0:1]), 1.0, 0.0).astype(BF16)
    before = jnp.dot(jnp.where(live, 1.0, 0.0).astype(BF16), ahead, preferred_element_type=F32)
    return jnp.where(live, before.astype(jnp.int32) + number * capacity, -1)[0:1]


def slot_column(tails, me, experts, rows, capacity):
    total = tails.shape[0]
    column = lax.broadcasted_iota(jnp.int32, tails.shape, 1)
    mine = (column == me) | (column == experts + me)
    weight = jnp.sum(jnp.where(mine, tails.astype(F32), 0.0), axis=1, keepdims=True)
    live = weight > 0.0
    number = lax.broadcasted_iota(jnp.int32, (total, 1), 0) // rows
    own = lax.broadcasted_iota(jnp.int32, (total, total), 0)
    above = lax.broadcasted_iota(jnp.int32, (total, total), 1)
    ahead = jnp.where((above < own) & (above >= number * rows), 1.0, 0.0).astype(BF16)
    flags = jnp.broadcast_to(jnp.where(live, 1.0, 0.0), (total, LANES)).astype(BF16)
    before = jnp.dot(ahead, flags, preferred_element_type=F32)[:, 0:1]
    return jnp.where(live, before.astype(jnp.int32) + number * capacity, -1), weight


def tight(groups, capacity):
    return len(groups) == 2 and capacity % 8 == 0 and all(len(members) == 1 for _, members in groups)


def layout(groups, capacity):
    if tight(groups, capacity):
        return [0, capacity, -(-2 * capacity // 16) * 16]
    offsets = [0]
    for _, members in groups:
        offsets.append(offsets[-1] + -(-len(members) * capacity // 16) * 16)
    return offsets


def multiply(x_ref, rows, weights, start, units, out_ref):
    def store(x, w, column, count):
        out_ref[rows, column:column + count] = jnp.dot(x, w, preferred_element_type=F32).astype(out_ref.dtype)

    x = x_ref[rows, :]
    if start is None:
        w_ref = weights[0]
        step = tile(w_ref.shape[1], (256, 384))
        for column in range(0, w_ref.shape[1], step):
            store(x, w_ref[:, column:column + step], column, step)
        return
    full = units // 256 * 256
    for i, ref in enumerate(weights):
        for column in range(0, full, 256):
            store(x, ref[:, pl.ds(pl.multiple_of(start + column, LANES), 256)], i * units + column, 256)
    if full < units:
        rest = pl.ds(pl.multiple_of(start + full, LANES), units - full)
        w = jnp.concatenate([ref[:, rest] for ref in weights], axis=1)
        y = jnp.dot(x, w, preferred_element_type=F32).astype(out_ref.dtype)
        out_ref[rows, full:units] = y[:, :units - full]
        out_ref[rows, units + full:] = y[:, units - full:]


def multiply_both(x_ref, bound, first, second, start, units, out_ref):
    x = x_ref[...]
    for (column, count, v), (_, _, w) in zip(tiles(first, start, units), tiles(second, start, units)):
        upper = lax.broadcasted_iota(jnp.int32, (x.shape[0], count), 0) < bound
        a = jnp.dot(x, v(), preferred_element_type=F32)
        b = jnp.dot(x, w(), preferred_element_type=F32)
        out_ref[:, column:column + count] = jnp.where(upper, a, b).astype(out_ref.dtype)


def tiles(weights, start, units):
    if start is None:
        ref = weights[0]
        step = tile(ref.shape[1], (256, 384))
        return [(c, step, lambda c=c: ref[:, c:c + step]) for c in range(0, ref.shape[1], step)]
    parts = []
    step = tile(units, (384, 256, LANES))
    for i, ref in enumerate(weights):
        for c in range(0, units, step):
            span = pl.ds(pl.multiple_of(start + c, LANES), step)
            parts.append((i * units + c, step, lambda ref=ref, span=span: ref[:, span]))
    return parts


def position(units):
    core, rank, parts = lax.axis_index("dp"), lax.axis_index("tensor"), lax.axis_size("tensor")
    first = lax.axis_index("expert") * 2
    places = [(rank + parts - s) % parts * units for s in range(parts)]
    return (first + core, first + 1 - core), (rank + 1) % parts * units, rank * units, places


def pick_kernel(width, experts, capacity, units, groups, count, kinds, split, copied, *refs):
    blocks, weights = refs[:count], refs[count:]
    if copied:
        *_, source_ref, chosen_ref, part_ref, target_ref, sem = refs
        copy = pltpu.make_async_copy(source_ref, target_ref, sem)
        copy.start()
    else:
        chosen_ref, part_ref = refs[-2:]
    rows = blocks[0].shape[0]
    mine_and_other, start, _, _ = position(units)
    offsets = layout(groups, capacity)
    step = tile(width, (512, 256))
    if tight(groups, capacity):
        taken = offsets[-1]
        place = lax.broadcasted_iota(jnp.int32, (taken, rows), 0)
        pick = jnp.zeros((taken, rows), F32)
        for g, (expert, _) in enumerate(groups):
            slot = slot_row(blocks[0][:, width:], mine_and_other[expert], experts, rows, capacity)
            pick = pick + jnp.where((place == slot + offsets[g]) & (slot >= 0), 1.0, 0.0)
        pick = pick.astype(BF16)
        for column in range(0, width, step):
            value = jnp.dot(pick, blocks[0][:, column:column + step], preferred_element_type=F32)
            chosen_ref[:, column:column + step] = value.astype(BF16)
        first, second = weights[:kinds], weights[kinds:2 * kinds]
        multiply_both(chosen_ref, offsets[1], first, second, start if split else None, units, part_ref)
        return
    for g, (expert, members) in enumerate(groups):
        tails = jnp.concatenate([blocks[m][:, width:] for m in members], axis=0)
        slot = slot_row(tails, mine_and_other[expert], experts, rows, capacity)
        here = offsets[g + 1] - offsets[g]
        place = lax.broadcasted_iota(jnp.int32, (here, len(members) * rows), 0)
        pick = jnp.where(place == slot, 1.0, 0.0).astype(BF16)
        for column in range(0, width, step):
            x = jnp.concatenate([blocks[m][:, column:column + step] for m in members], axis=0)
            value = jnp.dot(pick, x, preferred_element_type=F32).astype(BF16)
            chosen_ref[offsets[g]:offsets[g + 1], column:column + step] = value
    for g in range(len(groups)):
        mine = weights[kinds * g:kinds * (g + 1)]
        multiply(chosen_ref, slice(offsets[g], offsets[g + 1]), mine, start if split else None, units, part_ref)
    if copied:
        copy.wait()


def pick_rows(groups, blocks, weights, split, copying, after, width, experts, capacity, units):
    columns = 2 * units if split else weights[0][0].shape[1]
    taken = layout(groups, capacity)[-1]
    flat = [w for expert, _ in groups for w in weights[expert]]
    copied = len(copying)
    kernel = functools.partial(
        pick_kernel, width, experts, capacity, units, groups, len(blocks), len(weights[0]), split, copied
    )
    out = (jax.ShapeDtypeStruct((taken, width), BF16), jax.ShapeDtypeStruct((taken, columns), BF16))
    return pl.pallas_call(
        kernel,
        grid=(1,),
        out_shape=(*out, *[jax.ShapeDtypeStruct(a.shape, a.dtype) for a in copying]),
        in_specs=[whole(x) for x in (*blocks, *flat)] + [ANY] * (len(after) + copied),
        out_specs=(*[whole(o) for o in out], *[ANY] * copied),
        scratch_shapes=[pltpu.SemaphoreType.DMA] * copied,
        compiler_params=params(),
        cost_estimate=cost(),
    )(*blocks, *flat, *after, *copying)


def home_kernel(capacity, units, groups, kinds, split, passed, x_ref, *refs):
    _, _, start, _ = position(units)
    out_ref = refs[-1 - passed]
    offsets = layout(groups, capacity)
    if tight(groups, capacity):
        first, second = refs[:kinds], refs[kinds:2 * kinds]
        multiply_both(x_ref, offsets[1], first, second, start if split else None, units, out_ref)
        return
    for g in range(len(groups)):
        mine = refs[kinds * g:kinds * (g + 1)]
        multiply(x_ref, slice(offsets[g], offsets[g + 1]), mine, start if split else None, units, out_ref)


def home_rows(groups, chosen, weights, split, passing, after, capacity, units):
    flat = [w for expert, _ in groups for w in weights[expert]]
    out = jax.ShapeDtypeStruct((chosen.shape[0], 2 * units), F32)
    args = (chosen, *flat, *after, *passing)
    result = pl.pallas_call(
        functools.partial(home_kernel, capacity, units, groups, len(weights[0]), split, len(passing)),
        grid=(1,),
        out_shape=(out, *[jax.ShapeDtypeStruct(p.shape, p.dtype) for p in passing]),
        in_specs=[whole(chosen)] + [whole(w) for w in flat] + [ANY] * (len(after) + len(passing)),
        out_specs=(whole(out), *[ANY] * len(passing)),
        input_output_aliases={len(args) - len(passing) + i: 1 + i for i in range(len(passing))},
        compiler_params=params(),
        cost_estimate=cost(),
    )(*args)
    return result[0], result[1:]


def down_kernel(experts, capacity, groups, count, pieces, wide, passed, *refs):
    hiddens, refs = refs[:pieces], refs[pieces:]
    tail_refs, weights = refs[:count], refs[count:]
    scratch = refs[-len(groups):]
    out_ref = refs[-len(groups) - 1 - passed]
    rows = tail_refs[0].shape[0]
    units = hiddens[0].shape[1]
    mine_and_other, _, _, starts = position(units)
    offsets = layout(groups, capacity)
    width = out_ref.shape[1]
    step = tile(width, (256,))
    shares = []
    for g, (expert, members) in enumerate(groups):
        tails = jnp.concatenate([tail_refs[m][...] for m in members], axis=0)
        slot, weight = slot_column(tails, mine_and_other[expert], experts, rows, capacity)
        shares.append(jnp.broadcast_to(weight, (len(members) * rows, step)))
        low, high = (0, offsets[-1]) if tight(groups, capacity) else (offsets[g], offsets[g + 1])
        place = lax.broadcasted_iota(jnp.int32, (len(members) * rows, high - low), 1) - (offsets[g] - low)
        spread = jnp.where((place == slot) & (slot >= 0), 1.0, 0.0).astype(BF16)
        for s, ref in enumerate(hiddens):
            value = jnp.dot(spread, ref[low:high, :], preferred_element_type=F32).astype(BF16)
            if wide:
                scratch[g][:, pl.ds(pl.multiple_of(starts[s], LANES), units)] = value
            else:
                scratch[g][s] = value
    for column in range(0, width, step):
        sums = [None] * count
        for g, (expert, members) in enumerate(groups):
            w_ref = weights[g]
            if wide:
                result = jnp.dot(scratch[g][...], w_ref[:, column:column + step], preferred_element_type=F32)
            else:
                result = jnp.zeros((len(members) * rows, step), F32)
                for s in range(pieces):
                    w = w_ref[pl.ds(pl.multiple_of(starts[s], 16), units), column:column + step]
                    result = result + jnp.dot(scratch[g][s], w, preferred_element_type=F32)
            result = result * shares[g]
            for k, m in enumerate(members):
                part = result[k * rows:(k + 1) * rows]
                sums[m] = part if sums[m] is None else sums[m] + part
        for m, value in enumerate(sums):
            out_ref[m * rows:(m + 1) * rows, column:column + step] = value.astype(BF16)


def down_rows(groups, hiddens, blocks, weights, passing, after, width, experts, capacity):
    rows, padded = blocks[0].shape
    units = hiddens[0].shape[1]
    pieces = len(hiddens)
    wide = units % LANES == 0
    tail = pl.BlockSpec((rows, padded - width), lambda i: (0, width // (padded - width)))
    scratch = []
    for _, members in groups:
        spread = (len(members) * rows, pieces * units) if wide else (pieces, len(members) * rows, units)
        scratch.append(pltpu.VMEM(spread, BF16))
    out = jax.ShapeDtypeStruct((len(blocks) * rows, width), BF16)
    args = (*hiddens, *blocks, *[weights[e] for e, _ in groups], *after, *passing)
    result = pl.pallas_call(
        functools.partial(down_kernel, experts, capacity, groups, len(blocks), pieces, wide, len(passing)),
        grid=(1,),
        out_shape=(out, *[jax.ShapeDtypeStruct(p.shape, p.dtype) for p in passing]),
        in_specs=[whole(h) for h in hiddens] + [tail] * len(blocks)
        + [whole(weights[0])] * len(groups) + [ANY] * (len(after) + len(passing)),
        out_specs=(whole(out), *[ANY] * len(passing)),
        input_output_aliases={len(args) - len(passing) + i: 1 + i for i in range(len(passing))},
        scratch_shapes=scratch,
        compiler_params=params(),
        cost_estimate=cost(),
    )(*args)
    return result[0], result[1:]


def add_kernel(count, *refs):
    out_ref = refs[-1]
    total = refs[0][...].astype(F32)
    for ref in refs[1:count]:
        total = total + ref[...].astype(F32)
    out_ref[...] = total.astype(out_ref.dtype)


def added(terms, kind, after):
    out = jax.ShapeDtypeStruct(terms[0].shape, kind)
    return pl.pallas_call(
        functools.partial(add_kernel, len(terms)),
        grid=(1,),
        out_shape=out,
        in_specs=[whole(t) for t in terms] + [ANY] * len(after),
        out_specs=whole(out),
        compiler_params=params(),
        cost_estimate=cost(),
    )(*terms, *after)


def on_device(tokens, expert_ids, route_weights, w_gate, w_up, w_down):
    rows, width = tokens.shape
    top = expert_ids.shape[1]
    ring = lax.axis_size("expert")
    experts = ring * lax.axis_size("dp")
    capacity = min(rows, max(2, 3 * rows * top // (2 * experts)))
    parts = lax.axis_size("tensor")
    units = w_gate.shape[2] // parts
    rank = lax.axis_index("tensor")
    hops = ring // 2

    def over_y(x):
        return lax.ppermute(x, "expert", [(i, i ^ 1) for i in range(ring)])

    def over_z(x):
        return lax.ppermute(x, "expert", [(i, (i + 2) % ring) for i in range(ring)])

    def home_over_both(x, hop):
        return lax.ppermute(x, "expert", [(i, ((i - 2 * hop) % ring) ^ 1) for i in range(ring)])

    def over_core(x):
        return lax.ppermute(x, "dp", [(0, 1), (1, 0)])

    def over_x(x, step):
        return lax.ppermute(x, "tensor", [(i, (i + step) % parts) for i in range(parts)])

    gates = (w_gate[0], over_core(w_gate)[0])
    ups = (w_up[0], over_core(w_up)[0])
    split = parts == 2 and units % LANES == 0
    if split:
        away = home = tuple(zip(gates, ups))
    else:
        def unit_slice(w, offset):
            return lax.dynamic_slice_in_dim(w, (rank + offset) % parts * units, units, 1)

        away, home = [], []
        for gate, up in zip(gates, ups):
            pairs = [(unit_slice(gate, s), unit_slice(up, s)) for s in range(parts)]
            away.append((jnp.concatenate([w for pair in pairs[1:] for w in pair], axis=1),))
            home.append((jnp.concatenate(pairs[0], axis=1),))

    blocks, arrived = {(0, "s"): make_block(tokens, expert_ids, route_weights, experts)}, {}
    blocks[0, "c"] = over_core(blocks[0, "s"])

    def send_on(hop):
        block = blocks[hop, "s"]
        if hop + 1 < hops:
            arrived[hop + 1] = over_z(block)
        blocks[hop, "b"] = over_y(block)

    both = ((0, (0, 1)), (1, (0, 1)))
    one = ((0, (0,)), (1, (0,)))
    plan = [([(0, "s")], ((0, (0,)),)), ([(0, "s"), (0, "b"), (1, "s")], ((1, (0, 1, 2)), (0, (1, 2))))]
    plan += [([(1, "b")], one)] + [([(hop, "b"), (hop, "s")], both) for hop in range(2, hops - 1)]
    plan += [([(hops - 1, "b")], one), ([(hops - 1, "s")], one)]
    count = len(plan)
    straight = ()
    chosen, parts_in, totals, hidden, returned, carried, gathered = {}, {}, {}, {}, {}, {}, []
    downs = [w_down[0]]
    order = []

    def passing(hop):
        return [arrived[hop]] if hop in arrived else []

    def take_on(hop, passed):
        if passed:
            blocks[hop, "s"] = passed[0]
            send_on(hop)

    def pick(i):
        keys, groups = plan[i]
        mine = [blocks[k] for k in keys]
        chosen[i], part = pick_rows(
            groups, mine, away, split, [], order, width, experts, capacity, units
        )
        if i == 1:
            later, _ = lax.optimization_barrier((w_down, part))
            downs.append(over_core(later)[0])
        cut = 2 * units
        parts_in[i] = []
        for step in range(1, parts):
            columns = range(2 * units * (step - 1), 2 * units * step, cut)
            parts_in[i].append([over_x(part[:, c:c + cut], step) for c in columns])
        order[:] = [part]

    def home_product(i, hop=None):
        totals[i], passed = home_rows(
            plan[i][1], chosen[i], home, split, passing(hop), order, capacity, units
        )
        order[:] = [totals[i]]
        take_on(hop, passed)

    def activate(i):
        total = totals[i]
        for pieces in parts_in[i]:
            total = total + jnp.concatenate(pieces, axis=1).astype(F32)
        value = (jax.nn.silu(total[:, :units]) * total[:, units:]).astype(BF16)
        hidden[i] = [value] + [over_x(value, s) for s in range(1, parts)]
        order.append(value)

    def down_product(i, hop=None):
        keys, groups = plan[i]
        mine = [blocks[k] for k in keys]
        term, passed = down_rows(
            groups, hidden[i], mine, downs, passing(hop), order, width, experts, capacity
        )
        order[:] = [term]
        take_on(hop, passed)
        for k, (at, kind) in enumerate(keys):
            piece = term[k * rows:(k + 1) * rows]
            if kind == "b" and at in straight:
                gathered.append(home_over_both(piece, at))
            elif kind == "b":
                returned[at, "b"] = over_y(piece)
            elif kind == "c":
                gathered.append(over_core(piece))
            elif at == 0:
                gathered.append(piece)
            else:
                returned[at, "s"] = piece

    def add_hop(hop):
        if hop == 0:
            gathered[:] = [added(gathered + [returned[hop, "b"]], F32, order)]
            order[:] = [gathered[0]]
        else:
            terms = [returned[hop, "s"]] + ([returned[hop, "b"]] if hop not in straight else [])
            terms += [carried[hop]] if hop in carried else []
            total = added(terms, BF16, order)
            order[:] = [total]
            carried[hop + 1] = over_z(total)

    def await_beside(hop):
        if (hop, "b") in blocks:
            order.append(blocks[hop, "b"])

    send_on(0)
    if hops == 4:
        pick(0)
        order.append(blocks[0, "b"])
        home_product(0, 1)
        activate(0)
        pick(1)
        order.extend(downs[1:])
        down_product(0)
        home_product(1, 2)
        pick(2)
        home_product(2, 3)
        activate(2)
        pick(3)
        activate(1)
        down_product(1)
        down_product(2)
        order.append(blocks[2, "b"])
        pick(4)
        home_product(3)
        order.extend(downs[1:])
        home_product(4)
        pick(5)
        activate(3)
        home_product(5)
        add_hop(0)
        down_product(3)
        add_hop(1)
        add_hop(2)
        order.append(blocks[2, "b"])
        activate(4)
        down_product(4)
        activate(5)
        down_product(5)
        add_hop(3)
    else:
        for i in range(count):
            pick(i)
            home_product(i, i + 1)
            if i > 0:
                activate(i - 1)
                down_product(i - 1)
        activate(count - 1)
        down_product(count - 1)
        for hop in range(hops):
            add_hop(hop)
    return sum(x.astype(F32) for x in gathered + [carried[hops]]).astype(BF16)


def solution(mesh):
    placed = (
        P(("group", "expert", "dp"), "tensor"),
        P(("group", "expert", "dp"), None),
        P(("group", "expert", "dp"), None),
        P(("expert", "dp"), "tensor", None),
        P(("expert", "dp"), "tensor", None),
        P(("expert", "dp"), None, "tensor"),
    )
    return jax.shard_map(
        on_device,
        mesh=mesh,
        in_specs=placed,
        out_specs=P(("group", "expert", "dp"), "tensor"),
        check_vma=False,
    )
```
